32 devices in a mesh: blk: 2 (over x), tp: 4 (over y, core), enc: 4 (over z).
Axes of the slice: x: 2, y: 2, z: 4, core: 2. Of those that a mesh axis runs over, the one named last changes fastest.
Arguments:
- self_query_columns: bfloat16 [1024, 4096], P('blk', ('tp', 'enc')), may hold values from -12 to 12
- text_key_value: bfloat16 [1024, 2, 512], P('blk', None, 'tp'), may hold values from -9 to 9
- cross_query_columns: bfloat16 [1024, 4096], P('blk', ('tp', 'enc')), may hold values from -12 to 12
- image_kv: bfloat16 [2, 2, 6404, 512], P('blk', None, 'enc', 'tp'), may hold values from -9 to 9
- block_images: int32 [8, 2], P('blk'), may hold values from 0 to 1, as said below
- image_owner: int32 [2], replicated, may hold values from 0 to 1, each once
Outputs:
- self_out: bfloat16 [1024, 4096], P('blk', ('tp', 'enc'))
- cross_out: bfloat16 [1024, 4096], P('blk', ('tp', 'enc'))
The draws below stay inside these ranges and needn't reach their ends.
Inputs may be any that keep to these rules, and one draw needn't show every extreme that they name: `block_images`: each block of 128 text tokens sees one or two images: the image most recently placed before it and, in some blocks, the image placed before that one. Image ids rise along the text, every image is seen by some block, and some block sees two. A permutation: image i's keys and values are slot image_owner[i] of image_kv.
All inputs are finite; a program needn't handle non-finite values.
Results may differ from the reference program's by a relative error of at most 0.007.
Values may be sent and summed in bfloat16 or wider, within the bound.
No kernel may reach another device: no remote copies, remote signals or barrier semaphores. Data moves between devices by JAX's collectives and lax.ppermute only.
A program may use at most 64 MiB of HBM per device.

```python
import math
import jax
import jax.numpy as jnp
from jax import lax

QUERY_HEADS = 32
KEY_VALUE_HEADS = 4
HEAD_SIZE = 128
IMAGE_TOKENS = 6404
MASK_BLOCK_TOKENS = 128
TEXT_TOKENS = 1024
MASK_BLOCK_COUNT = 8
IMAGE_COUNT = 2


def draw_self_query_columns(key, part):
    key = jax.random.fold_in(key, 11)
    drawn_result = 2.5 * jnp.clip(jax.random.normal(key, (TEXT_TOKENS, QUERY_HEADS, HEAD_SIZE), jnp.float32), -4.0, 4.0)
    return drawn_result.reshape(TEXT_TOKENS, QUERY_HEADS * HEAD_SIZE).astype(jnp.bfloat16)


def draw_cross_query_columns(key, part):
    key = jax.random.fold_in(key, 23)
    drawn_result = 2.5 * jnp.clip(jax.random.normal(key, (TEXT_TOKENS, QUERY_HEADS, HEAD_SIZE), jnp.float32), -4.0, 4.0)
    return drawn_result.reshape(TEXT_TOKENS, QUERY_HEADS * HEAD_SIZE).astype(jnp.bfloat16)


def draw_text_key_value(key, part):
    key = jax.random.fold_in(key, 37)
    drawn_result = jnp.clip(jax.random.normal(key, (TEXT_TOKENS, 2, KEY_VALUE_HEADS, HEAD_SIZE), jnp.float32), -4.0, 4.0)
    return drawn_result.reshape(TEXT_TOKENS, 2, KEY_VALUE_HEADS * HEAD_SIZE).astype(jnp.bfloat16)


def draw_image_kv(key, part):
    key = jax.random.fold_in(key, 44)
    drawn_result = jnp.clip(jax.random.normal(key, (IMAGE_COUNT, 2, IMAGE_TOKENS, KEY_VALUE_HEADS, HEAD_SIZE), jnp.float32), -4.0, 4.0)
    return drawn_result.reshape(IMAGE_COUNT, 2, IMAGE_TOKENS, KEY_VALUE_HEADS * HEAD_SIZE).astype(jnp.bfloat16)


def draw_block_images(key, part):
    key = jax.random.fold_in(key, 59)
    order = jax.random.permutation(jax.random.fold_in(key, 1), MASK_BLOCK_COUNT - 1) + 1
    cuts = order[:IMAGE_COUNT - 1]
    is_cut = jnp.zeros((MASK_BLOCK_COUNT,), jnp.int32).at[cuts].set(1)
    current = jnp.cumsum(is_cut).astype(jnp.int32)
    second = jax.random.randint(jax.random.fold_in(key, 2), (MASK_BLOCK_COUNT,), 0, 4) > 0
    second = second & (current > 0)
    second = second.at[MASK_BLOCK_COUNT - 1].set(True)
    image_ids = jnp.arange(IMAGE_COUNT, dtype=jnp.int32)
    latest = image_ids[None, :] == current[:, None]
    before = second[:, None] & (image_ids[None, :] == current[:, None] - 1)
    return (latest | before).astype(jnp.int32)


def setup_inputs(seed: int = 0) -> dict:
    seeds = jax.random.split(jax.random.key(seed), 7)
    return {
        "self_query_columns": draw_self_query_columns(jax.random.fold_in(seeds[6], 71), 0),
        "text_key_value": draw_text_key_value(jax.random.fold_in(seeds[6], 71), 0),
        "cross_query_columns": draw_cross_query_columns(jax.random.fold_in(seeds[6], 71), 0),
        "image_kv": draw_image_kv(jax.random.fold_in(seeds[6], 71), 0),
        "block_images": draw_block_images(jax.random.fold_in(seeds[6], 71), 0),
        "image_owner": jax.random.permutation(seeds[5], IMAGE_COUNT).astype(jnp.int32),
    }


def attend_rows(queries, key_row_block, value_row_block, allowed):
    scores = jnp.einsum('rkgd,tkd->kgrt', queries, key_row_block) * (1.0 / math.sqrt(HEAD_SIZE))
    scores = jnp.where(allowed, scores, -1e+30)
    highest = lax.optimization_barrier(jnp.max(scores, axis=-1, keepdims=True))
    weights = jnp.where(allowed, jnp.exp(scores - highest), 0.0)
    totals = lax.optimization_barrier(jnp.sum(weights, axis=-1))
    rounded = lax.optimization_barrier(weights.astype(jnp.bfloat16)).astype(jnp.float32)
    mixed = jnp.einsum('kgrt,tkd->rkgd', rounded, value_row_block)
    mixed = mixed / jnp.transpose(totals, (2, 0, 1))[..., None]
    return mixed.reshape(queries.shape[0], QUERY_HEADS * HEAD_SIZE).astype(jnp.bfloat16)

def reference(self_query_columns, text_key_value, cross_query_columns, image_kv, block_images, image_owner):
    query_group_width = QUERY_HEADS // KEY_VALUE_HEADS
    key_row_block = text_key_value[:, 0].astype(jnp.float32).reshape(TEXT_TOKENS, KEY_VALUE_HEADS, HEAD_SIZE)
    value_row_block = text_key_value[:, 1].astype(jnp.float32).reshape(TEXT_TOKENS, KEY_VALUE_HEADS, HEAD_SIZE)
    key_pos = jnp.arange(TEXT_TOKENS, dtype=jnp.int32)
    self_block_list = self_query_columns.reshape(MASK_BLOCK_COUNT, MASK_BLOCK_TOKENS, KEY_VALUE_HEADS, query_group_width, HEAD_SIZE)

    def self_block(element):
        queries, block_index = element
        query_pos = block_index * MASK_BLOCK_TOKENS + jnp.arange(MASK_BLOCK_TOKENS, dtype=jnp.int32)
        allowed = key_pos[None, :] <= query_pos[:, None]
        return attend_rows(queries.astype(jnp.float32), key_row_block, value_row_block, allowed)
    self_out = lax.map(self_block, (self_block_list, jnp.arange(MASK_BLOCK_COUNT, dtype=jnp.int32)))
    self_out = self_out.reshape(TEXT_TOKENS, QUERY_HEADS * HEAD_SIZE)
    image_ids = jnp.arange(IMAGE_COUNT, dtype=jnp.int32)
    cross_block_list = cross_query_columns.reshape(MASK_BLOCK_COUNT, MASK_BLOCK_TOKENS, KEY_VALUE_HEADS, query_group_width, HEAD_SIZE)

    def cross_block(element):
        queries, seen = element
        latest = jnp.max(jnp.where(seen > 0, image_ids, -1)).astype(jnp.int32)
        earlier = jnp.max(jnp.where((seen > 0) & (image_ids < latest), image_ids, -1)).astype(jnp.int32)
        first_slot = image_owner[latest].astype(jnp.int32)
        second_slot = image_owner[jnp.maximum(earlier, 0)].astype(jnp.int32)
        first_image = lax.dynamic_index_in_dim(image_kv, first_slot, 0, keepdims=False)
        second_image = lax.dynamic_index_in_dim(image_kv, second_slot, 0, keepdims=False)
        joined_parts = jnp.concatenate([first_image, second_image], axis=1).astype(jnp.float32)
        key_section = joined_parts[0].reshape(2 * IMAGE_TOKENS, KEY_VALUE_HEADS, HEAD_SIZE)
        value_section = joined_parts[1].reshape(2 * IMAGE_TOKENS, KEY_VALUE_HEADS, HEAD_SIZE)
        allowed = jnp.concatenate([jnp.ones((IMAGE_TOKENS,), dtype=jnp.bool_), jnp.full((IMAGE_TOKENS,), earlier >= 0)])
        return attend_rows(queries.astype(jnp.float32), key_section, value_section, allowed)
    cross_out = lax.map(cross_block, (cross_block_list, block_images))
    cross_out = cross_out.reshape(TEXT_TOKENS, QUERY_HEADS * HEAD_SIZE)
    return (self_out, cross_out)
```

```python
import functools
import math

import jax
import jax.numpy as jnp
from jax import lax
from jax.experimental import pallas as pl
from jax.experimental.pallas import tpu as pltpu
from jax.sharding import PartitionSpec as P

HEAD_SIZE = 128
MASK_BLOCK_TOKENS = 128
LANES = 128
VALUE_ROWS = HEAD_SIZE + 16
LOWEST = -1e30
LOG2_SCALE = math.log2(math.e) / math.sqrt(HEAD_SIZE)
VMEM_LIMIT = 48 * 1024 * 1024

VMEM = pl.BlockSpec(memory_space=pltpu.VMEM)
SMEM = pl.BlockSpec(memory_space=pltpu.SMEM)


def padded(count):
    return -(-count // LANES) * LANES


def nt_dot(a, b):
    return lax.dot_general(a, b, (((1,), (1,)), ((), ())), preferred_element_type=jnp.float32)


def stacked_heads(q_ref, block):
    rows = q_ref[pl.ds(pl.multiple_of(block * MASK_BLOCK_TOKENS, MASK_BLOCK_TOKENS), MASK_BLOCK_TOKENS), :]
    heads = rows.shape[1] // HEAD_SIZE
    return jnp.concatenate([rows[:, h * HEAD_SIZE : (h + 1) * HEAD_SIZE] for h in range(heads)], axis=0)


def fold(scores, value_t, high_ref, acc_ref):
    high = high_ref[0:1, :]
    new_high = jnp.maximum(high, jnp.max(scores, axis=0, keepdims=True))
    weights = jnp.exp2(scores * LOG2_SCALE - new_high * LOG2_SCALE).astype(jnp.bfloat16)
    fading = jnp.exp2((high - new_high) * LOG2_SCALE)
    acc_ref[...] = acc_ref[...] * fading + jnp.dot(value_t, weights, preferred_element_type=jnp.float32)
    high_ref[0:1, :] = new_high


def clear(high_ref, acc_ref):
    high_ref[...] = jnp.full_like(high_ref, LOWEST)
    acc_ref[...] = jnp.zeros_like(acc_ref)


def prepare_kernel(kv_ref, key_ref, value_ref):
    count = kv_ref.shape[1]
    whole = count // LANES * LANES
    rest = count - whole
    if whole:
        key_ref[0:whole, :] = kv_ref[0, 0:whole, :]
        value_ref[0:HEAD_SIZE, 0:whole] = kv_ref[1, 0:whole, :].T
        value_ref[HEAD_SIZE:, 0:whole] = (
            lax.broadcasted_iota(jnp.int32, (VALUE_ROWS - HEAD_SIZE, whole), 0) == 0
        ).astype(jnp.bfloat16)
    if rest:
        tail_key = kv_ref[0, whole:count, :].astype(jnp.float32)
        tail_value = kv_ref[1, whole:count, :].astype(jnp.float32)
        empty = jnp.zeros((LANES - rest, HEAD_SIZE), jnp.float32)
        key_ref[whole : whole + LANES, :] = jnp.concatenate([tail_key, empty], axis=0).astype(jnp.bfloat16)
        value_ref[0:HEAD_SIZE, whole : whole + LANES] = jnp.concatenate([tail_value, empty], axis=0).T.astype(
            jnp.bfloat16
        )
        shape = (VALUE_ROWS - HEAD_SIZE, LANES)
        ones = (lax.broadcasted_iota(jnp.int32, shape, 0) == 0) & (lax.broadcasted_iota(jnp.int32, shape, 1) < rest)
        value_ref[HEAD_SIZE:, whole : whole + LANES] = ones.astype(jnp.bfloat16)


def prepare(kv):
    width = padded(kv.shape[1])
    return pl.pallas_call(
        prepare_kernel,
        out_shape=(
            jax.ShapeDtypeStruct((width, HEAD_SIZE), jnp.bfloat16),
            jax.ShapeDtypeStruct((VALUE_ROWS, width), jnp.bfloat16),
        ),
        in_specs=[VMEM],
        out_specs=(VMEM, VMEM),
        compiler_params=pltpu.CompilerParams(vmem_limit_bytes=VMEM_LIMIT),
        cost_estimate=pl.CostEstimate(flops=0, bytes_accessed=2 * kv.size * 2, transcendentals=0),
        name="prepare",
    )(kv)


def lse_rows(block_count):
    return -(-3 * block_count // 16) * 16


def cross_kernel(key_count, pieces, position_ref, images_ref, owner_ref, q_ref, *refs):
    keys, values = refs[:pieces], refs[pieces : 2 * pieces]
    out_ref, high_ref, acc_ref, lse_ref = refs[2 * pieces :]
    block_count = q_ref.shape[0] // MASK_BLOCK_TOKENS
    width = q_ref.shape[1] // HEAD_SIZE * MASK_BLOCK_TOKENS
    chunk = 4 * LANES
    lse_ref[...] = jnp.zeros_like(lse_ref)

    def per_block(block, carry):
        queries = stacked_heads(q_ref, block)
        clear(high_ref, acc_ref)
        for piece in range(pieces):
            slot = lax.rem(position_ref[0] + (pieces - piece), pieces)
            seen = jnp.int32(0)
            for image in range(images_ref.shape[1]):
                seen = seen + jnp.where(owner_ref[image] == slot, images_ref[block, image], 0)

            @pl.when(seen > 0)
            def _(piece=piece):
                for start in range(0, keys[piece].shape[0], chunk):
                    stop = min(start + chunk, keys[piece].shape[0])
                    scores = nt_dot(keys[piece][start:stop, :], queries)
                    if stop > key_count:
                        key_id = start + lax.broadcasted_iota(jnp.int32, scores.shape, 0)
                        scores = jnp.where(key_id < key_count, scores, LOWEST)
                    fold(scores, values[piece][:, start:stop], high_ref, acc_ref)

        total = acc_ref[HEAD_SIZE : HEAD_SIZE + 1, :]
        at = pl.ds(pl.multiple_of(block * HEAD_SIZE, HEAD_SIZE), HEAD_SIZE)
        out_ref[at, :] = (acc_ref[0:HEAD_SIZE, :] / total).astype(jnp.bfloat16)
        lse_ref[pl.ds(block, 1), :] = high_ref[0:1, :] * LOG2_SCALE + jnp.log2(total)
        return carry

    lax.fori_loop(0, block_count, per_block, 0)
    lse = lse_ref[...]
    first = lse.astype(jnp.bfloat16).astype(jnp.float32)
    second = (lse - first).astype(jnp.bfloat16).astype(jnp.float32)
    third = lse - first - second
    parts = [part[0:block_count, :] for part in (first, second, third)]
    spare = lse_rows(block_count) - 3 * block_count
    if spare:
        parts.append(jnp.zeros((spare, width), jnp.float32))
    out_ref[block_count * HEAD_SIZE :, :] = jnp.concatenate(parts, axis=0).astype(jnp.bfloat16)


def cross_part(position, block_images, image_owner, queries, prepared, key_count):
    rows, columns = queries.shape
    pieces = len(prepared)
    block_count = rows // MASK_BLOCK_TOKENS
    width = columns // HEAD_SIZE * MASK_BLOCK_TOKENS
    out_rows = block_count * HEAD_SIZE + lse_rows(block_count)
    flops = 4 * block_count * width * key_count * HEAD_SIZE * 2
    return pl.pallas_call(
        functools.partial(cross_kernel, key_count, pieces),
        out_shape=jax.ShapeDtypeStruct((out_rows, width), jnp.bfloat16),
        in_specs=[SMEM, SMEM, SMEM] + [VMEM] * (1 + 2 * pieces),
        out_specs=VMEM,
        scratch_shapes=[
            pltpu.VMEM((8, width), jnp.float32),
            pltpu.VMEM((VALUE_ROWS, width), jnp.float32),
            pltpu.VMEM((-(-block_count // 8) * 8, width), jnp.float32),
        ],
        compiler_params=pltpu.CompilerParams(vmem_limit_bytes=VMEM_LIMIT),
        cost_estimate=pl.CostEstimate(flops=2 * flops, bytes_accessed=4 * 1024 * 1024, transcendentals=0),
        name="cross_part",
    )(position, block_images, image_owner, queries, *[p[0] for p in prepared], *[p[1] for p in prepared])


def combine_kernel(parts, *refs):
    part_refs, out_ref = refs[:parts], refs[parts]
    rows, columns = out_ref.shape
    block_count = rows // MASK_BLOCK_TOKENS
    first_lse = block_count * HEAD_SIZE
    lse = []
    for ref in part_refs:
        tail = ref[first_lse:, :].astype(jnp.float32)
        lse.append(
            tail[0:block_count] + tail[block_count : 2 * block_count] + tail[2 * block_count : 3 * block_count]
        )
    highest = functools.reduce(jnp.maximum, lse)
    weights = [jnp.exp2(one - highest) for one in lse]
    total = functools.reduce(jnp.add, weights)
    weights = [one / total for one in weights]
    for block in range(block_count):
        mixed = 0.0
        for ref, weight in zip(part_refs, weights):
            mixed = mixed + weight[block : block + 1, :] * ref[
                block * HEAD_SIZE : (block + 1) * HEAD_SIZE, :
            ].astype(jnp.float32)
        for head in range(columns // HEAD_SIZE):
            piece = mixed[:, head * MASK_BLOCK_TOKENS : (head + 1) * MASK_BLOCK_TOKENS]
            out_ref[
                block * MASK_BLOCK_TOKENS : (block + 1) * MASK_BLOCK_TOKENS,
                head * HEAD_SIZE : (head + 1) * HEAD_SIZE,
            ] = piece.T.astype(jnp.bfloat16)


def combined(parts, shape):
    return pl.pallas_call(
        functools.partial(combine_kernel, len(parts)),
        out_shape=jax.ShapeDtypeStruct(shape, jnp.bfloat16),
        in_specs=[VMEM] * len(parts),
        out_specs=VMEM,
        compiler_params=pltpu.CompilerParams(vmem_limit_bytes=VMEM_LIMIT),
        cost_estimate=pl.CostEstimate(flops=0, bytes_accessed=2 * 1024 * 1024, transcendentals=0),
        name="combine",
    )(*parts)


def self_kernel(pieces, position_ref, q_ref, *refs):
    texts = refs[:pieces]
    out_ref, value_ref, high_ref, acc_ref = refs[pieces:]
    rows, columns = q_ref.shape
    block_count = rows // MASK_BLOCK_TOKENS
    heads = columns // HEAD_SIZE
    width = heads * MASK_BLOCK_TOKENS
    ones = (lax.broadcasted_iota(jnp.int32, (VALUE_ROWS - HEAD_SIZE, rows), 0) == 0).astype(jnp.bfloat16)
    for piece in range(pieces):
        value_ref[piece, 0:HEAD_SIZE, :] = texts[piece][:, HEAD_SIZE:].T
        value_ref[piece, HEAD_SIZE:, :] = ones
    for block in range(block_count):
        queries = stacked_heads(q_ref, block)
        clear(high_ref, acc_ref)
        before = block * MASK_BLOCK_TOKENS
        if before:
            scores = nt_dot(texts[0][0:before, 0:HEAD_SIZE], queries)
            fold(scores, value_ref[0, :, 0:before], high_ref, acc_ref)
        stop = before + MASK_BLOCK_TOKENS
        scores = nt_dot(texts[0][before:stop, 0:HEAD_SIZE], queries)
        key_id = lax.broadcasted_iota(jnp.int32, scores.shape, 0)
        query_id = lax.broadcasted_iota(jnp.int32, scores.shape, 1) % MASK_BLOCK_TOKENS
        scores = jnp.where(key_id <= query_id, scores, LOWEST)
        fold(scores, value_ref[0, :, before:stop], high_ref, acc_ref)
        for piece in range(1, pieces):

            @pl.when(position_ref[0] >= piece)
            def _(piece=piece):
                scores = nt_dot(texts[piece][:, 0:HEAD_SIZE], queries)
                fold(scores, value_ref[piece], high_ref, acc_ref)

        mixed = acc_ref[0:HEAD_SIZE, :] / acc_ref[HEAD_SIZE : HEAD_SIZE + 1, :]
        for head in range(heads):
            out_ref[before:stop, head * HEAD_SIZE : (head + 1) * HEAD_SIZE] = mixed[
                :, head * MASK_BLOCK_TOKENS : (head + 1) * MASK_BLOCK_TOKENS
            ].T.astype(jnp.bfloat16)


def self_attention(position, queries, texts):
    rows, columns = queries.shape
    pieces = len(texts)
    width = columns // HEAD_SIZE * MASK_BLOCK_TOKENS
    return pl.pallas_call(
        functools.partial(self_kernel, pieces),
        out_shape=jax.ShapeDtypeStruct((rows, columns), jnp.bfloat16),
        in_specs=[SMEM] + [VMEM] * (1 + pieces),
        out_specs=VMEM,
        scratch_shapes=[
            pltpu.VMEM((pieces, VALUE_ROWS, rows), jnp.bfloat16),
            pltpu.VMEM((8, width), jnp.float32),
            pltpu.VMEM((VALUE_ROWS, width), jnp.float32),
        ],
        compiler_params=pltpu.CompilerParams(vmem_limit_bytes=VMEM_LIMIT),
        cost_estimate=pl.CostEstimate(flops=2 * rows * columns * rows * 4, bytes_accessed=1024 * 1024, transcendentals=0),
        name="self_attention",
    )(position, queries, *texts)


def shifted(value, axis, steps):
    count = lax.axis_size(axis)
    return lax.ppermute(value, axis, [(source, (source + steps) % count) for source in range(count)])


def per_device(self_queries, text_kv, cross_queries, image_kv, block_images, image_owner):
    rows = self_queries.shape[0]
    key_count = image_kv.shape[2]
    cycle = lax.axis_size("blk")
    ring = lax.axis_size("enc")
    position = lax.axis_index("blk").astype(jnp.int32)[None]

    images = [image_kv[0]]
    for _ in range(1, cycle):
        images.append(shifted(images[-1], "blk", 1))
    order = sorted(range(1, ring), key=lambda step: (abs(2 * step - ring), step))
    group_queries = {step: shifted(cross_queries, "enc", ring - step) for step in order}
    group_queries[0] = cross_queries

    text = text_kv.reshape(rows, 2 * HEAD_SIZE)
    after, _ = lax.optimization_barrier((text, images[-1]))
    texts = [text]
    for step in range(1, cycle):
        after = lax.ppermute(after, "blk", [(source, source + 1) for source in range(cycle - 1)])
        texts.append(after)

    prepared = [prepare(image) for image in images]
    part = functools.partial(cross_part, position, block_images, image_owner)
    received = []
    for step in order:
        mine = part(group_queries[step], prepared, key_count)
        received.append(shifted(mine, "enc", step))
    own = part(group_queries[0], prepared, key_count)
    self_out = self_attention(position, self_queries, texts)
    cross_out = combined([own] + received, cross_queries.shape)
    return (self_out, cross_out)


def solution(mesh):
    placed = (
        P("blk", ("tp", "enc")),
        P("blk", None, "tp"),
        P("blk", ("tp", "enc")),
        P("blk", None, "enc", "tp"),
        P("blk", None),
        P(),
    )
    return jax.shard_map(
        per_device,
        mesh=mesh,
        in_specs=placed,
        out_specs=(P("blk", ("tp", "enc")), P("blk", ("tp", "enc"))),
        check_vma=False,
    )
```

```python
import functools
import math

import jax
import jax.numpy as jnp
from jax import lax
from jax.experimental import pallas as pl
from jax.experimental.pallas import tpu as pltpu
from jax.sharding import PartitionSpec as P

HEAD_SIZE = 128
MASK_BLOCK_TOKENS = 128
LANES = 128
LOWEST = -1e30
LOG2_SCALE = math.log2(math.e) / math.sqrt(HEAD_SIZE)
VMEM_LIMIT = 48 * 1024 * 1024

VMEM = pl.BlockSpec(memory_space=pltpu.VMEM)
SMEM = pl.BlockSpec(memory_space=pltpu.SMEM)


def padded(count):
    return -(-count // LANES) * LANES


def nt_dot(a, b):
    return lax.dot_general(a, b, (((1,), (1,)), ((), ())), preferred_element_type=jnp.float32)


def at_block(block):
    return pl.ds(pl.multiple_of(block * MASK_BLOCK_TOKENS, MASK_BLOCK_TOKENS), MASK_BLOCK_TOKENS)


def stacked_heads(rows):
    heads = rows.shape[1] // HEAD_SIZE
    return jnp.concatenate([rows[:, h * HEAD_SIZE : (h + 1) * HEAD_SIZE] for h in range(heads)], axis=0)


def lane_tiles(wide):
    return [wide[:, at : at + LANES] for at in range(0, wide.shape[1], LANES)]


def empty_state(rows):
    return (
        jnp.full((rows, 1), LOWEST, jnp.float32),
        jnp.zeros((rows, LANES), jnp.float32),
        jnp.zeros((rows, HEAD_SIZE), jnp.float32),
    )


def fold(state, scores, value):
    high, total, mixed = state
    new_high = jnp.maximum(high, jnp.max(functools.reduce(jnp.maximum, lane_tiles(scores)), axis=1, keepdims=True))
    weights = jnp.exp2(scores * LOG2_SCALE - new_high * LOG2_SCALE)
    fading = jnp.exp2((high - new_high) * LOG2_SCALE)
    total = total * fading + functools.reduce(jnp.add, lane_tiles(weights))
    mixed = mixed * fading + jnp.dot(weights.astype(jnp.bfloat16), value, preferred_element_type=jnp.float32)
    return (new_high, total, mixed)


def prepare_kernel(kv_ref, out_ref):
    count = kv_ref.shape[1]
    whole = count // LANES * LANES
    rest = count - whole
    for at in range(0, whole, LANES):
        out_ref[0, at : at + LANES, :] = kv_ref[0, at : at + LANES, :].T
    out_ref[1, 0:whole, :] = kv_ref[1, 0:whole, :]
    if rest:
        empty = jnp.zeros((LANES - rest, HEAD_SIZE), jnp.float32)
        tail_key = jnp.concatenate([kv_ref[0, whole:count, :].astype(jnp.float32), empty], axis=0)
        tail_value = jnp.concatenate([kv_ref[1, whole:count, :].astype(jnp.float32), empty], axis=0)
        out_ref[0, whole : whole + LANES, :] = tail_key.T.astype(jnp.bfloat16)
        out_ref[1, whole : whole + LANES, :] = tail_value.astype(jnp.bfloat16)


def prepare(kv):
    return pl.pallas_call(
        prepare_kernel,
        out_shape=jax.ShapeDtypeStruct((2, padded(kv.shape[1]), HEAD_SIZE), jnp.bfloat16),
        in_specs=[VMEM],
        out_specs=VMEM,
        compiler_params=pltpu.CompilerParams(vmem_limit_bytes=VMEM_LIMIT),
        cost_estimate=pl.CostEstimate(flops=0, bytes_accessed=2 * kv.size * 2, transcendentals=0),
        name="prepare",
    )(kv)


def chunk_starts(width):
    half = width // LANES // 2 * LANES
    return [(0, half), (half, width)] if half else [(0, width)]


def lse_rows(block_count):
    return -(-3 * block_count // 16) * 16


def cross_kernel(key_count, pieces, offset, last, position_ref, images_ref, owner_ref, q_ref, *refs):
    images, refs = refs[:pieces], refs[pieces:]
    if offset:
        before, refs = refs[:3], refs[3:]
    if last:
        out_ref, lse_ref = refs[0], refs[1]
        state_refs = refs[2:]
        lse_ref[...] = jnp.zeros_like(lse_ref)
    else:
        state_refs = refs
    slots = images_ref.shape[1]
    block_count = q_ref.shape[0] // MASK_BLOCK_TOKENS
    heads = q_ref.shape[1] // HEAD_SIZE
    rows = heads * MASK_BLOCK_TOKENS

    def per_block(block, carry):
        at = pl.ds(pl.multiple_of(block * rows, rows), rows)
        here = at if not last else slice(None)
        if offset:
            for ref, old in zip(state_refs, before):
                ref[here, :] = old[at, :]
        else:
            for ref, value in zip(state_refs, empty_state(rows)):
                ref[here, :] = jnp.broadcast_to(value, (rows, LANES))
        for piece in range(pieces):
            slot = lax.rem(position_ref[0] + (slots - offset - piece), slots)
            seen = jnp.int32(0)
            for image in range(slots):
                seen = seen + jnp.where(owner_ref[image] == slot, images_ref[block, image], 0)

            @pl.when(seen > 0)
            def _(piece=piece):
                image = images[piece]
                queries = stacked_heads(q_ref[at_block(block), :])
                state = (state_refs[0][here, 0:1], state_refs[1][here, :], state_refs[2][here, :])
                for start, stop in chunk_starts(image.shape[1]):
                    keys = jnp.concatenate(
                        [image[0, c : c + LANES, :] for c in range(start, stop, LANES)], axis=1
                    )
                    scores = jnp.dot(queries, keys, preferred_element_type=jnp.float32)
                    if stop > key_count:
                        key_id = start + lax.broadcasted_iota(jnp.int32, scores.shape, 1)
                        scores = jnp.where(key_id < key_count, scores, LOWEST)
                    state = fold(state, scores, image[1, start:stop, :])
                for ref, value in zip(state_refs, state):
                    ref[here, :] = jnp.broadcast_to(value, (rows, LANES))

        if last:
            total = jnp.sum(state_refs[1][...], axis=1, keepdims=True)
            mixed = state_refs[2][...] / total
            lse = state_refs[0][...] * LOG2_SCALE + jnp.log2(total)
            for head in range(heads):
                own = slice(head * MASK_BLOCK_TOKENS, (head + 1) * MASK_BLOCK_TOKENS)
                out_ref[at_block(block), head * HEAD_SIZE : (head + 1) * HEAD_SIZE] = mixed[own].astype(jnp.bfloat16)
                row = lax.broadcasted_iota(jnp.int32, (lse_ref.shape[0], MASK_BLOCK_TOKENS), 0)
                lse_ref[:, own] = jnp.where(row == block, lse[own].T[0:1, :], lse_ref[:, own])
        return carry

    lax.fori_loop(0, block_count, per_block, 0)
    if last:
        lse = lse_ref[...]
        first = lse.astype(jnp.bfloat16).astype(jnp.float32)
        second = (lse - first).astype(jnp.bfloat16).astype(jnp.float32)
        third = lse - first - second
        parts = [part[0:block_count, :] for part in (first, second, third)]
        spare = lse_rows(block_count) - 3 * block_count
        if spare:
            parts.append(jnp.zeros((spare, rows), jnp.float32))
        out_ref[q_ref.shape[0] :, :] = jnp.concatenate(parts, axis=0).astype(jnp.bfloat16)


def cross_part(tables, queries, images, key_count, offset, last, before=()):
    tokens, columns = queries.shape
    block_count = tokens // MASK_BLOCK_TOKENS
    rows = columns // HEAD_SIZE * MASK_BLOCK_TOKENS
    if last:
        out_shape = jax.ShapeDtypeStruct((tokens + lse_rows(block_count), columns), jnp.bfloat16)
        scratch = [pltpu.VMEM((-(-block_count // 8) * 8, rows), jnp.float32)]
        scratch += [pltpu.VMEM((rows, LANES), jnp.float32)] * 3
    else:
        out_shape = (jax.ShapeDtypeStruct((block_count * rows, LANES), jnp.float32),) * 3
        scratch = []
    flops = 4 * block_count * rows * key_count * HEAD_SIZE * len(images)
    return pl.pallas_call(
        functools.partial(cross_kernel, key_count, len(images), offset, last),
        out_shape=out_shape,
        in_specs=[SMEM, SMEM, SMEM] + [VMEM] * (1 + len(images) + len(before)),
        out_specs=VMEM if last else (VMEM,) * 3,
        scratch_shapes=scratch,
        compiler_params=pltpu.CompilerParams(vmem_limit_bytes=VMEM_LIMIT),
        cost_estimate=pl.CostEstimate(flops=2 * flops, bytes_accessed=4 * 1024 * 1024, transcendentals=0),
        name="cross_last" if last else "cross_first",
    )(*tables, queries, *images, *before)


def combine_kernel(parts, *refs):
    part_refs, out_ref = refs[:parts], refs[parts]
    tokens, columns = out_ref.shape
    block_count = tokens // MASK_BLOCK_TOKENS
    heads = columns // HEAD_SIZE
    lse = []
    for ref in part_refs:
        tail = ref[tokens:, :].astype(jnp.float32)
        lse.append(
            tail[0:block_count] + tail[block_count : 2 * block_count] + tail[2 * block_count : 3 * block_count]
        )
    highest = functools.reduce(jnp.maximum, lse)
    weights = [jnp.exp2(one - highest) for one in lse]
    total = functools.reduce(jnp.add, weights)
    by_row = [
        (one / total)[:, head * MASK_BLOCK_TOKENS : (head + 1) * MASK_BLOCK_TOKENS]
        for one in weights
        for head in range(heads)
    ]
    used = len(by_row) * block_count
    by_row.append(jnp.zeros((padded(used) - used, MASK_BLOCK_TOKENS), jnp.float32))
    columns_of = jnp.concatenate(by_row, axis=0).T
    for block in range(block_count):
        at = slice(block * MASK_BLOCK_TOKENS, (block + 1) * MASK_BLOCK_TOKENS)
        for head in range(heads):
            dims = slice(head * HEAD_SIZE, (head + 1) * HEAD_SIZE)
            mixed = 0.0
            for index, ref in enumerate(part_refs):
                column = (index * heads + head) * block_count + block
                mixed = mixed + columns_of[:, column : column + 1] * ref[at, dims].astype(jnp.float32)
            out_ref[at, dims] = mixed.astype(jnp.bfloat16)


def combined(parts, shape):
    return pl.pallas_call(
        functools.partial(combine_kernel, len(parts)),
        out_shape=jax.ShapeDtypeStruct(shape, jnp.bfloat16),
        in_specs=[VMEM] * len(parts),
        out_specs=VMEM,
        compiler_params=pltpu.CompilerParams(vmem_limit_bytes=VMEM_LIMIT),
        cost_estimate=pl.CostEstimate(flops=0, bytes_accessed=2 * 1024 * 1024, transcendentals=0),
        name="combine",
    )(*parts)


def self_kernel(pieces, position_ref, q_ref, *refs):
    texts = refs[:pieces]
    out_ref, high_ref, total_ref, mixed_ref = refs[pieces:]
    tokens, columns = q_ref.shape
    heads = columns // HEAD_SIZE
    rows = heads * MASK_BLOCK_TOKENS
    state_refs = (high_ref, total_ref, mixed_ref)
    for block in range(tokens // MASK_BLOCK_TOKENS):
        start = block * MASK_BLOCK_TOKENS
        stop = start + MASK_BLOCK_TOKENS
        queries = stacked_heads(q_ref[start:stop, :])
        scores = nt_dot(queries, texts[0][0:stop, 0:HEAD_SIZE])
        key_id = lax.broadcasted_iota(jnp.int32, scores.shape, 1)
        query_id = start + lax.broadcasted_iota(jnp.int32, scores.shape, 0) % MASK_BLOCK_TOKENS
        scores = jnp.where(key_id <= query_id, scores, LOWEST)
        state = fold(empty_state(rows), scores, texts[0][0:stop, HEAD_SIZE:])
        for ref, value in zip(state_refs, state):
            ref[...] = jnp.broadcast_to(value, (rows, LANES))
        for piece in range(1, pieces):

            @pl.when(position_ref[0] >= piece)
            def _(piece=piece):
                scores = nt_dot(queries, texts[piece][:, 0:HEAD_SIZE])
                state = fold((high_ref[:, 0:1], total_ref[...], mixed_ref[...]), scores, texts[piece][:, HEAD_SIZE:])
                for ref, value in zip(state_refs, state):
                    ref[...] = jnp.broadcast_to(value, (rows, LANES))

        mixed = mixed_ref[...] / jnp.sum(total_ref[...], axis=1, keepdims=True)
        for head in range(heads):
            out_ref[start:stop, head * HEAD_SIZE : (head + 1) * HEAD_SIZE] = mixed[
                head * MASK_BLOCK_TOKENS : (head + 1) * MASK_BLOCK_TOKENS
            ].astype(jnp.bfloat16)


def self_attention(position, queries, texts):
    tokens, columns = queries.shape
    pieces = len(texts)
    rows = columns // HEAD_SIZE * MASK_BLOCK_TOKENS
    return pl.pallas_call(
        functools.partial(self_kernel, pieces),
        out_shape=jax.ShapeDtypeStruct((tokens, columns), jnp.bfloat16),
        in_specs=[SMEM] + [VMEM] * (1 + pieces),
        out_specs=VMEM,
        scratch_shapes=[pltpu.VMEM((rows, LANES), jnp.float32)] * 3,
        compiler_params=pltpu.CompilerParams(vmem_limit_bytes=VMEM_LIMIT),
        cost_estimate=pl.CostEstimate(flops=8 * tokens * columns * tokens, bytes_accessed=1024 * 1024, transcendentals=0),
        name="self_attention",
    )(position, queries, *texts)


def shifted(value, axis, steps):
    count = lax.axis_size(axis)
    return lax.ppermute(value, axis, [(source, (source + steps) % count) for source in range(count)])


def per_device(self_queries, text_kv, cross_queries, image_kv, block_images, image_owner):
    rows = self_queries.shape[0]
    key_count = image_kv.shape[2]
    cycle = lax.axis_size("blk")
    ring = lax.axis_size("enc")
    position = lax.axis_index("blk").astype(jnp.int32)[None]

    tables = (position, block_images, image_owner)

    images = [prepare(image_kv[0])]
    for _ in range(1, cycle):
        images.append(shifted(images[-1], "blk", 1))
    order = sorted(range(1, ring), key=lambda step: (abs(2 * step - ring), step))
    queries = {step: shifted(cross_queries, "enc", ring - step) for step in order}
    queries[0] = cross_queries

    alone = cycle == 1
    states = {}
    for step in [0] + order:
        states[step] = () if alone else cross_part(tables, queries[step], images[:1], key_count, 0, False)

    def finished(step):
        offset = 0 if alone else 1
        return cross_part(tables, queries[step], images[offset:], key_count, offset, True, states[step])

    received = [shifted(finished(step), "enc", step) for step in order]

    text = text_kv.reshape(rows, 2 * HEAD_SIZE)
    after, _ = lax.optimization_barrier((text, images[-1]))
    texts = [text]
    for step in range(1, cycle):
        after = lax.ppermute(after, "blk", [(source, source + 1) for source in range(cycle - 1)])
        texts.append(after)

    own = finished(0)
    self_out = self_attention(position, self_queries, texts)
    cross_out = combined([own] + received, cross_queries.shape)
    return (self_out, cross_out)


def solution(mesh):
    placed = (
        P("blk", ("tp", "enc")),
        P("blk", None, "tp"),
        P("blk", ("tp", "enc")),
        P("blk", None, "enc", "tp"),
        P("blk", None),
        P(),
    )
    return jax.shard_map(
        per_device,
        mesh=mesh,
        in_specs=placed,
        out_specs=(P("blk", ("tp", "enc")), P("blk", ("tp", "enc"))),
        check_vma=False,
    )
```

```python
import functools
import math

import jax
import jax.numpy as jnp
from jax import lax
from jax.experimental import pallas as pl
from jax.experimental.pallas import tpu as pltpu
from jax.sharding import PartitionSpec as P

HEAD_SIZE = 128
MASK_BLOCK_TOKENS = 128
LANES = 128
LOWEST = -1e30
MIXED_ROWS = HEAD_SIZE + 16
SHIFT_KEYS = 256
MOST_SUM = 2.0**100
LOG2_SCALE = math.log2(math.e) / math.sqrt(HEAD_SIZE)
VMEM_LIMIT = 48 * 1024 * 1024

VMEM = pl.BlockSpec(memory_space=pltpu.VMEM)
SMEM = pl.BlockSpec(memory_space=pltpu.SMEM)


def padded(count):
    return -(-count // LANES) * LANES


def nt_dot(a, b):
    return lax.dot_general(a, b, (((1,), (1,)), ((), ())), preferred_element_type=jnp.float32)


def at_block(block, size):
    return pl.ds(pl.multiple_of(block * size, size), size)


def stacked_heads(rows):
    heads = rows.shape[1] // HEAD_SIZE
    return jnp.concatenate([rows[:, h * HEAD_SIZE : (h + 1) * HEAD_SIZE] for h in range(heads)], axis=0)


def with_ones(value_t):
    shape = (MIXED_ROWS - HEAD_SIZE, value_t.shape[1])
    ones = (lax.broadcasted_iota(jnp.int32, shape, 0) == 0).astype(jnp.bfloat16)
    return jnp.concatenate([value_t, ones], axis=0)


def fold(high, mixed, scores, value_t, exact):
    seen = scores if exact else scores[0 : min(SHIFT_KEYS, scores.shape[0]), :]
    new_high = jnp.maximum(high, jnp.max(seen, axis=0, keepdims=True))
    weights = jnp.exp2(scores * LOG2_SCALE - new_high * LOG2_SCALE).astype(jnp.bfloat16)
    fading = jnp.exp2((high - new_high) * LOG2_SCALE)
    mixed = mixed * fading + jnp.dot(with_ones(value_t), weights, preferred_element_type=jnp.float32)
    return new_high, mixed


def prepare_kernel(kv_ref, out_ref):
    count = kv_ref.shape[1]
    whole = count // LANES * LANES
    rest = count - whole
    out_ref[0, 0:whole, :] = kv_ref[0, 0:whole, :]
    for at in range(0, whole, LANES):
        out_ref[1, at : at + LANES, :] = kv_ref[1, at : at + LANES, :].T
    if rest:
        empty = jnp.zeros((LANES - rest, HEAD_SIZE), jnp.float32)
        tail_key = jnp.concatenate([kv_ref[0, whole:count, :].astype(jnp.float32), empty], axis=0)
        tail_value = jnp.concatenate([kv_ref[1, whole:count, :].astype(jnp.float32), empty], axis=0)
        out_ref[0, whole : whole + LANES, :] = tail_key.astype(jnp.bfloat16)
        out_ref[1, whole : whole + LANES, :] = tail_value.T.astype(jnp.bfloat16)


def prepare(kv):
    return pl.pallas_call(
        prepare_kernel,
        out_shape=jax.ShapeDtypeStruct((2, padded(kv.shape[1]), HEAD_SIZE), jnp.bfloat16),
        in_specs=[VMEM],
        out_specs=VMEM,
        compiler_params=pltpu.CompilerParams(vmem_limit_bytes=VMEM_LIMIT),
        cost_estimate=pl.CostEstimate(flops=0, bytes_accessed=2 * kv.size * 2, transcendentals=0),
        name="prepare",
    )(kv)


def lse_rows(block_count):
    return -(-3 * block_count // 16) * 16


def cross_kernel(key_count, pieces, offset, last, position_ref, images_ref, owner_ref, q_ref, *refs):
    images, refs = refs[:pieces], refs[pieces:]
    if offset:
        before, refs = refs[:2], refs[2:]
    if last:
        out_ref, lse_ref, high_ref, mixed_ref, most_ref = refs
        lse_ref[...] = jnp.zeros_like(lse_ref)
    else:
        high_ref, mixed_ref, most_ref = refs
    slots = images_ref.shape[1]
    block_count = q_ref.shape[0] // MASK_BLOCK_TOKENS
    heads = q_ref.shape[1] // HEAD_SIZE
    rows = heads * MASK_BLOCK_TOKENS

    def attempt(exact):
        most_ref[...] = jnp.zeros_like(most_ref)

        def per_block(block, carry):
            here = 0 if last else block
            if offset:
                high_ref[here] = before[0][block]
                mixed_ref[here] = before[1][block]
            else:
                high_ref[here] = jnp.full(high_ref.shape[1:], LOWEST, jnp.float32)
                mixed_ref[here] = jnp.zeros(mixed_ref.shape[1:], jnp.float32)
            for piece in range(pieces):
                slot = lax.rem(position_ref[0] + (slots - offset - piece), slots)
                seen = jnp.int32(0)
                for image in range(slots):
                    seen = seen + jnp.where(owner_ref[image] == slot, images_ref[block, image], 0)

                @pl.when(seen > 0)
                def _(piece=piece):
                    image = images[piece]
                    width = image.shape[1]
                    queries = stacked_heads(q_ref[at_block(block, MASK_BLOCK_TOKENS), :])
                    scores = nt_dot(image[0], queries)
                    if width > key_count:
                        body = width - LANES
                        tail = scores[body:, :]
                        key_id = body + lax.broadcasted_iota(jnp.int32, tail.shape, 0)
                        tail = jnp.where(key_id < key_count, tail, LOWEST)
                        scores = jnp.concatenate([scores[:body, :], tail], axis=0) if body else tail
                    value_t = jnp.concatenate([image[1, c : c + LANES, :] for c in range(0, width, LANES)], axis=1)
                    high, mixed = fold(high_ref[here][0:1], mixed_ref[here], scores, value_t, exact)
                    high_ref[here] = jnp.broadcast_to(high, high_ref.shape[1:])
                    mixed_ref[here] = mixed

            total = mixed_ref[here][HEAD_SIZE : HEAD_SIZE + 1, :]
            most_ref[0:1, :] = jnp.maximum(most_ref[0:1, :], total)
            if last:
                out_ref[at_block(block, HEAD_SIZE), :] = (mixed_ref[here][0:HEAD_SIZE, :] / total).astype(jnp.bfloat16)
                lse = high_ref[here][0:1] * LOG2_SCALE + jnp.log2(total)
                row = lax.broadcasted_iota(jnp.int32, lse_ref.shape, 0)
                lse_ref[...] = jnp.where(row == block, lse, lse_ref[...])
            return carry

        lax.fori_loop(0, block_count, per_block, 0)

    attempt(False)
    fine = jnp.min((most_ref[0:1, :] <= MOST_SUM).astype(jnp.int32))

    @pl.when(fine == 0)
    def _():
        attempt(True)

    if last:
        lse = lse_ref[...]
        first = lse.astype(jnp.bfloat16).astype(jnp.float32)
        second = (lse - first).astype(jnp.bfloat16).astype(jnp.float32)
        third = lse - first - second
        parts = [part[0:block_count, :] for part in (first, second, third)]
        spare = lse_rows(block_count) - 3 * block_count
        if spare:
            parts.append(jnp.zeros((spare, rows), jnp.float32))
        out_ref[block_count * HEAD_SIZE :, :] = jnp.concatenate(parts, axis=0).astype(jnp.bfloat16)


def cross_part(tables, queries, images, key_count, offset, last, before=()):
    tokens, columns = queries.shape
    block_count = tokens // MASK_BLOCK_TOKENS
    rows = columns // HEAD_SIZE * MASK_BLOCK_TOKENS
    state = [(8, rows), (MIXED_ROWS, rows)]
    scratch = [pltpu.VMEM((8, rows), jnp.float32)]
    if last:
        out_shape = jax.ShapeDtypeStruct((block_count * HEAD_SIZE + lse_rows(block_count), rows), jnp.bfloat16)
        scratch = [pltpu.VMEM((1,) + shape, jnp.float32) for shape in state] + scratch
        scratch = [pltpu.VMEM((-(-block_count // 8) * 8, rows), jnp.float32)] + scratch
    else:
        out_shape = tuple(jax.ShapeDtypeStruct((block_count,) + shape, jnp.float32) for shape in state)
    flops = 4 * block_count * rows * key_count * HEAD_SIZE * len(images)
    return pl.pallas_call(
        functools.partial(cross_kernel, key_count, len(images), offset, last),
        out_shape=out_shape,
        in_specs=[SMEM, SMEM, SMEM] + [VMEM] * (1 + len(images) + len(before)),
        out_specs=VMEM if last else (VMEM,) * 2,
        scratch_shapes=scratch,
        compiler_params=pltpu.CompilerParams(vmem_limit_bytes=VMEM_LIMIT),
        cost_estimate=pl.CostEstimate(flops=2 * flops, bytes_accessed=4 * 1024 * 1024, transcendentals=0),
        name="cross_last" if last else "cross_first",
    )(*tables, queries, *images, *before)


def combine_kernel(parts, *refs):
    part_refs, out_ref = refs[:parts], refs[parts]
    tokens, columns = out_ref.shape
    block_count = tokens // MASK_BLOCK_TOKENS
    first_lse = block_count * HEAD_SIZE
    lse = []
    for ref in part_refs:
        tail = ref[first_lse:, :].astype(jnp.float32)
        lse.append(
            tail[0:block_count] + tail[block_count : 2 * block_count] + tail[2 * block_count : 3 * block_count]
        )
    highest = functools.reduce(jnp.maximum, lse)
    weights = [jnp.exp2(one - highest) for one in lse]
    total = functools.reduce(jnp.add, weights)
    weights = [one / total for one in weights]
    for block in range(block_count):
        mixed = 0.0
        for ref, weight in zip(part_refs, weights):
            part = ref[block * HEAD_SIZE : (block + 1) * HEAD_SIZE, :].astype(jnp.float32)
            mixed = mixed + weight[block : block + 1, :] * part
        store_heads(out_ref, block, mixed)


def store_heads(out_ref, block, mixed):
    at = slice(block * MASK_BLOCK_TOKENS, (block + 1) * MASK_BLOCK_TOKENS)
    for head in range(out_ref.shape[1] // HEAD_SIZE):
        piece = mixed[:, head * MASK_BLOCK_TOKENS : (head + 1) * MASK_BLOCK_TOKENS]
        out_ref[at, head * HEAD_SIZE : (head + 1) * HEAD_SIZE] = piece.T.astype(jnp.bfloat16)


def combined(parts, shape):
    return pl.pallas_call(
        functools.partial(combine_kernel, len(parts)),
        out_shape=jax.ShapeDtypeStruct(shape, jnp.bfloat16),
        in_specs=[VMEM] * len(parts),
        out_specs=VMEM,
        compiler_params=pltpu.CompilerParams(vmem_limit_bytes=VMEM_LIMIT),
        cost_estimate=pl.CostEstimate(flops=0, bytes_accessed=2 * 1024 * 1024, transcendentals=0),
        name="combine",
    )(*parts)


def self_kernel(pieces, position_ref, q_ref, *refs):
    texts = refs[:pieces]
    out_ref, value_ref, high_ref, mixed_ref = refs[pieces:]
    tokens, columns = q_ref.shape
    rows = columns // HEAD_SIZE * MASK_BLOCK_TOKENS
    value_ref[0] = texts[0][:, HEAD_SIZE:].T
    for piece in range(1, pieces):

        @pl.when(position_ref[0] >= piece)
        def _(piece=piece):
            value_ref[piece] = texts[piece][:, HEAD_SIZE:].T

    for block in range(tokens // MASK_BLOCK_TOKENS):
        start = block * MASK_BLOCK_TOKENS
        stop = start + MASK_BLOCK_TOKENS
        queries = stacked_heads(q_ref[start:stop, :])
        scores = nt_dot(texts[0][0:stop, 0:HEAD_SIZE], queries)
        tail = scores[start:, :]
        key_id = lax.broadcasted_iota(jnp.int32, tail.shape, 0)
        query_id = lax.broadcasted_iota(jnp.int32, tail.shape, 1) % MASK_BLOCK_TOKENS
        tail = jnp.where(key_id <= query_id, tail, LOWEST)
        scores = jnp.concatenate([scores[:start, :], tail], axis=0) if start else tail
        high = jnp.full((1, rows), LOWEST, jnp.float32)
        mixed = jnp.zeros((MIXED_ROWS, rows), jnp.float32)
        high, mixed = fold(high, mixed, scores, value_ref[0, :, 0:stop], True)
        high_ref[0:1, :] = high
        mixed_ref[...] = mixed
        for piece in range(1, pieces):

            @pl.when(position_ref[0] >= piece)
            def _(piece=piece):
                scores = nt_dot(texts[piece][:, 0:HEAD_SIZE], queries)
                high, mixed = fold(high_ref[0:1, :], mixed_ref[...], scores, value_ref[piece], True)
                high_ref[0:1, :] = high
                mixed_ref[...] = mixed

        store_heads(out_ref, block, mixed_ref[0:HEAD_SIZE, :] / mixed_ref[HEAD_SIZE : HEAD_SIZE + 1, :])


def self_attention(position, queries, texts):
    tokens, columns = queries.shape
    pieces = len(texts)
    rows = columns // HEAD_SIZE * MASK_BLOCK_TOKENS
    return pl.pallas_call(
        functools.partial(self_kernel, pieces),
        out_shape=jax.ShapeDtypeStruct((tokens, columns), jnp.bfloat16),
        in_specs=[SMEM] + [VMEM] * (1 + pieces),
        out_specs=VMEM,
        scratch_shapes=[
            pltpu.VMEM((pieces, HEAD_SIZE, tokens), jnp.bfloat16),
            pltpu.VMEM((8, rows), jnp.float32),
            pltpu.VMEM((MIXED_ROWS, rows), jnp.float32),
        ],
        compiler_params=pltpu.CompilerParams(vmem_limit_bytes=VMEM_LIMIT),
        cost_estimate=pl.CostEstimate(flops=8 * tokens * columns * tokens, bytes_accessed=1024 * 1024, transcendentals=0),
        name="self_attention",
    )(position, queries, *texts)


def shifted(value, axis, steps):
    count = lax.axis_size(axis)
    return lax.ppermute(value, axis, [(source, (source + steps) % count) for source in range(count)])


def per_device(self_queries, text_kv, cross_queries, image_kv, block_images, image_owner):
    rows = self_queries.shape[0]
    key_count = image_kv.shape[2]
    cycle = lax.axis_size("blk")
    ring = lax.axis_size("enc")
    position = lax.axis_index("blk").astype(jnp.int32)[None]

    tables = (position, block_images, image_owner)

    images = [prepare(image_kv[0])]
    for _ in range(1, cycle):
        images.append(shifted(images[-1], "blk", 1))
    order = sorted(range(1, ring), key=lambda step: (abs(2 * step - ring), step))
    queries = {step: shifted(cross_queries, "enc", ring - step) for step in order}
    queries[0] = cross_queries

    text = text_kv.reshape(rows, 2 * HEAD_SIZE)
    texts = [text]
    for step in range(1, cycle):
        texts.append(lax.ppermute(texts[-1], "blk", [(source, source + 1) for source in range(cycle - 1)]))

    alone = cycle == 1
    states = {0: ()}
    if not alone:
        states[0] = cross_part(tables, queries[0], images[:1], key_count, 0, False)
    earlier = states[0]
    for step in order:
        if alone:
            states[step] = ()
        else:
            queries[step], _ = lax.optimization_barrier((queries[step], earlier))
            earlier = states[step] = cross_part(tables, queries[step], images[:1], key_count, 0, False)

    def finished(step):
        offset = 0 if alone else 1
        return cross_part(tables, queries[step], images[offset:], key_count, offset, True, states[step])

    received = [shifted(finished(step), "enc", step) for step in order]

    own = finished(0)
    self_out = self_attention(position, self_queries, texts)
    cross_out = combined([own] + received, cross_queries.shape)
    return (self_out, cross_out)


def solution(mesh):
    placed = (
        P("blk", ("tp", "enc")),
        P("blk", None, "tp"),
        P("blk", ("tp", "enc")),
        P("blk", None, "enc", "tp"),
        P("blk", None),
        P(),
    )
    return jax.shard_map(
        per_device,
        mesh=mesh,
        in_specs=placed,
        out_specs=(P("blk", ("tp", "enc")), P("blk", ("tp", "enc"))),
        check_vma=False,
    )
```

```python
import functools
import math

import jax
import jax.numpy as jnp
from jax import lax
from jax.experimental import pallas as pl
from jax.experimental.pallas import tpu as pltpu
from jax.sharding import PartitionSpec as P

HEAD_SIZE = 128
MASK_BLOCK_TOKENS = 128
LANES = 128
LOWEST = -1e30
MIXED_ROWS = HEAD_SIZE + 16
SHIFT_KEYS = 256
CHUNK = 256
MOST_SUM = 2.0**100
LOG2_SCALE = math.log2(math.e) / math.sqrt(HEAD_SIZE)
VMEM_LIMIT = 48 * 1024 * 1024

VMEM = pl.BlockSpec(memory_space=pltpu.VMEM)
SMEM = pl.BlockSpec(memory_space=pltpu.SMEM)


def padded(count):
    return -(-count // LANES) * LANES


def nt_dot(a, b):
    return lax.dot_general(a, b, (((1,), (1,)), ((), ())), preferred_element_type=jnp.float32)


def at_block(block, size):
    return pl.ds(pl.multiple_of(block * size, size), size)


def stacked_heads(rows):
    heads = rows.shape[1] // HEAD_SIZE
    return jnp.concatenate([rows[:, h * HEAD_SIZE : (h + 1) * HEAD_SIZE] for h in range(heads)], axis=0)


def with_ones(value_t):
    shape = (MIXED_ROWS - HEAD_SIZE, value_t.shape[1])
    ones = (lax.broadcasted_iota(jnp.int32, shape, 0) == 0).astype(jnp.bfloat16)
    return jnp.concatenate([value_t, ones], axis=0)


def fold(high, mixed, scores, value_t, exact):
    seen = scores if exact else scores[0 : min(SHIFT_KEYS, scores.shape[0]), :]
    new_high = jnp.maximum(high, jnp.max(seen, axis=0, keepdims=True))
    weights = jnp.exp2(scores * LOG2_SCALE - new_high * LOG2_SCALE).astype(jnp.bfloat16)
    fading = jnp.exp2((high - new_high) * LOG2_SCALE)
    mixed = mixed * fading + jnp.dot(with_ones(value_t), weights, preferred_element_type=jnp.float32)
    return new_high, mixed


def fold_chunks(high, mixed, chunks, scores_of, values_of, exact):
    scores = scores_of(chunks[0])
    seen = jnp.max(scores, axis=0, keepdims=True)
    if exact:
        for chunk in chunks[1:]:
            seen = jnp.maximum(seen, jnp.max(scores_of(chunk), axis=0, keepdims=True))
    new_high = jnp.maximum(high, seen)
    shift = new_high * LOG2_SCALE
    mixed = mixed * jnp.exp2((high - new_high) * LOG2_SCALE)
    waiting = None
    for index, chunk in enumerate(chunks):
        following = scores_of(chunks[index + 1]) if index + 1 < len(chunks) else None
        weights = jnp.exp2(scores * LOG2_SCALE - shift).astype(jnp.bfloat16)
        if waiting is not None:
            mixed = mixed + jnp.dot(*waiting, preferred_element_type=jnp.float32)
        waiting = (with_ones(values_of(chunk)), weights)
        scores = following
    mixed = mixed + jnp.dot(*waiting, preferred_element_type=jnp.float32)
    return new_high, mixed


def prepare_kernel(kv_ref, out_ref):
    count = kv_ref.shape[1]
    whole = count // LANES * LANES
    rest = count - whole
    out_ref[0, 0:whole, :] = kv_ref[0, 0:whole, :]
    for at in range(0, whole, LANES):
        out_ref[1, at : at + LANES, :] = kv_ref[1, at : at + LANES, :].T
    if rest:
        empty = jnp.zeros((LANES - rest, HEAD_SIZE), jnp.float32)
        tail_key = jnp.concatenate([kv_ref[0, whole:count, :].astype(jnp.float32), empty], axis=0)
        tail_value = jnp.concatenate([kv_ref[1, whole:count, :].astype(jnp.float32), empty], axis=0)
        out_ref[0, whole : whole + LANES, :] = tail_key.astype(jnp.bfloat16)
        out_ref[1, whole : whole + LANES, :] = tail_value.T.astype(jnp.bfloat16)


def prepare(kv):
    return pl.pallas_call(
        prepare_kernel,
        out_shape=jax.ShapeDtypeStruct((2, padded(kv.shape[1]), HEAD_SIZE), jnp.bfloat16),
        in_specs=[VMEM],
        out_specs=VMEM,
        compiler_params=pltpu.CompilerParams(vmem_limit_bytes=VMEM_LIMIT),
        cost_estimate=pl.CostEstimate(flops=0, bytes_accessed=2 * kv.size * 2, transcendentals=0),
        name="prepare",
    )(kv)


def lse_rows(block_count):
    return -(-3 * block_count // 16) * 16


def cross_kernel(key_count, pieces, offset, last, position_ref, images_ref, owner_ref, q_ref, *refs):
    images, refs = refs[:pieces], refs[pieces:]
    if offset:
        before, refs = refs[:2], refs[2:]
    if last:
        out_ref, lse_ref, high_ref, mixed_ref, most_ref = refs
        lse_ref[...] = jnp.zeros_like(lse_ref)
    else:
        high_ref, mixed_ref, most_ref = refs
    slots = images_ref.shape[1]
    block_count = q_ref.shape[0] // MASK_BLOCK_TOKENS
    heads = q_ref.shape[1] // HEAD_SIZE
    rows = heads * MASK_BLOCK_TOKENS

    def attempt(exact):
        most_ref[...] = jnp.zeros_like(most_ref)

        def per_block(block, carry):
            here = 0 if last else block
            if offset:
                high_ref[here] = before[0][block]
                mixed_ref[here] = before[1][block]
            else:
                high_ref[here] = jnp.full(high_ref.shape[1:], LOWEST, jnp.float32)
                mixed_ref[here] = jnp.zeros(mixed_ref.shape[1:], jnp.float32)
            for piece in range(pieces):
                slot = lax.rem(position_ref[0] + (slots - offset - piece), slots)
                seen = jnp.int32(0)
                for image in range(slots):
                    seen = seen + jnp.where(owner_ref[image] == slot, images_ref[block, image], 0)

                @pl.when(seen > 0)
                def _(piece=piece):
                    image = images[piece]
                    width = image.shape[1]
                    queries = stacked_heads(q_ref[at_block(block, MASK_BLOCK_TOKENS), :])
                    chunks = [(c, min(c + CHUNK, width)) for c in range(0, width, CHUNK)]

                    def scores_of(chunk):
                        start, stop = chunk
                        scores = nt_dot(image[0, start:stop, :], queries)
                        if stop > key_count:
                            key_id = start + lax.broadcasted_iota(jnp.int32, scores.shape, 0)
                            scores = jnp.where(key_id < key_count, scores, LOWEST)
                        return scores

                    def values_of(chunk):
                        return jnp.concatenate([image[1, c : c + LANES, :] for c in range(*chunk, LANES)], axis=1)

                    high, mixed = fold_chunks(
                        high_ref[here][0:1], mixed_ref[here], chunks, scores_of, values_of, exact
                    )
                    high_ref[here] = jnp.broadcast_to(high, high_ref.shape[1:])
                    mixed_ref[here] = mixed

            total = mixed_ref[here][HEAD_SIZE : HEAD_SIZE + 1, :]
            most_ref[0:1, :] = jnp.maximum(most_ref[0:1, :], total)
            if last:
                out_ref[at_block(block, HEAD_SIZE), :] = (mixed_ref[here][0:HEAD_SIZE, :] / total).astype(jnp.bfloat16)
                lse = high_ref[here][0:1] * LOG2_SCALE + jnp.log2(total)
                row = lax.broadcasted_iota(jnp.int32, lse_ref.shape, 0)
                lse_ref[...] = jnp.where(row == block, lse, lse_ref[...])
            return carry

        lax.fori_loop(0, block_count, per_block, 0)

    attempt(False)
    fine = jnp.min((most_ref[0:1, :] <= MOST_SUM).astype(jnp.int32))

    @pl.when(fine == 0)
    def _():
        attempt(True)

    if last:
        lse = lse_ref[...]
        first = lse.astype(jnp.bfloat16).astype(jnp.float32)
        second = (lse - first).astype(jnp.bfloat16).astype(jnp.float32)
        third = lse - first - second
        parts = [part[0:block_count, :] for part in (first, second, third)]
        spare = lse_rows(block_count) - 3 * block_count
        if spare:
            parts.append(jnp.zeros((spare, rows), jnp.float32))
        out_ref[block_count * HEAD_SIZE :, :] = jnp.concatenate(parts, axis=0).astype(jnp.bfloat16)


def cross_part(tables, queries, images, key_count, offset, last, before=()):
    tokens, columns = queries.shape
    block_count = tokens // MASK_BLOCK_TOKENS
    rows = columns // HEAD_SIZE * MASK_BLOCK_TOKENS
    state = [(8, rows), (MIXED_ROWS, rows)]
    scratch = [pltpu.VMEM((8, rows), jnp.float32)]
    if last:
        out_shape = jax.ShapeDtypeStruct((block_count * HEAD_SIZE + lse_rows(block_count), rows), jnp.bfloat16)
        scratch = [pltpu.VMEM((1,) + shape, jnp.float32) for shape in state] + scratch
        scratch = [pltpu.VMEM((-(-block_count // 8) * 8, rows), jnp.float32)] + scratch
    else:
        out_shape = tuple(jax.ShapeDtypeStruct((block_count,) + shape, jnp.float32) for shape in state)
    flops = 4 * block_count * rows * key_count * HEAD_SIZE * len(images)
    return pl.pallas_call(
        functools.partial(cross_kernel, key_count, len(images), offset, last),
        out_shape=out_shape,
        in_specs=[SMEM, SMEM, SMEM] + [VMEM] * (1 + len(images) + len(before)),
        out_specs=VMEM if last else (VMEM,) * 2,
        scratch_shapes=scratch,
        compiler_params=pltpu.CompilerParams(vmem_limit_bytes=VMEM_LIMIT),
        cost_estimate=pl.CostEstimate(flops=2 * flops, bytes_accessed=4 * 1024 * 1024, transcendentals=0),
        name="cross_last" if last else "cross_first",
    )(*tables, queries, *images, *before)


def combine_kernel(parts, *refs):
    part_refs, out_ref = refs[:parts], refs[parts]
    tokens, columns = out_ref.shape
    block_count = tokens // MASK_BLOCK_TOKENS
    first_lse = block_count * HEAD_SIZE
    lse = []
    for ref in part_refs:
        tail = ref[first_lse:, :].astype(jnp.float32)
        lse.append(
            tail[0:block_count] + tail[block_count : 2 * block_count] + tail[2 * block_count : 3 * block_count]
        )
    highest = functools.reduce(jnp.maximum, lse)
    weights = [jnp.exp2(one - highest) for one in lse]
    total = functools.reduce(jnp.add, weights)
    weights = [one / total for one in weights]
    for block in range(block_count):
        mixed = 0.0
        for ref, weight in zip(part_refs, weights):
            part = ref[block * HEAD_SIZE : (block + 1) * HEAD_SIZE, :].astype(jnp.float32)
            mixed = mixed + weight[block : block + 1, :] * part
        store_heads(out_ref, block, mixed)


def store_heads(out_ref, block, mixed):
    at = slice(block * MASK_BLOCK_TOKENS, (block + 1) * MASK_BLOCK_TOKENS)
    for head in range(out_ref.shape[1] // HEAD_SIZE):
        piece = mixed[:, head * MASK_BLOCK_TOKENS : (head + 1) * MASK_BLOCK_TOKENS]
        out_ref[at, head * HEAD_SIZE : (head + 1) * HEAD_SIZE] = piece.T.astype(jnp.bfloat16)


def combined(parts, shape):
    return pl.pallas_call(
        functools.partial(combine_kernel, len(parts)),
        out_shape=jax.ShapeDtypeStruct(shape, jnp.bfloat16),
        in_specs=[VMEM] * len(parts),
        out_specs=VMEM,
        compiler_params=pltpu.CompilerParams(vmem_limit_bytes=VMEM_LIMIT),
        cost_estimate=pl.CostEstimate(flops=0, bytes_accessed=2 * 1024 * 1024, transcendentals=0),
        name="combine",
    )(*parts)


def self_kernel(pieces, position_ref, q_ref, *refs):
    texts = refs[:pieces]
    out_ref, value_ref, high_ref, mixed_ref = refs[pieces:]
    tokens, columns = q_ref.shape
    rows = columns // HEAD_SIZE * MASK_BLOCK_TOKENS
    value_ref[0] = texts[0][:, HEAD_SIZE:].T
    for piece in range(1, pieces):

        @pl.when(position_ref[0] >= piece)
        def _(piece=piece):
            value_ref[piece] = texts[piece][:, HEAD_SIZE:].T

    for block in range(tokens // MASK_BLOCK_TOKENS):
        start = block * MASK_BLOCK_TOKENS
        stop = start + MASK_BLOCK_TOKENS
        queries = stacked_heads(q_ref[start:stop, :])
        scores = nt_dot(texts[0][0:stop, 0:HEAD_SIZE], queries)
        tail = scores[start:, :]
        key_id = lax.broadcasted_iota(jnp.int32, tail.shape, 0)
        query_id = lax.broadcasted_iota(jnp.int32, tail.shape, 1) % MASK_BLOCK_TOKENS
        tail = jnp.where(key_id <= query_id, tail, LOWEST)
        scores = jnp.concatenate([scores[:start, :], tail], axis=0) if start else tail
        high = jnp.full((1, rows), LOWEST, jnp.float32)
        mixed = jnp.zeros((MIXED_ROWS, rows), jnp.float32)
        high, mixed = fold(high, mixed, scores, value_ref[0, :, 0:stop], True)
        high_ref[0:1, :] = high
        mixed_ref[...] = mixed
        for piece in range(1, pieces):

            @pl.when(position_ref[0] >= piece)
            def _(piece=piece):
                scores = nt_dot(texts[piece][:, 0:HEAD_SIZE], queries)
                high, mixed = fold(high_ref[0:1, :], mixed_ref[...], scores, value_ref[piece], True)
                high_ref[0:1, :] = high
                mixed_ref[...] = mixed

        store_heads(out_ref, block, mixed_ref[0:HEAD_SIZE, :] / mixed_ref[HEAD_SIZE : HEAD_SIZE + 1, :])


def self_attention(position, queries, texts):
    tokens, columns = queries.shape
    pieces = len(texts)
    rows = columns // HEAD_SIZE * MASK_BLOCK_TOKENS
    return pl.pallas_call(
        functools.partial(self_kernel, pieces),
        out_shape=jax.ShapeDtypeStruct((tokens, columns), jnp.bfloat16),
        in_specs=[SMEM] + [VMEM] * (1 + pieces),
        out_specs=VMEM,
        scratch_shapes=[
            pltpu.VMEM((pieces, HEAD_SIZE, tokens), jnp.bfloat16),
            pltpu.VMEM((8, rows), jnp.float32),
            pltpu.VMEM((MIXED_ROWS, rows), jnp.float32),
        ],
        compiler_params=pltpu.CompilerParams(vmem_limit_bytes=VMEM_LIMIT),
        cost_estimate=pl.CostEstimate(flops=8 * tokens * columns * tokens, bytes_accessed=1024 * 1024, transcendentals=0),
        name="self_attention",
    )(position, queries, *texts)


def shifted(value, axis, steps):
    count = lax.axis_size(axis)
    return lax.ppermute(value, axis, [(source, (source + steps) % count) for source in range(count)])


def per_device(self_queries, text_kv, cross_queries, image_kv, block_images, image_owner):
    rows = self_queries.shape[0]
    key_count = image_kv.shape[2]
    cycle = lax.axis_size("blk")
    ring = lax.axis_size("enc")
    position = lax.axis_index("blk").astype(jnp.int32)[None]

    tables = (position, block_images, image_owner)

    images = [prepare(image_kv[0])]
    for _ in range(1, cycle):
        images.append(shifted(images[-1], "blk", 1))
    order = sorted(range(1, ring), key=lambda step: (abs(2 * step - ring), step))
    queries = {step: shifted(cross_queries, "enc", ring - step) for step in order}
    queries[0] = cross_queries

    text = text_kv.reshape(rows, 2 * HEAD_SIZE)
    texts = [text]
    for step in range(1, cycle):
        texts.append(lax.ppermute(texts[-1], "blk", [(source, source + 1) for source in range(cycle - 1)]))

    alone = cycle == 1
    states = {0: ()}
    if not alone:
        states[0] = cross_part(tables, queries[0], images[:1], key_count, 0, False)
    earlier = states[0]
    for step in order:
        if alone:
            states[step] = ()
        else:
            queries[step], _ = lax.optimization_barrier((queries[step], earlier))
            earlier = states[step] = cross_part(tables, queries[step], images[:1], key_count, 0, False)

    def finished(step):
        offset = 0 if alone else 1
        return cross_part(tables, queries[step], images[offset:], key_count, offset, True, states[step])

    received = [shifted(finished(step), "enc", step) for step in order]

    own = finished(0)
    self_out = self_attention(position, self_queries, texts)
    cross_out = combined([own] + received, cross_queries.shape)
    return (self_out, cross_out)


def solution(mesh):
    placed = (
        P("blk", ("tp", "enc")),
        P("blk", None, "tp"),
        P("blk", ("tp", "enc")),
        P("blk", None, "enc", "tp"),
        P("blk", None),
        P(),
    )
    return jax.shard_map(
        per_device,
        mesh=mesh,
        in_specs=placed,
        out_specs=(P("blk", ("tp", "enc")), P("blk", ("tp", "enc"))),
        check_vma=False,
    )
```

```python
import functools
import math

import jax
import jax.numpy as jnp
from jax import lax
from jax.experimental import pallas as pl
from jax.experimental.pallas import tpu as pltpu
from jax.sharding import PartitionSpec as P

HEAD_SIZE = 128
MASK_BLOCK_TOKENS = 128
LANES = 128
LOWEST = -1e30
SHIFT_KEYS = 256
CHUNK = 512
MOST_SUM = 2.0**100
LOG2_SCALE = math.log2(math.e) / math.sqrt(HEAD_SIZE)
VMEM_LIMIT = 48 * 1024 * 1024

VMEM = pl.BlockSpec(memory_space=pltpu.VMEM)
SMEM = pl.BlockSpec(memory_space=pltpu.SMEM)


def padded(count):
    return -(-count // LANES) * LANES


def nt_dot(a, b):
    return lax.dot_general(a, b, (((1,), (1,)), ((), ())), preferred_element_type=jnp.float32)


def at_block(block, size=MASK_BLOCK_TOKENS):
    return pl.ds(pl.multiple_of(block * size, size), size)


def stacked_heads(rows):
    heads = rows.shape[1] // HEAD_SIZE
    return jnp.concatenate([rows[:, h * HEAD_SIZE : (h + 1) * HEAD_SIZE] for h in range(heads)], axis=0)


def lane_tiles(wide):
    return [wide[:, at : at + LANES] for at in range(0, wide.shape[1], LANES)]


def row_max(scores):
    return jnp.max(functools.reduce(jnp.maximum, lane_tiles(scores)), axis=1, keepdims=True)


def empty_state(rows):
    return (
        jnp.full((rows, LANES), LOWEST, jnp.float32),
        jnp.zeros((rows, LANES), jnp.float32),
        jnp.zeros((rows, HEAD_SIZE), jnp.float32),
    )


def fold_chunks(state, chunks, scores_of, values_of, exact):
    high, total, mixed = state
    scores = scores_of(chunks[0])
    seen = row_max(scores[:, 0 : min(SHIFT_KEYS, scores.shape[1])])
    if exact:
        seen = functools.reduce(jnp.maximum, [row_max(scores_of(chunk)) for chunk in chunks])
    new_high = jnp.maximum(high, seen)
    shift = new_high * LOG2_SCALE
    fading = jnp.exp2((high - new_high) * LOG2_SCALE)
    total = total * fading
    mixed = mixed * fading
    waiting = None
    for index, chunk in enumerate(chunks):
        following = scores_of(chunks[index + 1]) if index + 1 < len(chunks) else None
        weights = [jnp.exp2(tile * LOG2_SCALE - shift) for tile in lane_tiles(scores)]
        total = total + functools.reduce(jnp.add, weights)
        if waiting is not None:
            mixed = mixed + jnp.dot(*waiting, preferred_element_type=jnp.float32)
        weights = [tile.astype(jnp.bfloat16) for tile in weights]
        waiting = (jnp.concatenate(weights, axis=1) if len(weights) > 1 else weights[0], values_of(chunk))
        scores = following
    mixed = mixed + jnp.dot(*waiting, preferred_element_type=jnp.float32)
    return new_high, total, mixed


def prepare_kernel(kv_ref, out_ref):
    count = kv_ref.shape[1]
    whole = count // LANES * LANES
    rest = count - whole
    for at in range(0, whole, LANES):
        out_ref[0, at : at + LANES, :] = kv_ref[0, at : at + LANES, :].T
    out_ref[1, 0:whole, :] = kv_ref[1, 0:whole, :]
    if rest:
        empty = jnp.zeros((LANES - rest, HEAD_SIZE), jnp.float32)
        tail_key = jnp.concatenate([kv_ref[0, whole:count, :].astype(jnp.float32), empty], axis=0)
        tail_value = jnp.concatenate([kv_ref[1, whole:count, :].astype(jnp.float32), empty], axis=0)
        out_ref[0, whole : whole + LANES, :] = tail_key.T.astype(jnp.bfloat16)
        out_ref[1, whole : whole + LANES, :] = tail_value.astype(jnp.bfloat16)


def prepare(kv):
    return pl.pallas_call(
        prepare_kernel,
        out_shape=jax.ShapeDtypeStruct((2, padded(kv.shape[1]), HEAD_SIZE), jnp.bfloat16),
        in_specs=[VMEM],
        out_specs=VMEM,
        compiler_params=pltpu.CompilerParams(vmem_limit_bytes=VMEM_LIMIT),
        cost_estimate=pl.CostEstimate(flops=0, bytes_accessed=2 * kv.size * 2, transcendentals=0),
        name="prepare",
    )(kv)


def lse_rows(block_count):
    return -(-3 * block_count // 16) * 16


def chunks_of(width):
    starts = list(range(0, max(width - CHUNK // 2, 1), CHUNK))
    return list(zip(starts, starts[1:] + [width]))


def cross_kernel(key_count, pieces, offset, last, position_ref, images_ref, owner_ref, q_ref, *refs):
    images, refs = refs[:pieces], refs[pieces:]
    if offset:
        before, refs = refs[:3], refs[3:]
    if last:
        out_ref, lse_ref, list_ref, *state_refs = refs
    else:
        *state_refs, list_ref = refs
    slots = images_ref.shape[1]
    block_count = q_ref.shape[0] // MASK_BLOCK_TOKENS
    heads = q_ref.shape[1] // HEAD_SIZE
    rows = heads * MASK_BLOCK_TOKENS

    def attempt(exact):
        for block in range(block_count):
            at = slice(block * rows, (block + 1) * rows)
            for index, value in enumerate(empty_state(rows)):
                state_refs[index][at, :] = before[index][at, :] if offset else value
        for piece in range(pieces):
            slot = lax.rem(position_ref[0] + (slots - offset - piece), slots)

            def collect(block, count):
                seen = jnp.int32(0)
                for image in range(slots):
                    seen = seen + jnp.where(owner_ref[image] == slot, images_ref[block, image], 0)
                list_ref[count] = block
                return count + jnp.where(seen > 0, 1, 0)

            count = jnp.int32(0)
            for block in range(block_count):
                count = collect(block, count)

            def per_pair(pair, carry, piece=piece, count=count):
                image = images[piece]
                blocks = [list_ref[2 * pair], list_ref[jnp.minimum(2 * pair + 1, count - 1)]]
                queries = jnp.concatenate([stacked_heads(q_ref[at_block(block), :]) for block in blocks], axis=0)
                state = [
                    jnp.concatenate([ref[at_block(block, rows), :] for block in blocks], axis=0) for ref in state_refs
                ]

                def scores_of(chunk):
                    start, stop = chunk
                    keys = jnp.concatenate([image[0, c : c + LANES, :] for c in range(start, stop, LANES)], axis=1)
                    scores = jnp.dot(queries, keys, preferred_element_type=jnp.float32)
                    if stop > key_count:
                        key_id = start + lax.broadcasted_iota(jnp.int32, scores.shape, 1)
                        scores = jnp.where(key_id < key_count, scores, LOWEST)
                    return scores

                def values_of(chunk):
                    return image[1, chunk[0] : chunk[1], :]

                state = fold_chunks(state, chunks_of(image.shape[1]), scores_of, values_of, exact)
                for ref, value in zip(state_refs, state):
                    for index, block in enumerate(blocks):
                        ref[at_block(block, rows), :] = value[index * rows : (index + 1) * rows]
                return carry

            lax.fori_loop(0, (count + 1) // 2, per_pair, 0)

    attempt(False)
    fine = jnp.min((jnp.max(state_refs[1][...], axis=0, keepdims=True) <= MOST_SUM).astype(jnp.int32))

    @pl.when(fine == 0)
    def _():
        attempt(True)

    if last:
        lse_ref[...] = jnp.zeros_like(lse_ref)
        for block in range(block_count):
            at = slice(block * rows, (block + 1) * rows)
            total = jnp.sum(state_refs[1][at, :], axis=1, keepdims=True)
            mixed = state_refs[2][at, :] / total
            lse = state_refs[0][at, :] * LOG2_SCALE + jnp.log2(total)
            for head in range(heads):
                own = slice(head * MASK_BLOCK_TOKENS, (head + 1) * MASK_BLOCK_TOKENS)
                here = slice(block * MASK_BLOCK_TOKENS, (block + 1) * MASK_BLOCK_TOKENS)
                out_ref[here, head * HEAD_SIZE : (head + 1) * HEAD_SIZE] = mixed[own].astype(jnp.bfloat16)
                lse_ref[block : block + 1, own] = lse[own].T[0:1, :]
        lse = lse_ref[...]
        first = lse.astype(jnp.bfloat16).astype(jnp.float32)
        second = (lse - first).astype(jnp.bfloat16).astype(jnp.float32)
        third = lse - first - second
        parts = [part[0:block_count, :] for part in (first, second, third)]
        spare = lse_rows(block_count) - 3 * block_count
        if spare:
            parts.append(jnp.zeros((spare, rows), jnp.float32))
        out_ref[q_ref.shape[0] :, :] = jnp.concatenate(parts, axis=0).astype(jnp.bfloat16)


def cross_part(tables, queries, images, key_count, offset, last, before=()):
    tokens, columns = queries.shape
    block_count = tokens // MASK_BLOCK_TOKENS
    rows = columns // HEAD_SIZE * MASK_BLOCK_TOKENS
    state = (block_count * rows, LANES)
    scratch = [pltpu.SMEM((block_count + 1,), jnp.int32)]
    if last:
        out_shape = jax.ShapeDtypeStruct((tokens + lse_rows(block_count), columns), jnp.bfloat16)
        scratch = [pltpu.VMEM((-(-block_count // 8) * 8, rows), jnp.float32)] + scratch
        scratch += [pltpu.VMEM(state, jnp.float32)] * 3
    else:
        out_shape = (jax.ShapeDtypeStruct(state, jnp.float32),) * 3
    flops = 4 * block_count * rows * key_count * HEAD_SIZE * len(images)
    return pl.pallas_call(
        functools.partial(cross_kernel, key_count, len(images), offset, last),
        out_shape=out_shape,
        in_specs=[SMEM, SMEM, SMEM] + [VMEM] * (1 + len(images) + len(before)),
        out_specs=VMEM if last else (VMEM,) * 3,
        scratch_shapes=scratch,
        compiler_params=pltpu.CompilerParams(vmem_limit_bytes=VMEM_LIMIT),
        cost_estimate=pl.CostEstimate(flops=2 * flops, bytes_accessed=4 * 1024 * 1024, transcendentals=0),
        name="cross_last" if last else "cross_first",
    )(*tables, queries, *images, *before)


def combine_kernel(parts, *refs):
    part_refs, out_ref = refs[:parts], refs[parts]
    tokens, columns = out_ref.shape
    block_count = tokens // MASK_BLOCK_TOKENS
    heads = columns // HEAD_SIZE
    lse = []
    for ref in part_refs:
        tail = ref[tokens:, :].astype(jnp.float32)
        lse.append(
            tail[0:block_count] + tail[block_count : 2 * block_count] + tail[2 * block_count : 3 * block_count]
        )
    highest = functools.reduce(jnp.maximum, lse)
    weights = [jnp.exp2(one - highest) for one in lse]
    total = functools.reduce(jnp.add, weights)
    by_row = [
        (one / total)[:, head * MASK_BLOCK_TOKENS : (head + 1) * MASK_BLOCK_TOKENS]
        for one in weights
        for head in range(heads)
    ]
    used = len(by_row) * block_count
    by_row.append(jnp.zeros((padded(used) - used, MASK_BLOCK_TOKENS), jnp.float32))
    columns_of = jnp.concatenate(by_row, axis=0).T
    for block in range(block_count):
        at = slice(block * MASK_BLOCK_TOKENS, (block + 1) * MASK_BLOCK_TOKENS)
        for head in range(heads):
            dims = slice(head * HEAD_SIZE, (head + 1) * HEAD_SIZE)
            mixed = 0.0
            for index, ref in enumerate(part_refs):
                column = (index * heads + head) * block_count + block
                mixed = mixed + columns_of[:, column : column + 1] * ref[at, dims].astype(jnp.float32)
            out_ref[at, dims] = mixed.astype(jnp.bfloat16)


def combined(parts, shape):
    return pl.pallas_call(
        functools.partial(combine_kernel, len(parts)),
        out_shape=jax.ShapeDtypeStruct(shape, jnp.bfloat16),
        in_specs=[VMEM] * len(parts),
        out_specs=VMEM,
        compiler_params=pltpu.CompilerParams(vmem_limit_bytes=VMEM_LIMIT),
        cost_estimate=pl.CostEstimate(flops=0, bytes_accessed=2 * 1024 * 1024, transcendentals=0),
        name="combine",
    )(*parts)


def self_kernel(pieces, position_ref, q_ref, *refs):
    texts = refs[:pieces]
    out_ref, *state_refs = refs[pieces:]
    tokens, columns = q_ref.shape
    heads = columns // HEAD_SIZE
    rows = heads * MASK_BLOCK_TOKENS
    for block in range(tokens // MASK_BLOCK_TOKENS):
        start = block * MASK_BLOCK_TOKENS
        stop = start + MASK_BLOCK_TOKENS
        queries = stacked_heads(q_ref[start:stop, :])

        def own_scores(chunk):
            scores = nt_dot(queries, texts[0][0:stop, 0:HEAD_SIZE])
            key_id = lax.broadcasted_iota(jnp.int32, scores.shape, 1)
            query_id = start + lax.broadcasted_iota(jnp.int32, scores.shape, 0) % MASK_BLOCK_TOKENS
            return jnp.where(key_id <= query_id, scores, LOWEST)

        state = fold_chunks(
            empty_state(rows), [(0, stop)], own_scores, lambda chunk: texts[0][0:stop, HEAD_SIZE:], True
        )
        for ref, value in zip(state_refs, state):
            ref[...] = value
        for piece in range(1, pieces):

            @pl.when(position_ref[0] >= piece)
            def _(piece=piece):
                state = fold_chunks(
                    [ref[...] for ref in state_refs],
                    [(0, tokens)],
                    lambda chunk: nt_dot(queries, texts[piece][:, 0:HEAD_SIZE]),
                    lambda chunk: texts[piece][:, HEAD_SIZE:],
                    True,
                )
                for ref, value in zip(state_refs, state):
                    ref[...] = value

        mixed = state_refs[2][...] / jnp.sum(state_refs[1][...], axis=1, keepdims=True)
        for head in range(heads):
            out_ref[start:stop, head * HEAD_SIZE : (head + 1) * HEAD_SIZE] = mixed[
                head * MASK_BLOCK_TOKENS : (head + 1) * MASK_BLOCK_TOKENS
            ].astype(jnp.bfloat16)


def self_attention(position, queries, texts):
    tokens, columns = queries.shape
    pieces = len(texts)
    rows = columns // HEAD_SIZE * MASK_BLOCK_TOKENS
    return pl.pallas_call(
        functools.partial(self_kernel, pieces),
        out_shape=jax.ShapeDtypeStruct((tokens, columns), jnp.bfloat16),
        in_specs=[SMEM] + [VMEM] * (1 + pieces),
        out_specs=VMEM,
        scratch_shapes=[pltpu.VMEM((rows, LANES), jnp.float32)] * 3,
        compiler_params=pltpu.CompilerParams(vmem_limit_bytes=VMEM_LIMIT),
        cost_estimate=pl.CostEstimate(flops=8 * tokens * columns * tokens, bytes_accessed=1024 * 1024, transcendentals=0),
        name="self_attention",
    )(position, queries, *texts)


def shifted(value, axis, steps):
    count = lax.axis_size(axis)
    return lax.ppermute(value, axis, [(source, (source + steps) % count) for source in range(count)])


def per_device(self_queries, text_kv, cross_queries, image_kv, block_images, image_owner):
    rows = self_queries.shape[0]
    key_count = image_kv.shape[2]
    cycle = lax.axis_size("blk")
    ring = lax.axis_size("enc")
    position = lax.axis_index("blk").astype(jnp.int32)[None]

    tables = (position, block_images, image_owner)

    images = [prepare(image_kv[0])]
    for _ in range(1, cycle):
        images.append(shifted(images[-1], "blk", 1))
    order = sorted(range(1, ring), key=lambda step: (abs(2 * step - ring), step))
    queries = {step: shifted(cross_queries, "enc", ring - step) for step in order}
    queries[0] = cross_queries

    text = text_kv.reshape(rows, 2 * HEAD_SIZE)
    texts = [text]
    for step in range(1, cycle):
        texts.append(lax.ppermute(texts[-1], "blk", [(source, source + 1) for source in range(cycle - 1)]))

    alone = cycle == 1
    states = {0: ()}
    if not alone:
        states[0] = cross_part(tables, queries[0], images[:1], key_count, 0, False)
    earlier = states[0]
    for step in order:
        if alone:
            states[step] = ()
        else:
            queries[step], _ = lax.optimization_barrier((queries[step], earlier))
            earlier = states[step] = cross_part(tables, queries[step], images[:1], key_count, 0, False)

    def finished(step):
        offset = 0 if alone else 1
        return cross_part(tables, queries[step], images[offset:], key_count, offset, True, states[step])

    received = [shifted(finished(step), "enc", step) for step in order]

    own = finished(0)
    self_out = self_attention(position, self_queries, texts)
    cross_out = combined([own] + received, cross_queries.shape)
    return (self_out, cross_out)


def solution(mesh):
    placed = (
        P("blk", ("tp", "enc")),
        P("blk", None, "tp"),
        P("blk", ("tp", "enc")),
        P("blk", None, "enc", "tp"),
        P("blk", None),
        P(),
    )
    return jax.shard_map(
        per_device,
        mesh=mesh,
        in_specs=placed,
        out_specs=(P("blk", ("tp", "enc")), P("blk", ("tp", "enc"))),
        check_vma=False,
    )
```

```python
import functools
import math

import jax
import jax.numpy as jnp
from jax import lax
from jax.experimental import pallas as pl
from jax.experimental.pallas import tpu as pltpu
from jax.sharding import PartitionSpec as P

HEAD_SIZE = 128
MASK_BLOCK_TOKENS = 128
LANES = 128
LOWEST = -1e30
MIXED_ROWS = HEAD_SIZE + 16
SHIFT_KEYS = 256
MOST_SUM = 2.0**100
LOG2_SCALE = math.log2(math.e) / math.sqrt(HEAD_SIZE)
VMEM_LIMIT = 48 * 1024 * 1024

VMEM = pl.BlockSpec(memory_space=pltpu.VMEM)
SMEM = pl.BlockSpec(memory_space=pltpu.SMEM)


def padded(count):
    return -(-count // LANES) * LANES


def nt_dot(a, b):
    return lax.dot_general(a, b, (((1,), (1,)), ((), ())), preferred_element_type=jnp.float32)


def at_block(block, size=MASK_BLOCK_TOKENS):
    return pl.ds(pl.multiple_of(block * size, size), size)


def stacked_heads(rows):
    heads = rows.shape[1] // HEAD_SIZE
    return jnp.concatenate([rows[:, h * HEAD_SIZE : (h + 1) * HEAD_SIZE] for h in range(heads)], axis=0)


def with_ones(value_t):
    shape = (MIXED_ROWS - HEAD_SIZE, value_t.shape[1])
    ones = (lax.broadcasted_iota(jnp.int32, shape, 0) == 0).astype(jnp.bfloat16)
    return jnp.concatenate([value_t, ones], axis=0)


def fold(high, mixed, scores, value_t, exact):
    seen = scores if exact else scores[0 : min(SHIFT_KEYS, scores.shape[0]), :]
    new_high = jnp.maximum(high, jnp.max(seen, axis=0, keepdims=True))
    weights = jnp.exp2(scores * LOG2_SCALE - new_high * LOG2_SCALE).astype(jnp.bfloat16)
    fading = jnp.exp2((high - new_high) * LOG2_SCALE)
    mixed = mixed * fading + jnp.dot(with_ones(value_t), weights, preferred_element_type=jnp.float32)
    return new_high, mixed


def prepare_kernel(kv_ref, out_ref):
    count = kv_ref.shape[1]
    whole = count // LANES * LANES
    rest = count - whole
    out_ref[0, 0:whole, :] = kv_ref[0, 0:whole, :]
    for at in range(0, whole, LANES):
        out_ref[1, at : at + LANES, :] = kv_ref[1, at : at + LANES, :].T
    if rest:
        empty = jnp.zeros((LANES - rest, HEAD_SIZE), jnp.float32)
        tail_key = jnp.concatenate([kv_ref[0, whole:count, :].astype(jnp.float32), empty], axis=0)
        tail_value = jnp.concatenate([kv_ref[1, whole:count, :].astype(jnp.float32), empty], axis=0)
        out_ref[0, whole : whole + LANES, :] = tail_key.astype(jnp.bfloat16)
        out_ref[1, whole : whole + LANES, :] = tail_value.T.astype(jnp.bfloat16)


def prepare(kv):
    return pl.pallas_call(
        prepare_kernel,
        out_shape=jax.ShapeDtypeStruct((2, padded(kv.shape[1]), HEAD_SIZE), jnp.bfloat16),
        in_specs=[VMEM],
        out_specs=VMEM,
        compiler_params=pltpu.CompilerParams(vmem_limit_bytes=VMEM_LIMIT),
        cost_estimate=pl.CostEstimate(flops=0, bytes_accessed=2 * kv.size * 2, transcendentals=0),
        name="prepare",
    )(kv)


def lse_rows(block_count):
    return -(-3 * block_count // 16) * 16


def table_kernel(position_ref, images_ref, owner_ref, table_ref):
    block_count, slots = images_ref.shape
    for piece in range(slots):
        slot = lax.rem(position_ref[0] + (slots - piece), slots)
        base = piece * (block_count + 1)
        count = jnp.int32(0)
        for block in range(block_count):
            table_ref[base + 1 + block] = jnp.int32(0)
        for block in range(block_count):
            seen = lax.fori_loop(
                0,
                slots,
                lambda image, sum, block=block, slot=slot: sum
                + jnp.where(owner_ref[image] == slot, images_ref[block, image], 0),
                jnp.int32(0),
            )

            @pl.when(seen > 0)
            def _(base=base, block=block, count=count):
                table_ref[base + 1 + count] = jnp.int32(block)

            count = count + jnp.where(seen > 0, 1, 0)
        table_ref[base] = count


def seen_table(position, block_images, image_owner):
    block_count, slots = block_images.shape
    return pl.pallas_call(
        table_kernel,
        out_shape=jax.ShapeDtypeStruct((slots * (block_count + 1),), jnp.int32),
        in_specs=[SMEM] * 3,
        out_specs=SMEM,
        name="seen_table",
    )(position, block_images, image_owner)


def chunks_of(width):
    half = width // LANES // 2 * LANES
    return [(0, half), (half, width)] if half else [(0, width)]


def cross_kernel(key_count, pieces, offset, last, parts, table_ref, *refs):
    q_refs, images, refs = refs[:parts], refs[parts : parts + pieces], refs[parts + pieces :]
    if offset:
        before, refs = refs[:2], refs[2:]
    if last:
        out_ref, lse_ref, high_ref, mixed_ref, peak_ref, redo_ref = refs
    else:
        high_ref, mixed_ref, peak_ref, redo_ref = refs
    block_count = q_refs[0].shape[0] // MASK_BLOCK_TOKENS
    rows = q_refs[0].shape[1] // HEAD_SIZE * MASK_BLOCK_TOKENS
    peak_ref[...] = jnp.full_like(peak_ref, LOWEST)
    redo_ref[0] = jnp.int32(0)

    def fold_pair(blocks, image, exact):
        width = image.shape[1]
        queries = [functools.reduce(jnp.add, [q[at_block(block), :] for q in q_refs]) for block in blocks]
        queries = jnp.concatenate([stacked_heads(one) for one in queries], axis=0)
        chunks = chunks_of(width)

        def scores_of(start, stop):
            scores = nt_dot(image[0, start:stop, :], queries)
            if stop > key_count:
                body = stop - start - LANES
                tail = scores[body:, :]
                key_id = start + body + lax.broadcasted_iota(jnp.int32, tail.shape, 0)
                tail = jnp.where(key_id < key_count, tail, LOWEST)
                scores = jnp.concatenate([scores[:body, :], tail], axis=0) if body else tail
            return scores

        @pl.when(exact)
        def _():
            tops = [jnp.max(scores_of(*chunk), axis=0, keepdims=True) for chunk in chunks]
            peak_ref[0:1, :] = functools.reduce(jnp.maximum, tops)

        high = jnp.concatenate([high_ref[block][0:1] for block in blocks], axis=1)
        mixed = jnp.concatenate([mixed_ref[block] for block in blocks], axis=1)
        scores = scores_of(*chunks[0])
        seen = jnp.max(scores[0 : min(SHIFT_KEYS, scores.shape[0])], axis=0, keepdims=True)
        new_high = jnp.maximum(jnp.maximum(high, seen), peak_ref[0:1, :])
        shift = new_high * LOG2_SCALE
        mixed = mixed * jnp.exp2((high - new_high) * LOG2_SCALE)
        for index, (start, stop) in enumerate(chunks):
            following = scores_of(*chunks[index + 1]) if index + 1 < len(chunks) else None
            weights = jnp.exp2(scores * LOG2_SCALE - shift).astype(jnp.bfloat16)
            value_t = jnp.concatenate([image[1, c : c + LANES, :] for c in range(start, stop, LANES)], axis=1)
            mixed = mixed + jnp.dot(with_ones(value_t), weights, preferred_element_type=jnp.float32)
            scores = following
        for index, block in enumerate(blocks):
            own = slice(index * rows, (index + 1) * rows)
            high_ref[block] = jnp.broadcast_to(new_high[:, own], high_ref.shape[1:])
            mixed_ref[block] = mixed[:, own]

    def attempt(trial, carry):
        @pl.when((trial == 0) | (redo_ref[0] > 0))
        def _():
            if offset:
                high_ref[...] = before[0][...]
                mixed_ref[...] = before[1][...]
            else:
                high_ref[...] = jnp.full_like(high_ref, LOWEST)
                mixed_ref[...] = jnp.zeros_like(mixed_ref)
            for piece in range(pieces):
                base = (offset + piece) * (block_count + 1)
                count = table_ref[base]

                def pair_step(pair, carry, piece=piece, base=base, count=count):
                    blocks = [table_ref[base + 1 + 2 * pair], table_ref[base + jnp.minimum(2 * pair + 2, count)]]
                    fold_pair(blocks, images[piece], trial > 0)
                    return carry

                lax.fori_loop(0, (count + 1) // 2, pair_step, 0)
            most = functools.reduce(
                jnp.maximum, [mixed_ref[block, HEAD_SIZE : HEAD_SIZE + 1, :] for block in range(block_count)]
            )
            redo_ref[0] = 1 - jnp.min((most <= MOST_SUM).astype(jnp.int32))

        return carry

    lax.fori_loop(0, 2, attempt, 0)

    if last:
        lse_ref[...] = jnp.zeros_like(lse_ref)
        for block in range(block_count):
            total = mixed_ref[block, HEAD_SIZE : HEAD_SIZE + 1, :]
            out_ref[block * HEAD_SIZE : (block + 1) * HEAD_SIZE, :] = (
                mixed_ref[block, 0:HEAD_SIZE, :] / total
            ).astype(jnp.bfloat16)
            lse_ref[block : block + 1, :] = high_ref[block, 0:1, :] * LOG2_SCALE + jnp.log2(total)
        out_ref[block_count * HEAD_SIZE :, :] = lse_pieces(lse_ref[0:block_count, :], block_count)


def cross_part(table, queries, images, key_count, offset, last, before=()):
    tokens, columns = queries[0].shape
    block_count = tokens // MASK_BLOCK_TOKENS
    rows = columns // HEAD_SIZE * MASK_BLOCK_TOKENS
    state = [(block_count, 8, rows), (block_count, MIXED_ROWS, rows)]
    scratch = [pltpu.VMEM((8, 2 * rows), jnp.float32), pltpu.SMEM((1,), jnp.int32)]
    if last:
        out_shape = jax.ShapeDtypeStruct((block_count * HEAD_SIZE + lse_rows(block_count), rows), jnp.bfloat16)
        scratch = [pltpu.VMEM(shape, jnp.float32) for shape in state] + scratch
        scratch = [pltpu.VMEM((-(-block_count // 8) * 8, rows), jnp.float32)] + scratch
    else:
        out_shape = tuple(jax.ShapeDtypeStruct(shape, jnp.float32) for shape in state)
    flops = 4 * block_count * rows * key_count * HEAD_SIZE * len(images)
    return pl.pallas_call(
        functools.partial(cross_kernel, key_count, len(images), offset, last, len(queries)),
        out_shape=out_shape,
        in_specs=[SMEM] + [VMEM] * (len(queries) + len(images) + len(before)),
        out_specs=VMEM if last else (VMEM,) * 2,
        scratch_shapes=scratch,
        compiler_params=pltpu.CompilerParams(vmem_limit_bytes=VMEM_LIMIT),
        cost_estimate=pl.CostEstimate(flops=2 * flops, bytes_accessed=4 * 1024 * 1024, transcendentals=0),
        name="cross_last" if last else "cross_first",
    )(table, *queries, *images, *before)


def lse_of(ref, block_count):
    tail = ref[block_count * HEAD_SIZE :, :].astype(jnp.float32)
    return tail[0:block_count] + tail[block_count : 2 * block_count] + tail[2 * block_count : 3 * block_count]


def lse_pieces(lse, block_count):
    first = lse.astype(jnp.bfloat16).astype(jnp.float32)
    second = (lse - first).astype(jnp.bfloat16).astype(jnp.float32)
    pieces = [first, second, lse - first - second]
    spare = lse_rows(block_count) - 3 * block_count
    if spare:
        pieces.append(jnp.zeros((spare, lse.shape[1]), jnp.float32))
    return jnp.concatenate(pieces, axis=0).astype(jnp.bfloat16)


def shares(lse):
    highest = functools.reduce(jnp.maximum, lse)
    weights = [jnp.exp2(one - highest) for one in lse]
    total = functools.reduce(jnp.add, weights)
    return [one / total for one in weights], highest + jnp.log2(total)


def mixed_block(part_refs, weights, block):
    at = slice(block * HEAD_SIZE, (block + 1) * HEAD_SIZE)
    terms = [weight[block : block + 1, :] * ref[at, :].astype(jnp.float32) for ref, weight in zip(part_refs, weights)]
    return functools.reduce(jnp.add, terms)


def merge_kernel(block_count, first_ref, second_ref, out_ref):
    part_refs = (first_ref, second_ref)
    weights, lse = shares([lse_of(ref, block_count) for ref in part_refs])
    for block in range(block_count):
        out_ref[block * HEAD_SIZE : (block + 1) * HEAD_SIZE, :] = mixed_block(part_refs, weights, block).astype(
            jnp.bfloat16
        )
    out_ref[block_count * HEAD_SIZE :, :] = lse_pieces(lse, block_count)


def merged(first, second, block_count):
    return pl.pallas_call(
        functools.partial(merge_kernel, block_count),
        out_shape=jax.ShapeDtypeStruct(first.shape, first.dtype),
        in_specs=[VMEM] * 2,
        out_specs=VMEM,
        compiler_params=pltpu.CompilerParams(vmem_limit_bytes=VMEM_LIMIT),
        cost_estimate=pl.CostEstimate(flops=0, bytes_accessed=1024 * 1024, transcendentals=0),
        name="merge",
    )(first, second)


def combine_kernel(counts, valid_ref, *refs):
    out_ref = refs[-1]
    block_count = out_ref.shape[0] // MASK_BLOCK_TOKENS
    lse, parts, at = [], [], 0
    for index, count in enumerate(counts):
        arrays = refs[at : at + count]
        at += count
        one = functools.reduce(jnp.add, [lse_of(ref, block_count) for ref in arrays])
        lse.append(jnp.where(valid_ref[index] > 0, one, LOWEST))
        parts.append(arrays)
    weights, _ = shares(lse)
    for block in range(block_count):
        arrays = [ref for part in parts for ref in part]
        each = [weight for part, weight in zip(parts, weights) for _ in part]
        store_heads(out_ref, block, mixed_block(arrays, each, block))


def store_heads(out_ref, block, mixed):
    at = slice(block * MASK_BLOCK_TOKENS, (block + 1) * MASK_BLOCK_TOKENS)
    for head in range(out_ref.shape[1] // HEAD_SIZE):
        piece = mixed[:, head * MASK_BLOCK_TOKENS : (head + 1) * MASK_BLOCK_TOKENS]
        out_ref[at, head * HEAD_SIZE : (head + 1) * HEAD_SIZE] = piece.T.astype(jnp.bfloat16)


def combined(valid, parts, shape):
    arrays = [array for part in parts for array in part]
    return pl.pallas_call(
        functools.partial(combine_kernel, tuple(len(part) for part in parts)),
        out_shape=jax.ShapeDtypeStruct(shape, jnp.bfloat16),
        in_specs=[SMEM] + [VMEM] * len(arrays),
        out_specs=VMEM,
        compiler_params=pltpu.CompilerParams(vmem_limit_bytes=VMEM_LIMIT),
        cost_estimate=pl.CostEstimate(flops=0, bytes_accessed=2 * 1024 * 1024, transcendentals=0),
        name="combine",
    )(valid, *arrays)


def pair_queries(q_ref, first, blocks):
    return jnp.concatenate(
        [
            stacked_heads(q_ref[block * MASK_BLOCK_TOKENS : (block + 1) * MASK_BLOCK_TOKENS, :])
            for block in range(first, first + blocks)
        ],
        axis=0,
    )


def self_first_kernel(group, q_ref, text_ref, high_ref, mixed_ref, value_ref):
    tokens, columns = q_ref.shape
    rows = columns // HEAD_SIZE * MASK_BLOCK_TOKENS
    value_ref[...] = text_ref[:, HEAD_SIZE:].T
    for index in range(tokens // MASK_BLOCK_TOKENS // group):
        first = index * group
        start, stop = first * MASK_BLOCK_TOKENS, (first + group) * MASK_BLOCK_TOKENS
        scores = nt_dot(text_ref[0:stop, 0:HEAD_SIZE], pair_queries(q_ref, first, group))
        tail = scores[start:, :]
        key_id = lax.broadcasted_iota(jnp.int32, tail.shape, 0)
        column = lax.broadcasted_iota(jnp.int32, tail.shape, 1)
        query_id = column // rows * MASK_BLOCK_TOKENS + column % MASK_BLOCK_TOKENS
        tail = jnp.where(key_id <= query_id, tail, LOWEST)
        scores = jnp.concatenate([scores[:start, :], tail], axis=0) if start else tail
        high = jnp.full((1, group * rows), LOWEST, jnp.float32)
        mixed = jnp.zeros((MIXED_ROWS, group * rows), jnp.float32)
        high, mixed = fold(high, mixed, scores, value_ref[:, 0:stop], True)
        high_ref[index] = jnp.broadcast_to(high, high_ref.shape[1:])
        mixed_ref[index] = mixed


def self_last_kernel(group, pieces, position_ref, q_ref, high_ref, mixed_ref, *refs):
    texts = refs[:pieces]
    out_ref, value_ref, new_high_ref, new_mixed_ref = refs[pieces:]
    rows = q_ref.shape[1] // HEAD_SIZE * MASK_BLOCK_TOKENS
    new_high_ref[...] = high_ref[...]
    new_mixed_ref[...] = mixed_ref[...]
    for piece in range(pieces):

        @pl.when(position_ref[0] >= piece + 1)
        def _(piece=piece):
            value_ref[...] = texts[piece][:, HEAD_SIZE:].T
            for index in range(high_ref.shape[0]):
                scores = nt_dot(texts[piece][:, 0:HEAD_SIZE], pair_queries(q_ref, index * group, group))
                high, mixed = fold(new_high_ref[index, 0:1, :], new_mixed_ref[index], scores, value_ref[...], True)
                new_high_ref[index] = jnp.broadcast_to(high, high_ref.shape[1:])
                new_mixed_ref[index] = mixed

    for index in range(high_ref.shape[0]):
        total = new_mixed_ref[index, HEAD_SIZE : HEAD_SIZE + 1, :]
        mixed = new_mixed_ref[index, 0:HEAD_SIZE, :] / total
        for block in range(group):
            store_heads(out_ref, index * group + block, mixed[:, block * rows : (block + 1) * rows])


def self_first(queries, text):
    tokens, columns = queries.shape
    block_count = tokens // MASK_BLOCK_TOKENS
    group = 1 if block_count % 2 else 2
    width = group * columns // HEAD_SIZE * MASK_BLOCK_TOKENS
    return pl.pallas_call(
        functools.partial(self_first_kernel, group),
        out_shape=(
            jax.ShapeDtypeStruct((block_count // group, 8, width), jnp.float32),
            jax.ShapeDtypeStruct((block_count // group, MIXED_ROWS, width), jnp.float32),
        ),
        in_specs=[VMEM] * 2,
        out_specs=(VMEM,) * 2,
        scratch_shapes=[pltpu.VMEM((HEAD_SIZE, tokens), jnp.bfloat16)],
        compiler_params=pltpu.CompilerParams(vmem_limit_bytes=VMEM_LIMIT),
        cost_estimate=pl.CostEstimate(flops=8 * tokens * columns * tokens, bytes_accessed=1024 * 1024, transcendentals=0),
        name="self_first",
    )(queries, text)


def self_last(position, queries, state, texts):
    tokens, columns = queries.shape
    group = tokens // MASK_BLOCK_TOKENS // state[0].shape[0]
    return pl.pallas_call(
        functools.partial(self_last_kernel, group, len(texts)),
        out_shape=jax.ShapeDtypeStruct((tokens, columns), jnp.bfloat16),
        in_specs=[SMEM] + [VMEM] * (3 + len(texts)),
        out_specs=VMEM,
        scratch_shapes=[pltpu.VMEM((HEAD_SIZE, tokens), jnp.bfloat16)]
        + [pltpu.VMEM(one.shape, jnp.float32) for one in state],
        compiler_params=pltpu.CompilerParams(vmem_limit_bytes=VMEM_LIMIT),
        cost_estimate=pl.CostEstimate(flops=8 * tokens * columns * tokens, bytes_accessed=1024 * 1024, transcendentals=0),
        name="self_last",
    )(position, queries, *state, *texts)


def shifted(value, axis, steps):
    count = lax.axis_size(axis)
    return lax.ppermute(value, axis, [(source, (source + steps) % count) for source in range(count)])


def swapped(value, axis, bits):
    return lax.ppermute(value, axis, [(source, source ^ bits) for source in range(lax.axis_size(axis))])


def moved(value, pairs):
    return lax.ppermute(value, "enc", pairs)


def gathered_queries(queries, ring):
    if ring != 4:
        return {step: [shifted(queries, "enc", ring - step)] for step in range(1, ring)}
    next_but_one = swapped(queries, "enc", 2)
    near = swapped(queries, "enc", 1)
    middle = moved(queries, [(1, 2), (2, 1)])
    ends = moved(next_but_one, [(2, 3), (1, 0)])
    return {1: [near], 2: [next_but_one], 3: [middle, ends]}


def after(value, earlier):
    return lax.optimization_barrier((value, earlier))[0]


def per_device(
    self_queries, text_kv, cross_queries, image_kv, block_images, image_owner
):
    rows = self_queries.shape[0]
    block_count = rows // MASK_BLOCK_TOKENS
    key_count = image_kv.shape[2]
    cycle = lax.axis_size("blk")
    ring = lax.axis_size("enc")
    position = lax.axis_index("blk").astype(jnp.int32)[None]
    place = lax.axis_index("enc").astype(jnp.int32)

    images = [prepare(image_kv[0])]
    for _ in range(1, cycle):
        images.append(shifted(images[-1], "blk", 1))
    queries = gathered_queries(cross_queries, ring)
    queries[0] = [cross_queries]
    table = seen_table(position, block_images, image_owner)

    text = text_kv.reshape(rows, 2 * HEAD_SIZE)
    texts = []
    onward = after(text, images[-1])
    for _ in range(1, cycle):
        onward = lax.ppermute(onward, "blk", [(source, source + 1) for source in range(cycle - 1)])
        texts.append(onward)

    latest = [None]

    def in_turn(arrays):
        return arrays if latest[0] is None else [after(one, latest[0]) for one in arrays]

    def begun(step):
        latest[0] = cross_part(table, in_turn(queries[step]), images[:1], key_count, 0, False)
        return latest[0]

    def finished(step, state=None):
        used = images if state is None else images[1:]
        before = () if state is None else state
        offset = 0 if state is None else 1
        latest[0] = cross_part(table, in_turn(queries[step]), used, key_count, offset, True, before)
        return latest[0]

    split = cycle > 1
    own = begun(0) if split else None
    self_state = latest[0] = self_first(in_turn([self_queries])[0], text)
    if ring == 4:
        second = begun(2) if split else None
        near = begun(1) if split else None
        far_part = finished(3)
        far_in = moved(far_part, [(0, 1), (3, 2)])
        far_middle = moved(far_part, [(1, 2), (2, 1)])
        second_part = finished(2, second)
        second_ends = moved(second_part, [(0, 2), (3, 1)])
        near_in = swapped(finished(1, near), "enc", 1)
        latest[0] = both = merged(second_part, after(far_in, latest[0]), block_count)
        second_middle = moved(both, [(1, 3), (2, 0)])
        received = [[near_in], [second_ends, second_middle], [far_middle]]
        inside = ((place == 1) | (place == 2)).astype(jnp.int32)
        valid = jnp.stack([jnp.int32(1), jnp.int32(1), jnp.int32(1), inside])
    else:
        received = [[shifted(finished(step), "enc", step)] for step in range(1, ring)]
        valid = jnp.ones((ring,), jnp.int32)
    own_part = finished(0, own)
    self_out = self_last(position, in_turn([self_queries])[0], self_state, texts)
    cross_out = combined(valid, [[own_part]] + received, cross_queries.shape)
    return (self_out, cross_out)


def solution(mesh):
    placed = (
        P("blk", ("tp", "enc")),
        P("blk", None, "tp"),
        P("blk", ("tp", "enc")),
        P("blk", None, "enc", "tp"),
        P("blk", None),
        P(),
    )
    return jax.shard_map(
        per_device,
        mesh=mesh,
        in_specs=placed,
        out_specs=(P("blk", ("tp", "enc")), P("blk", ("tp", "enc"))),
        check_vma=False,
    )
```

```python
import functools
import math

import jax
import jax.numpy as jnp
from jax import lax
from jax.experimental import pallas as pl
from jax.experimental.pallas import tpu as pltpu
from jax.sharding import PartitionSpec as P

HEAD_SIZE = 128
MASK_BLOCK_TOKENS = 128
LANES = 128
LOWEST = -1e30
MIXED_ROWS = HEAD_SIZE + 16
SHIFT_KEYS = 256
MOST_SUM = 2.0**100
LOG2_SCALE = math.log2(math.e) / math.sqrt(HEAD_SIZE)
VMEM_LIMIT = 48 * 1024 * 1024

LITTLE = pl.CostEstimate(flops=0, bytes_accessed=1024, transcendentals=0)
MUCH = pl.CostEstimate(flops=2_000_000_000, bytes_accessed=1024, transcendentals=0)

VMEM = pl.BlockSpec(memory_space=pltpu.VMEM)
SMEM = pl.BlockSpec(memory_space=pltpu.SMEM)


def padded(count):
    return -(-count // LANES) * LANES


def nt_dot(a, b):
    return lax.dot_general(a, b, (((1,), (1,)), ((), ())), preferred_element_type=jnp.float32)


def at_block(block, size=MASK_BLOCK_TOKENS):
    return pl.ds(pl.multiple_of(block * size, size), size)


def stacked_heads(rows):
    heads = rows.shape[1] // HEAD_SIZE
    return jnp.concatenate([rows[:, h * HEAD_SIZE : (h + 1) * HEAD_SIZE] for h in range(heads)], axis=0)


def with_ones(value_t):
    shape = (MIXED_ROWS - HEAD_SIZE, value_t.shape[1])
    ones = (lax.broadcasted_iota(jnp.int32, shape, 0) == 0).astype(jnp.bfloat16)
    return jnp.concatenate([value_t, ones], axis=0)


def fold(high, mixed, scores, value_t, exact):
    seen = scores if exact else scores[0 : min(SHIFT_KEYS, scores.shape[0]), :]
    new_high = jnp.maximum(high, jnp.max(seen, axis=0, keepdims=True))
    weights = jnp.exp2(scores * LOG2_SCALE - new_high * LOG2_SCALE).astype(jnp.bfloat16)
    fading = jnp.exp2((high - new_high) * LOG2_SCALE)
    mixed = mixed * fading + jnp.dot(with_ones(value_t), weights, preferred_element_type=jnp.float32)
    return new_high, mixed


def prepare_kernel(kv_ref, out_ref):
    count = kv_ref.shape[1]
    whole = count // LANES * LANES
    rest = count - whole
    out_ref[0, 0:whole, :] = kv_ref[0, 0:whole, :]
    for at in range(0, whole, LANES):
        out_ref[1, at : at + LANES, :] = kv_ref[1, at : at + LANES, :].T
    if rest:
        empty = jnp.zeros((LANES - rest, HEAD_SIZE), jnp.float32)
        tail_key = jnp.concatenate([kv_ref[0, whole:count, :].astype(jnp.float32), empty], axis=0)
        tail_value = jnp.concatenate([kv_ref[1, whole:count, :].astype(jnp.float32), empty], axis=0)
        out_ref[0, whole : whole + LANES, :] = tail_key.astype(jnp.bfloat16)
        out_ref[1, whole : whole + LANES, :] = tail_value.T.astype(jnp.bfloat16)


def prepare(kv):
    return pl.pallas_call(
        prepare_kernel,
        out_shape=jax.ShapeDtypeStruct((2, padded(kv.shape[1]), HEAD_SIZE), jnp.bfloat16),
        in_specs=[VMEM],
        out_specs=VMEM,
        compiler_params=pltpu.CompilerParams(vmem_limit_bytes=VMEM_LIMIT),
        cost_estimate=LITTLE,
        name="prepare",
    )(kv)


def lse_rows(block_count):
    return -(-3 * block_count // 16) * 16


def packed_blocks(rows):
    return next(count for count in range(1, rows) if count * HEAD_SIZE + lse_rows(count) == rows)


def table_kernel(position_ref, images_ref, owner_ref, table_ref):
    block_count, slots = images_ref.shape
    for piece in range(slots):
        slot = lax.rem(position_ref[0] + (slots - piece), slots)
        base = piece * (block_count + 1)
        count = jnp.int32(0)
        for block in range(block_count):
            table_ref[base + 1 + block] = jnp.int32(0)
        for block in range(block_count):
            seen = lax.fori_loop(
                0,
                slots,
                lambda image, sum, block=block, slot=slot: sum
                + jnp.where(owner_ref[image] == slot, images_ref[block, image], 0),
                jnp.int32(0),
            )

            @pl.when(seen > 0)
            def _(base=base, block=block, count=count):
                table_ref[base + 1 + count] = jnp.int32(block)

            count = count + jnp.where(seen > 0, 1, 0)
        table_ref[base] = count


def seen_table(position, block_images, image_owner):
    block_count, slots = block_images.shape
    return pl.pallas_call(
        table_kernel,
        out_shape=jax.ShapeDtypeStruct((slots * (block_count + 1),), jnp.int32),
        in_specs=[SMEM] * 3,
        out_specs=SMEM,
        name="seen_table",
    )(position, block_images, image_owner)


def chunks_of(width):
    half = width // LANES // 2 * LANES
    return [(0, half), (half, width)] if half else [(0, width)]


def cross_kernel(key_count, pieces, offset, last, parts, table_ref, *refs):
    q_refs, images, refs = refs[:parts], refs[parts : parts + pieces], refs[parts + pieces :]
    if offset:
        before, refs = refs[:2], refs[2:]
    if last:
        out_ref, lse_ref, high_ref, mixed_ref, peak_ref, redo_ref = refs
    else:
        high_ref, mixed_ref, peak_ref, redo_ref = refs
    block_count = q_refs[0].shape[0] // MASK_BLOCK_TOKENS
    rows = q_refs[0].shape[1] // HEAD_SIZE * MASK_BLOCK_TOKENS
    peak_ref[...] = jnp.full_like(peak_ref, LOWEST)
    redo_ref[0] = jnp.int32(0)

    def fold_pair(blocks, image, exact):
        width = image.shape[1]
        queries = [functools.reduce(jnp.add, [q[at_block(block), :] for q in q_refs]) for block in blocks]
        queries = jnp.concatenate([stacked_heads(one) for one in queries], axis=0)
        chunks = chunks_of(width)

        def scores_of(start, stop):
            scores = nt_dot(image[0, start:stop, :], queries)
            if stop > key_count:
                body = stop - start - LANES
                tail = scores[body:, :]
                key_id = start + body + lax.broadcasted_iota(jnp.int32, tail.shape, 0)
                tail = jnp.where(key_id < key_count, tail, LOWEST)
                scores = jnp.concatenate([scores[:body, :], tail], axis=0) if body else tail
            return scores

        @pl.when(exact)
        def _():
            tops = [jnp.max(scores_of(*chunk), axis=0, keepdims=True) for chunk in chunks]
            peak_ref[0:1, :] = functools.reduce(jnp.maximum, tops)

        high = jnp.concatenate([high_ref[block][0:1] for block in blocks], axis=1)
        mixed = jnp.concatenate([mixed_ref[block] for block in blocks], axis=1)
        scores = scores_of(*chunks[0])
        seen = jnp.max(scores[0 : min(SHIFT_KEYS, scores.shape[0])], axis=0, keepdims=True)
        new_high = jnp.maximum(jnp.maximum(high, seen), peak_ref[0:1, :])
        shift = new_high * LOG2_SCALE
        mixed = mixed * jnp.exp2((high - new_high) * LOG2_SCALE)
        for index, (start, stop) in enumerate(chunks):
            following = scores_of(*chunks[index + 1]) if index + 1 < len(chunks) else None
            weights = jnp.exp2(scores * LOG2_SCALE - shift).astype(jnp.bfloat16)
            value_t = jnp.concatenate([image[1, c : c + LANES, :] for c in range(start, stop, LANES)], axis=1)
            mixed = mixed + jnp.dot(with_ones(value_t), weights, preferred_element_type=jnp.float32)
            scores = following
        for index, block in enumerate(blocks):
            own = slice(index * rows, (index + 1) * rows)
            high_ref[block] = jnp.broadcast_to(new_high[:, own], high_ref.shape[1:])
            mixed_ref[block] = mixed[:, own]

    def attempt(trial, carry):
        @pl.when((trial == 0) | (redo_ref[0] > 0))
        def _():
            if offset:
                high_ref[...] = before[0][...]
                mixed_ref[...] = before[1][...]
            else:
                high_ref[...] = jnp.full_like(high_ref, LOWEST)
                mixed_ref[...] = jnp.zeros_like(mixed_ref)
            for piece in range(pieces):
                base = (offset + piece) * (block_count + 1)
                count = table_ref[base]

                def pair_step(pair, carry, piece=piece, base=base, count=count):
                    blocks = [table_ref[base + 1 + 2 * pair], table_ref[base + jnp.minimum(2 * pair + 2, count)]]
                    fold_pair(blocks, images[piece], trial > 0)
                    return carry

                lax.fori_loop(0, (count + 1) // 2, pair_step, 0)
            most = functools.reduce(
                jnp.maximum, [mixed_ref[block, HEAD_SIZE : HEAD_SIZE + 1, :] for block in range(block_count)]
            )
            redo_ref[0] = 1 - jnp.min((most <= MOST_SUM).astype(jnp.int32))

        return carry

    lax.fori_loop(0, 2, attempt, 0)

    if last:
        lse_ref[...] = jnp.zeros_like(lse_ref)
        for block in range(block_count):
            total = mixed_ref[block, HEAD_SIZE : HEAD_SIZE + 1, :]
            out_ref[block * HEAD_SIZE : (block + 1) * HEAD_SIZE, :] = (
                mixed_ref[block, 0:HEAD_SIZE, :] / total
            ).astype(jnp.bfloat16)
            lse_ref[block : block + 1, :] = high_ref[block, 0:1, :] * LOG2_SCALE + jnp.log2(total)
        out_ref[block_count * HEAD_SIZE :, :] = lse_pieces(lse_ref[0:block_count, :], block_count)


def cross_part(table, queries, images, key_count, offset, last, before=()):
    tokens, columns = queries[0].shape
    block_count = tokens // MASK_BLOCK_TOKENS
    rows = columns // HEAD_SIZE * MASK_BLOCK_TOKENS
    state = [(block_count, 8, rows), (block_count, MIXED_ROWS, rows)]
    scratch = [pltpu.VMEM((8, 2 * rows), jnp.float32), pltpu.SMEM((1,), jnp.int32)]
    if last:
        out_shape = jax.ShapeDtypeStruct((block_count * HEAD_SIZE + lse_rows(block_count), rows), jnp.bfloat16)
        scratch = [pltpu.VMEM(shape, jnp.float32) for shape in state] + scratch
        scratch = [pltpu.VMEM((-(-block_count // 8) * 8, rows), jnp.float32)] + scratch
    else:
        out_shape = tuple(jax.ShapeDtypeStruct(shape, jnp.float32) for shape in state)
    return pl.pallas_call(
        functools.partial(cross_kernel, key_count, len(images), offset, last, len(queries)),
        out_shape=out_shape,
        in_specs=[SMEM] + [VMEM] * (len(queries) + len(images) + len(before)),
        out_specs=VMEM if last else (VMEM,) * 2,
        scratch_shapes=scratch,
        compiler_params=pltpu.CompilerParams(vmem_limit_bytes=VMEM_LIMIT),
        cost_estimate=MUCH,
        name="cross_last" if last else "cross_first",
    )(table, *queries, *images, *before)


def lse_of(ref, block_count):
    tail = ref[block_count * HEAD_SIZE :, :].astype(jnp.float32)
    return tail[0:block_count] + tail[block_count : 2 * block_count] + tail[2 * block_count : 3 * block_count]


def lse_pieces(lse, block_count):
    first = lse.astype(jnp.bfloat16).astype(jnp.float32)
    second = (lse - first).astype(jnp.bfloat16).astype(jnp.float32)
    pieces = [first, second, lse - first - second]
    spare = lse_rows(block_count) - 3 * block_count
    if spare:
        pieces.append(jnp.zeros((spare, lse.shape[1]), jnp.float32))
    return jnp.concatenate(pieces, axis=0).astype(jnp.bfloat16)


def mixed_block(part_refs, weights, block):
    at = slice(block * HEAD_SIZE, (block + 1) * HEAD_SIZE)
    terms = [weight[block : block + 1, :] * ref[at, :].astype(jnp.float32) for ref, weight in zip(part_refs, weights)]
    return functools.reduce(jnp.add, terms)


def combine_kernel(held, last, *refs):
    if held:
        mixed_ref, lse_ref, part_ref, *out_refs = refs
        block_count = lse_ref.shape[0]
        lse = [lse_ref[...], lse_of(part_ref, block_count)]
    else:
        mixed_ref, part_ref, *out_refs = refs
        block_count = packed_blocks(part_ref.shape[0])
        lse = [lse_of(mixed_ref, block_count), lse_of(part_ref, block_count)]
    highest = functools.reduce(jnp.maximum, lse)
    weights = [jnp.exp2(one - highest) for one in lse]
    total = functools.reduce(jnp.add, weights)
    weights = [one / total for one in weights]
    for block in range(block_count):
        mixed = mixed_block((mixed_ref, part_ref), weights, block)
        if last:
            store_heads(out_refs[0], block, mixed)
        else:
            out_refs[0][block * HEAD_SIZE : (block + 1) * HEAD_SIZE, :] = mixed
    if not last:
        out_refs[1][...] = highest + jnp.log2(total)


def store_heads(out_ref, block, mixed):
    at = slice(block * MASK_BLOCK_TOKENS, (block + 1) * MASK_BLOCK_TOKENS)
    for head in range(out_ref.shape[1] // HEAD_SIZE):
        piece = mixed[:, head * MASK_BLOCK_TOKENS : (head + 1) * MASK_BLOCK_TOKENS]
        out_ref[at, head * HEAD_SIZE : (head + 1) * HEAD_SIZE] = piece.T.astype(jnp.bfloat16)


def combined(so_far, part, shape, last):
    tokens, columns = shape
    held = len(so_far) == 2
    block_count = tokens // MASK_BLOCK_TOKENS
    rows = columns // HEAD_SIZE * MASK_BLOCK_TOKENS
    if last:
        out_shape = jax.ShapeDtypeStruct(shape, jnp.bfloat16)
    else:
        out_shape = (
            jax.ShapeDtypeStruct((block_count * HEAD_SIZE, rows), jnp.float32),
            jax.ShapeDtypeStruct((block_count, rows), jnp.float32),
        )
    return pl.pallas_call(
        functools.partial(combine_kernel, held, last),
        out_shape=out_shape,
        in_specs=[VMEM] * (len(so_far) + 1),
        out_specs=VMEM if last else (VMEM,) * 2,
        compiler_params=pltpu.CompilerParams(vmem_limit_bytes=VMEM_LIMIT),
        cost_estimate=MUCH,
        name="combine_last" if last else "combine",
    )(*so_far, part)


def pair_queries(q_ref, first, blocks):
    return jnp.concatenate(
        [
            stacked_heads(q_ref[block * MASK_BLOCK_TOKENS : (block + 1) * MASK_BLOCK_TOKENS, :])
            for block in range(first, first + blocks)
        ],
        axis=0,
    )


def self_first_kernel(group, q_ref, text_ref, high_ref, mixed_ref, value_ref):
    tokens, columns = q_ref.shape
    rows = columns // HEAD_SIZE * MASK_BLOCK_TOKENS
    value_ref[...] = text_ref[:, HEAD_SIZE:].T
    for index in range(tokens // MASK_BLOCK_TOKENS // group):
        first = index * group
        start, stop = first * MASK_BLOCK_TOKENS, (first + group) * MASK_BLOCK_TOKENS
        scores = nt_dot(text_ref[0:stop, 0:HEAD_SIZE], pair_queries(q_ref, first, group))
        tail = scores[start:, :]
        key_id = lax.broadcasted_iota(jnp.int32, tail.shape, 0)
        column = lax.broadcasted_iota(jnp.int32, tail.shape, 1)
        query_id = column // rows * MASK_BLOCK_TOKENS + column % MASK_BLOCK_TOKENS
        tail = jnp.where(key_id <= query_id, tail, LOWEST)
        scores = jnp.concatenate([scores[:start, :], tail], axis=0) if start else tail
        high = jnp.full((1, group * rows), LOWEST, jnp.float32)
        mixed = jnp.zeros((MIXED_ROWS, group * rows), jnp.float32)
        high, mixed = fold(high, mixed, scores, value_ref[:, 0:stop], True)
        high_ref[index] = jnp.broadcast_to(high, high_ref.shape[1:])
        mixed_ref[index] = mixed


def self_last_kernel(group, pieces, position_ref, q_ref, high_ref, mixed_ref, *refs):
    texts = refs[:pieces]
    out_ref, value_ref, new_high_ref, new_mixed_ref = refs[pieces:]
    rows = q_ref.shape[1] // HEAD_SIZE * MASK_BLOCK_TOKENS
    new_high_ref[...] = high_ref[...]
    new_mixed_ref[...] = mixed_ref[...]
    for piece in range(pieces):

        @pl.when(position_ref[0] >= piece + 1)
        def _(piece=piece):
            value_ref[...] = texts[piece][:, HEAD_SIZE:].T
            for index in range(high_ref.shape[0]):
                scores = nt_dot(texts[piece][:, 0:HEAD_SIZE], pair_queries(q_ref, index * group, group))
                high, mixed = fold(new_high_ref[index, 0:1, :], new_mixed_ref[index], scores, value_ref[...], True)
                new_high_ref[index] = jnp.broadcast_to(high, high_ref.shape[1:])
                new_mixed_ref[index] = mixed

    for index in range(high_ref.shape[0]):
        total = new_mixed_ref[index, HEAD_SIZE : HEAD_SIZE + 1, :]
        mixed = new_mixed_ref[index, 0:HEAD_SIZE, :] / total
        for block in range(group):
            store_heads(out_ref, index * group + block, mixed[:, block * rows : (block + 1) * rows])


def self_first(queries, text):
    tokens, columns = queries.shape
    block_count = tokens // MASK_BLOCK_TOKENS
    group = 1 if block_count % 2 else 2
    width = group * columns // HEAD_SIZE * MASK_BLOCK_TOKENS
    return pl.pallas_call(
        functools.partial(self_first_kernel, group),
        out_shape=(
            jax.ShapeDtypeStruct((block_count // group, 8, width), jnp.float32),
            jax.ShapeDtypeStruct((block_count // group, MIXED_ROWS, width), jnp.float32),
        ),
        in_specs=[VMEM] * 2,
        out_specs=(VMEM,) * 2,
        scratch_shapes=[pltpu.VMEM((HEAD_SIZE, tokens), jnp.bfloat16)],
        compiler_params=pltpu.CompilerParams(vmem_limit_bytes=VMEM_LIMIT),
        cost_estimate=LITTLE,
        name="self_first",
    )(queries, text)


def self_last(position, queries, state, texts):
    tokens, columns = queries.shape
    group = tokens // MASK_BLOCK_TOKENS // state[0].shape[0]
    return pl.pallas_call(
        functools.partial(self_last_kernel, group, len(texts)),
        out_shape=jax.ShapeDtypeStruct((tokens, columns), jnp.bfloat16),
        in_specs=[SMEM] + [VMEM] * (3 + len(texts)),
        out_specs=VMEM,
        scratch_shapes=[pltpu.VMEM((HEAD_SIZE, tokens), jnp.bfloat16)]
        + [pltpu.VMEM(one.shape, jnp.float32) for one in state],
        compiler_params=pltpu.CompilerParams(vmem_limit_bytes=VMEM_LIMIT),
        cost_estimate=LITTLE,
        name="self_last",
    )(position, queries, *state, *texts)


def shifted(value, axis, steps):
    count = lax.axis_size(axis)
    return lax.ppermute(value, axis, [(source, (source + steps) % count) for source in range(count)])


def swapped(value, axis, bits):
    return lax.ppermute(value, axis, [(source, source ^ bits) for source in range(lax.axis_size(axis))])


def moved(value, pairs):
    return lax.ppermute(value, "enc", pairs)


def gathered_queries(queries, ring):
    if ring != 4:
        return {step: [shifted(queries, "enc", ring - step)] for step in range(1, ring)}
    next_but_one = swapped(queries, "enc", 2)
    near = swapped(queries, "enc", 1)
    middle = moved(queries, [(1, 2), (2, 1)])
    ends = moved(next_but_one, [(2, 3), (1, 0)])
    return {1: [near], 2: [next_but_one], 3: [middle, ends]}


def after(value, earlier):
    return lax.optimization_barrier((value, earlier))[0]


def per_device(
    self_queries, text_kv, cross_queries, image_kv, block_images, image_owner
):
    rows = self_queries.shape[0]
    key_count = image_kv.shape[2]
    cycle = lax.axis_size("blk")
    ring = lax.axis_size("enc")
    position = lax.axis_index("blk").astype(jnp.int32)[None]

    images = [prepare(image_kv[0])]
    for _ in range(1, cycle):
        images.append(shifted(images[-1], "blk", 1))
    queries = gathered_queries(cross_queries, ring)
    queries[0] = [cross_queries]
    table = seen_table(position, block_images, image_owner)

    text = text_kv.reshape(rows, 2 * HEAD_SIZE)
    texts = []
    onward = after(text, images[-1])
    for _ in range(1, cycle):
        onward = lax.ppermute(onward, "blk", [(source, source + 1) for source in range(cycle - 1)])
        texts.append(onward)

    latest = [None]

    def in_turn(arrays):
        return arrays if latest[0] is None else [after(one, latest[0]) for one in arrays]

    def begun(step):
        latest[0] = cross_part(table, in_turn(queries[step]), images[:1], key_count, 0, False)
        return latest[0]

    def finished(step, state=None):
        used = images if state is None else images[1:]
        before = () if state is None else state
        offset = 0 if state is None else 1
        latest[0] = cross_part(table, in_turn(queries[step]), used, key_count, offset, True, before)
        return latest[0]

    split = cycle > 1
    own = begun(0) if split else None
    self_state = latest[0] = self_first(in_turn([self_queries])[0], text)
    steps = [2, 1, 3] if ring == 4 else list(range(1, ring))
    states = {step: begun(step) for step in steps[:-1]} if split else {}
    received = []
    for step in [2, 3, 1] if ring == 4 else steps:
        part = finished(step, states.get(step))
        received.append(swapped(part, "enc", step) if ring == 4 else shifted(part, "enc", step))
    own_part = finished(0, own)
    self_out = latest[0] = self_last(position, in_turn([self_queries])[0], self_state, texts)
    so_far = in_turn([own_part])
    for index, part in enumerate(received):
        so_far = combined(so_far, part, cross_queries.shape, index + 1 == len(received))
    return (self_out, so_far)


def solution(mesh):
    placed = (
        P("blk", ("tp", "enc")),
        P("blk", None, "tp"),
        P("blk", ("tp", "enc")),
        P("blk", None, "enc", "tp"),
        P("blk", None),
        P(),
    )
    return jax.shard_map(
        per_device,
        mesh=mesh,
        in_specs=placed,
        out_specs=(P("blk", ("tp", "enc")), P("blk", ("tp", "enc"))),
        check_vma=False,
    )
```

```python
import functools
import math

import jax
import jax.numpy as jnp
from jax import lax
from jax.experimental import pallas as pl
from jax.experimental.pallas import tpu as pltpu
from jax.sharding import PartitionSpec as P

HEAD_SIZE = 128
MASK_BLOCK_TOKENS = 128
LANES = 128
LOWEST = -1e30
MIXED_ROWS = HEAD_SIZE + 16
SHIFT_KEYS = 256
MOST_SUM = 2.0**100
LOG2_SCALE = math.log2(math.e) / math.sqrt(HEAD_SIZE)
VMEM_LIMIT = 48 * 1024 * 1024

LITTLE = pl.CostEstimate(flops=0, bytes_accessed=1024, transcendentals=0)
MUCH = pl.CostEstimate(flops=2_000_000_000, bytes_accessed=1024, transcendentals=0)

VMEM = pl.BlockSpec(memory_space=pltpu.VMEM)
SMEM = pl.BlockSpec(memory_space=pltpu.SMEM)


def padded(count):
    return -(-count // LANES) * LANES


def nt_dot(a, b):
    return lax.dot_general(a, b, (((1,), (1,)), ((), ())), preferred_element_type=jnp.float32)


def at_block(block, size=MASK_BLOCK_TOKENS):
    return pl.ds(pl.multiple_of(block * size, size), size)


def stacked_heads(rows):
    heads = rows.shape[1] // HEAD_SIZE
    return jnp.concatenate([rows[:, h * HEAD_SIZE : (h + 1) * HEAD_SIZE] for h in range(heads)], axis=0)


def with_ones(value_t):
    shape = (MIXED_ROWS - HEAD_SIZE, value_t.shape[1])
    ones = (lax.broadcasted_iota(jnp.int32, shape, 0) == 0).astype(jnp.bfloat16)
    return jnp.concatenate([value_t, ones], axis=0)


def fold(high, mixed, scores, value_t, exact):
    seen = scores if exact else scores[0 : min(SHIFT_KEYS, scores.shape[0]), :]
    new_high = jnp.maximum(high, jnp.max(seen, axis=0, keepdims=True))
    weights = jnp.exp2(scores * LOG2_SCALE - new_high * LOG2_SCALE).astype(jnp.bfloat16)
    fading = jnp.exp2((high - new_high) * LOG2_SCALE)
    mixed = mixed * fading + jnp.dot(with_ones(value_t), weights, preferred_element_type=jnp.float32)
    return new_high, mixed


def prepare_kernel(kv_ref, out_ref):
    count = kv_ref.shape[1]
    whole = count // LANES * LANES
    rest = count - whole
    out_ref[0, 0:whole, :] = kv_ref[0, 0:whole, :]
    for at in range(0, whole, LANES):
        out_ref[1, at : at + LANES, :] = kv_ref[1, at : at + LANES, :].T
    if rest:
        empty = jnp.zeros((LANES - rest, HEAD_SIZE), jnp.float32)
        tail_key = jnp.concatenate([kv_ref[0, whole:count, :].astype(jnp.float32), empty], axis=0)
        tail_value = jnp.concatenate([kv_ref[1, whole:count, :].astype(jnp.float32), empty], axis=0)
        out_ref[0, whole : whole + LANES, :] = tail_key.astype(jnp.bfloat16)
        out_ref[1, whole : whole + LANES, :] = tail_value.T.astype(jnp.bfloat16)


def prepare(kv):
    return pl.pallas_call(
        prepare_kernel,
        out_shape=jax.ShapeDtypeStruct((2, padded(kv.shape[1]), HEAD_SIZE), jnp.bfloat16),
        in_specs=[VMEM],
        out_specs=VMEM,
        compiler_params=pltpu.CompilerParams(vmem_limit_bytes=VMEM_LIMIT),
        cost_estimate=LITTLE,
        name="prepare",
    )(kv)


def lse_rows(block_count):
    return -(-3 * block_count // 16) * 16


def packed_blocks(rows):
    return next(count for count in range(1, rows) if count * HEAD_SIZE + lse_rows(count) == rows)


def table_kernel(position_ref, images_ref, owner_ref, table_ref):
    block_count, slots = images_ref.shape
    for piece in range(slots):
        slot = lax.rem(position_ref[0] + (slots - piece), slots)
        base = piece * (block_count + 1)
        count = jnp.int32(0)
        for block in range(block_count):
            table_ref[base + 1 + block] = jnp.int32(0)
        for block in range(block_count):
            seen = lax.fori_loop(
                0,
                slots,
                lambda image, sum, block=block, slot=slot: sum
                + jnp.where(owner_ref[image] == slot, images_ref[block, image], 0),
                jnp.int32(0),
            )

            @pl.when(seen > 0)
            def _(base=base, block=block, count=count):
                table_ref[base + 1 + count] = jnp.int32(block)

            count = count + jnp.where(seen > 0, 1, 0)
        table_ref[base] = count


def seen_table(position, block_images, image_owner):
    block_count, slots = block_images.shape
    return pl.pallas_call(
        table_kernel,
        out_shape=jax.ShapeDtypeStruct((slots * (block_count + 1),), jnp.int32),
        in_specs=[SMEM] * 3,
        out_specs=SMEM,
        name="seen_table",
    )(position, block_images, image_owner)


def chunks_of(width):
    half = width // LANES // 2 * LANES
    return [(0, half), (half, width)] if half else [(0, width)]


def cross_kernel(key_count, pieces, offset, last, parts, table_ref, *refs):
    q_refs, images, refs = refs[:parts], refs[parts : parts + pieces], refs[parts + pieces :]
    if offset:
        before, refs = refs[:2], refs[2:]
    if last:
        out_ref, lse_ref, high_ref, mixed_ref, peak_ref, redo_ref = refs
    else:
        high_ref, mixed_ref, peak_ref, redo_ref = refs
    block_count = q_refs[0].shape[0] // MASK_BLOCK_TOKENS
    rows = q_refs[0].shape[1] // HEAD_SIZE * MASK_BLOCK_TOKENS
    peak_ref[...] = jnp.full_like(peak_ref, LOWEST)
    redo_ref[0] = jnp.int32(0)

    def fold_pair(blocks, image, exact):
        width = image.shape[1]
        queries = [functools.reduce(jnp.add, [q[at_block(block), :] for q in q_refs]) for block in blocks]
        queries = jnp.concatenate([stacked_heads(one) for one in queries], axis=0)
        chunks = chunks_of(width)

        def scores_of(start, stop):
            scores = nt_dot(image[0, start:stop, :], queries)
            if stop > key_count:
                body = stop - start - LANES
                tail = scores[body:, :]
                key_id = start + body + lax.broadcasted_iota(jnp.int32, tail.shape, 0)
                tail = jnp.where(key_id < key_count, tail, LOWEST)
                scores = jnp.concatenate([scores[:body, :], tail], axis=0) if body else tail
            return scores

        @pl.when(exact)
        def _():
            tops = [jnp.max(scores_of(*chunk), axis=0, keepdims=True) for chunk in chunks]
            peak_ref[0:1, :] = functools.reduce(jnp.maximum, tops)

        high = jnp.concatenate([high_ref[block][0:1] for block in blocks], axis=1)
        mixed = jnp.concatenate([mixed_ref[block] for block in blocks], axis=1)
        scores = scores_of(*chunks[0])
        seen = jnp.max(scores[0 : min(SHIFT_KEYS, scores.shape[0])], axis=0, keepdims=True)
        new_high = jnp.maximum(jnp.maximum(high, seen), peak_ref[0:1, :])
        shift = new_high * LOG2_SCALE
        mixed = mixed * jnp.exp2((high - new_high) * LOG2_SCALE)
        for index, (start, stop) in enumerate(chunks):
            following = scores_of(*chunks[index + 1]) if index + 1 < len(chunks) else None
            weights = jnp.exp2(scores * LOG2_SCALE - shift).astype(jnp.bfloat16)
            value_t = jnp.concatenate([image[1, c : c + LANES, :] for c in range(start, stop, LANES)], axis=1)
            mixed = mixed + jnp.dot(with_ones(value_t), weights, preferred_element_type=jnp.float32)
            scores = following
        for index, block in enumerate(blocks):
            own = slice(index * rows, (index + 1) * rows)
            high_ref[block] = jnp.broadcast_to(new_high[:, own], high_ref.shape[1:])
            mixed_ref[block] = mixed[:, own]

    def attempt(trial, carry):
        @pl.when((trial == 0) | (redo_ref[0] > 0))
        def _():
            if offset:
                high_ref[...] = before[0][...]
                mixed_ref[...] = before[1][...]
            else:
                high_ref[...] = jnp.full_like(high_ref, LOWEST)
                mixed_ref[...] = jnp.zeros_like(mixed_ref)
            for piece in range(pieces):
                base = (offset + piece) * (block_count + 1)
                count = table_ref[base]

                def pair_step(pair, carry, piece=piece, base=base, count=count):
                    blocks = [table_ref[base + 1 + 2 * pair], table_ref[base + jnp.minimum(2 * pair + 2, count)]]
                    fold_pair(blocks, images[piece], trial > 0)
                    return carry

                lax.fori_loop(0, (count + 1) // 2, pair_step, 0)
            most = functools.reduce(
                jnp.maximum, [mixed_ref[block, HEAD_SIZE : HEAD_SIZE + 1, :] for block in range(block_count)]
            )
            redo_ref[0] = 1 - jnp.min((most <= MOST_SUM).astype(jnp.int32))

        return carry

    lax.fori_loop(0, 2, attempt, 0)

    if last:
        lse_ref[...] = jnp.zeros_like(lse_ref)
        for block in range(block_count):
            total = mixed_ref[block, HEAD_SIZE : HEAD_SIZE + 1, :]
            out_ref[block * HEAD_SIZE : (block + 1) * HEAD_SIZE, :] = (
                mixed_ref[block, 0:HEAD_SIZE, :] / total
            ).astype(jnp.bfloat16)
            lse_ref[block : block + 1, :] = high_ref[block, 0:1, :] * LOG2_SCALE + jnp.log2(total)
        out_ref[block_count * HEAD_SIZE :, :] = lse_pieces(lse_ref[0:block_count, :], block_count)


def cross_part(table, queries, images, key_count, offset, last, before=()):
    tokens, columns = queries[0].shape
    block_count = tokens // MASK_BLOCK_TOKENS
    rows = columns // HEAD_SIZE * MASK_BLOCK_TOKENS
    state = [(block_count, 8, rows), (block_count, MIXED_ROWS, rows)]
    scratch = [pltpu.VMEM((8, 2 * rows), jnp.float32), pltpu.SMEM((1,), jnp.int32)]
    if last:
        out_shape = jax.ShapeDtypeStruct((block_count * HEAD_SIZE + lse_rows(block_count), rows), jnp.bfloat16)
        scratch = [pltpu.VMEM(shape, jnp.float32) for shape in state] + scratch
        scratch = [pltpu.VMEM((-(-block_count // 8) * 8, rows), jnp.float32)] + scratch
    else:
        out_shape = tuple(jax.ShapeDtypeStruct(shape, jnp.float32) for shape in state)
    return pl.pallas_call(
        functools.partial(cross_kernel, key_count, len(images), offset, last, len(queries)),
        out_shape=out_shape,
        in_specs=[SMEM] + [VMEM] * (len(queries) + len(images) + len(before)),
        out_specs=VMEM if last else (VMEM,) * 2,
        scratch_shapes=scratch,
        compiler_params=pltpu.CompilerParams(vmem_limit_bytes=VMEM_LIMIT),
        cost_estimate=MUCH,
        name="cross_last" if last else "cross_first",
    )(table, *queries, *images, *before)


def lse_of(ref, block_count):
    tail = ref[block_count * HEAD_SIZE :, :].astype(jnp.float32)
    return tail[0:block_count] + tail[block_count : 2 * block_count] + tail[2 * block_count : 3 * block_count]


def lse_pieces(lse, block_count):
    first = lse.astype(jnp.bfloat16).astype(jnp.float32)
    second = (lse - first).astype(jnp.bfloat16).astype(jnp.float32)
    pieces = [first, second, lse - first - second]
    spare = lse_rows(block_count) - 3 * block_count
    if spare:
        pieces.append(jnp.zeros((spare, lse.shape[1]), jnp.float32))
    return jnp.concatenate(pieces, axis=0).astype(jnp.bfloat16)


def mixed_block(part_refs, weights, block):
    at = slice(block * HEAD_SIZE, (block + 1) * HEAD_SIZE)
    terms = [weight[block : block + 1, :] * ref[at, :].astype(jnp.float32) for ref, weight in zip(part_refs, weights)]
    return functools.reduce(jnp.add, terms)


def combine_kernel(held, last, *refs):
    if held:
        mixed_ref, lse_ref, part_ref, *out_refs = refs
        block_count = lse_ref.shape[0]
        lse = [lse_ref[...], lse_of(part_ref, block_count)]
    else:
        mixed_ref, part_ref, *out_refs = refs
        block_count = packed_blocks(part_ref.shape[0])
        lse = [lse_of(mixed_ref, block_count), lse_of(part_ref, block_count)]
    highest = functools.reduce(jnp.maximum, lse)
    weights = [jnp.exp2(one - highest) for one in lse]
    total = functools.reduce(jnp.add, weights)
    weights = [one / total for one in weights]
    for block in range(block_count):
        mixed = mixed_block((mixed_ref, part_ref), weights, block)
        if last:
            store_heads(out_refs[0], block, mixed)
        else:
            out_refs[0][block * HEAD_SIZE : (block + 1) * HEAD_SIZE, :] = mixed
    if not last:
        out_refs[1][...] = highest + jnp.log2(total)


def store_heads(out_ref, block, mixed):
    at = slice(block * MASK_BLOCK_TOKENS, (block + 1) * MASK_BLOCK_TOKENS)
    for head in range(out_ref.shape[1] // HEAD_SIZE):
        piece = mixed[:, head * MASK_BLOCK_TOKENS : (head + 1) * MASK_BLOCK_TOKENS]
        out_ref[at, head * HEAD_SIZE : (head + 1) * HEAD_SIZE] = piece.T.astype(jnp.bfloat16)


def combined(so_far, part, shape, last):
    tokens, columns = shape
    held = len(so_far) == 2
    block_count = tokens // MASK_BLOCK_TOKENS
    rows = columns // HEAD_SIZE * MASK_BLOCK_TOKENS
    if last:
        out_shape = jax.ShapeDtypeStruct(shape, jnp.bfloat16)
    else:
        out_shape = (
            jax.ShapeDtypeStruct((block_count * HEAD_SIZE, rows), jnp.float32),
            jax.ShapeDtypeStruct((block_count, rows), jnp.float32),
        )
    return pl.pallas_call(
        functools.partial(combine_kernel, held, last),
        out_shape=out_shape,
        in_specs=[VMEM] * (len(so_far) + 1),
        out_specs=VMEM if last else (VMEM,) * 2,
        compiler_params=pltpu.CompilerParams(vmem_limit_bytes=VMEM_LIMIT),
        cost_estimate=MUCH,
        name="combine_last" if last else "combine",
    )(*so_far, part)


def pair_queries(q_ref, first, blocks):
    return jnp.concatenate(
        [
            stacked_heads(q_ref[block * MASK_BLOCK_TOKENS : (block + 1) * MASK_BLOCK_TOKENS, :])
            for block in range(first, first + blocks)
        ],
        axis=0,
    )


def self_first_kernel(group, q_ref, text_ref, high_ref, mixed_ref, value_ref):
    tokens, columns = q_ref.shape
    rows = columns // HEAD_SIZE * MASK_BLOCK_TOKENS
    value_ref[...] = text_ref[:, HEAD_SIZE:].T
    for index in range(tokens // MASK_BLOCK_TOKENS // group):
        first = index * group
        start, stop = first * MASK_BLOCK_TOKENS, (first + group) * MASK_BLOCK_TOKENS
        scores = nt_dot(text_ref[0:stop, 0:HEAD_SIZE], pair_queries(q_ref, first, group))
        tail = scores[start:, :]
        key_id = lax.broadcasted_iota(jnp.int32, tail.shape, 0)
        column = lax.broadcasted_iota(jnp.int32, tail.shape, 1)
        query_id = column // rows * MASK_BLOCK_TOKENS + column % MASK_BLOCK_TOKENS
        tail = jnp.where(key_id <= query_id, tail, LOWEST)
        scores = jnp.concatenate([scores[:start, :], tail], axis=0) if start else tail
        high = jnp.full((1, group * rows), LOWEST, jnp.float32)
        mixed = jnp.zeros((MIXED_ROWS, group * rows), jnp.float32)
        high, mixed = fold(high, mixed, scores, value_ref[:, 0:stop], True)
        high_ref[index] = jnp.broadcast_to(high, high_ref.shape[1:])
        mixed_ref[index] = mixed


def self_last_kernel(group, pieces, position_ref, q_ref, high_ref, mixed_ref, *refs):
    texts = refs[:pieces]
    out_ref, value_ref, new_high_ref, new_mixed_ref = refs[pieces:]
    rows = q_ref.shape[1] // HEAD_SIZE * MASK_BLOCK_TOKENS
    new_high_ref[...] = high_ref[...]
    new_mixed_ref[...] = mixed_ref[...]
    for piece in range(pieces):

        @pl.when(position_ref[0] >= piece + 1)
        def _(piece=piece):
            value_ref[...] = texts[piece][:, HEAD_SIZE:].T
            for index in range(high_ref.shape[0]):
                scores = nt_dot(texts[piece][:, 0:HEAD_SIZE], pair_queries(q_ref, index * group, group))
                high, mixed = fold(new_high_ref[index, 0:1, :], new_mixed_ref[index], scores, value_ref[...], True)
                new_high_ref[index] = jnp.broadcast_to(high, high_ref.shape[1:])
                new_mixed_ref[index] = mixed

    for index in range(high_ref.shape[0]):
        total = new_mixed_ref[index, HEAD_SIZE : HEAD_SIZE + 1, :]
        mixed = new_mixed_ref[index, 0:HEAD_SIZE, :] / total
        for block in range(group):
            store_heads(out_ref, index * group + block, mixed[:, block * rows : (block + 1) * rows])


def self_first(queries, text):
    tokens, columns = queries.shape
    block_count = tokens // MASK_BLOCK_TOKENS
    group = 1 if block_count % 2 else 2
    width = group * columns // HEAD_SIZE * MASK_BLOCK_TOKENS
    return pl.pallas_call(
        functools.partial(self_first_kernel, group),
        out_shape=(
            jax.ShapeDtypeStruct((block_count // group, 8, width), jnp.float32),
            jax.ShapeDtypeStruct((block_count // group, MIXED_ROWS, width), jnp.float32),
        ),
        in_specs=[VMEM] * 2,
        out_specs=(VMEM,) * 2,
        scratch_shapes=[pltpu.VMEM((HEAD_SIZE, tokens), jnp.bfloat16)],
        compiler_params=pltpu.CompilerParams(vmem_limit_bytes=VMEM_LIMIT),
        cost_estimate=LITTLE,
        name="self_first",
    )(queries, text)


def self_last(position, queries, state, texts):
    tokens, columns = queries.shape
    group = tokens // MASK_BLOCK_TOKENS // state[0].shape[0]
    return pl.pallas_call(
        functools.partial(self_last_kernel, group, len(texts)),
        out_shape=jax.ShapeDtypeStruct((tokens, columns), jnp.bfloat16),
        in_specs=[SMEM] + [VMEM] * (3 + len(texts)),
        out_specs=VMEM,
        scratch_shapes=[pltpu.VMEM((HEAD_SIZE, tokens), jnp.bfloat16)]
        + [pltpu.VMEM(one.shape, jnp.float32) for one in state],
        compiler_params=pltpu.CompilerParams(vmem_limit_bytes=VMEM_LIMIT),
        cost_estimate=LITTLE,
        name="self_last",
    )(position, queries, *state, *texts)


def shifted(value, axis, steps):
    count = lax.axis_size(axis)
    return lax.ppermute(value, axis, [(source, (source + steps) % count) for source in range(count)])


def swapped(value, axis, bits):
    return lax.ppermute(value, axis, [(source, source ^ bits) for source in range(lax.axis_size(axis))])


def moved(value, pairs):
    return lax.ppermute(value, "enc", pairs)


def after(value, earlier):
    return lax.optimization_barrier((value, earlier))[0]


def per_device(
    self_queries, text_kv, cross_queries, image_kv, block_images, image_owner
):
    rows = self_queries.shape[0]
    key_count = image_kv.shape[2]
    cycle = lax.axis_size("blk")
    ring = lax.axis_size("enc")
    position = lax.axis_index("blk").astype(jnp.int32)[None]

    images = [prepare(image_kv[0])]
    for _ in range(1, cycle):
        images.append(shifted(images[-1], "blk", 1))
    if ring == 4:
        queries = {step: [swapped(cross_queries, "enc", step)] for step in (2, 1)}
    else:
        queries = {step: [shifted(cross_queries, "enc", ring - step)] for step in range(1, ring)}
    queries[0] = [cross_queries]
    table = seen_table(position, block_images, image_owner)

    text = text_kv.reshape(rows, 2 * HEAD_SIZE)
    texts = []
    onward = after(text, images[-1])
    for _ in range(1, cycle):
        onward = lax.ppermute(onward, "blk", [(source, source + 1) for source in range(cycle - 1)])
        texts.append(onward)

    latest = [None]

    def in_turn(arrays):
        return arrays if latest[0] is None else [after(one, latest[0]) for one in arrays]

    def begun(step):
        latest[0] = cross_part(table, in_turn(queries[step]), images[:1], key_count, 0, False)
        return latest[0]

    def finished(step, state=None):
        used = images if state is None else images[1:]
        before = () if state is None else state
        offset = 0 if state is None else 1
        latest[0] = cross_part(table, in_turn(queries[step]), used, key_count, offset, True, before)
        return latest[0]

    split = cycle > 1
    self_state = latest[0] = self_first(self_queries, text)
    own = begun(0) if split else None
    if ring == 4:
        middle = moved(in_turn([cross_queries])[0], [(1, 2), (2, 1)])
        ends = moved(queries[2][0], [(2, 3), (1, 0)])
        queries[3] = [middle, ends]
    steps = [2, 3, 1] if ring == 4 else list(range(1, ring))
    states = {step: begun(step) for step in steps[:1]} if split else {}
    received = []
    for step in steps:
        part = finished(step, states.get(step))
        received.append(swapped(part, "enc", step) if ring == 4 else shifted(part, "enc", step))
    own_part = finished(0, own)
    self_out = latest[0] = self_last(position, in_turn([self_queries])[0], self_state, texts)
    so_far = in_turn([own_part])
    for index, part in enumerate(received):
        so_far = combined(so_far, part, cross_queries.shape, index + 1 == len(received))
    return (self_out, so_far)


def solution(mesh):
    placed = (
        P("blk", ("tp", "enc")),
        P("blk", None, "tp"),
        P("blk", ("tp", "enc")),
        P("blk", None, "enc", "tp"),
        P("blk", None),
        P(),
    )
    return jax.shard_map(
        per_device,
        mesh=mesh,
        in_specs=placed,
        out_specs=(P("blk", ("tp", "enc")), P("blk", ("tp", "enc"))),
        check_vma=False,
    )
```

```python
import functools
import math

import jax
import jax.numpy as jnp
from jax import lax
from jax.experimental import pallas as pl
from jax.experimental.pallas import tpu as pltpu
from jax.sharding import PartitionSpec as P

HEAD_SIZE = 128
MASK_BLOCK_TOKENS = 128
LANES = 128
LOWEST = -1e30
MIXED_ROWS = HEAD_SIZE + 16
SHIFT_KEYS = 256
MOST_SUM = 2.0**100
LOG2_SCALE = math.log2(math.e) / math.sqrt(HEAD_SIZE)
VMEM_LIMIT = 48 * 1024 * 1024

LITTLE = pl.CostEstimate(flops=0, bytes_accessed=1024, transcendentals=0)
MUCH = pl.CostEstimate(flops=2_000_000_000, bytes_accessed=1024, transcendentals=0)

VMEM = pl.BlockSpec(memory_space=pltpu.VMEM)
SMEM = pl.BlockSpec(memory_space=pltpu.SMEM)


def padded(count):
    return -(-count // LANES) * LANES


def nt_dot(a, b):
    return lax.dot_general(a, b, (((1,), (1,)), ((), ())), preferred_element_type=jnp.float32)


def at_block(block, size=MASK_BLOCK_TOKENS):
    return pl.ds(pl.multiple_of(block * size, size), size)


def stacked_heads(rows):
    heads = rows.shape[1] // HEAD_SIZE
    return jnp.concatenate([rows[:, h * HEAD_SIZE : (h + 1) * HEAD_SIZE] for h in range(heads)], axis=0)


def with_ones(value_t):
    shape = (MIXED_ROWS - HEAD_SIZE, value_t.shape[1])
    ones = (lax.broadcasted_iota(jnp.int32, shape, 0) == 0).astype(jnp.bfloat16)
    return jnp.concatenate([value_t, ones], axis=0)


def fold(high, mixed, scores, value_t, exact):
    seen = scores if exact else scores[0 : min(SHIFT_KEYS, scores.shape[0]), :]
    new_high = jnp.maximum(high, jnp.max(seen, axis=0, keepdims=True))
    weights = jnp.exp2(scores * LOG2_SCALE - new_high * LOG2_SCALE).astype(jnp.bfloat16)
    fading = jnp.exp2((high - new_high) * LOG2_SCALE)
    mixed = mixed * fading + jnp.dot(with_ones(value_t), weights, preferred_element_type=jnp.float32)
    return new_high, mixed


def prepare_kernel(kv_ref, out_ref):
    count = kv_ref.shape[1]
    whole = count // LANES * LANES
    rest = count - whole
    out_ref[0, 0:whole, :] = kv_ref[0, 0:whole, :]
    for at in range(0, whole, LANES):
        out_ref[1, at : at + LANES, :] = kv_ref[1, at : at + LANES, :].T
    if rest:
        empty = jnp.zeros((LANES - rest, HEAD_SIZE), jnp.float32)
        tail_key = jnp.concatenate([kv_ref[0, whole:count, :].astype(jnp.float32), empty], axis=0)
        tail_value = jnp.concatenate([kv_ref[1, whole:count, :].astype(jnp.float32), empty], axis=0)
        out_ref[0, whole : whole + LANES, :] = tail_key.astype(jnp.bfloat16)
        out_ref[1, whole : whole + LANES, :] = tail_value.T.astype(jnp.bfloat16)


def prepare(kv):
    return pl.pallas_call(
        prepare_kernel,
        out_shape=jax.ShapeDtypeStruct((2, padded(kv.shape[1]), HEAD_SIZE), jnp.bfloat16),
        in_specs=[VMEM],
        out_specs=VMEM,
        compiler_params=pltpu.CompilerParams(vmem_limit_bytes=VMEM_LIMIT),
        cost_estimate=LITTLE,
        name="prepare",
    )(kv)


def lse_rows(block_count):
    return -(-3 * block_count // 16) * 16


def packed_blocks(rows):
    return next(count for count in range(1, rows) if count * HEAD_SIZE + lse_rows(count) == rows)


def table_kernel(position_ref, images_ref, owner_ref, table_ref):
    block_count, slots = images_ref.shape
    for piece in range(slots):
        slot = lax.rem(position_ref[0] + (slots - piece), slots)
        base = piece * (block_count + 1)
        count = jnp.int32(0)
        for block in range(block_count):
            table_ref[base + 1 + block] = jnp.int32(0)
        for block in range(block_count):
            seen = lax.fori_loop(
                0,
                slots,
                lambda image, sum, block=block, slot=slot: sum
                + jnp.where(owner_ref[image] == slot, images_ref[block, image], 0),
                jnp.int32(0),
            )

            @pl.when(seen > 0)
            def _(base=base, block=block, count=count):
                table_ref[base + 1 + count] = jnp.int32(block)

            count = count + jnp.where(seen > 0, 1, 0)
        table_ref[base] = count
    table_ref[slots * (block_count + 1)] = position_ref[1]


def seen_table(position, block_images, image_owner):
    block_count, slots = block_images.shape
    return pl.pallas_call(
        table_kernel,
        out_shape=jax.ShapeDtypeStruct((slots * (block_count + 1) + 1,), jnp.int32),
        in_specs=[SMEM] * 3,
        out_specs=SMEM,
        name="seen_table",
    )(position, block_images, image_owner)


def chunks_of(width):
    half = width // LANES // 2 * LANES
    return [(0, half), (half, width)] if half else [(0, width)]


def cross_kernel(key_count, pieces, offset, last, parts, table_ref, *refs):
    q_refs, images, refs = refs[:parts], refs[parts : parts + pieces], refs[parts + pieces :]
    if offset:
        before, refs = refs[:2], refs[2:]
    if last:
        out_ref, lse_ref, high_ref, mixed_ref, peak_ref, redo_ref = refs
    else:
        high_ref, mixed_ref, peak_ref, redo_ref = refs
    block_count = q_refs[0].shape[0] // MASK_BLOCK_TOKENS
    rows = q_refs[0].shape[1] // HEAD_SIZE * MASK_BLOCK_TOKENS
    peak_ref[...] = jnp.full_like(peak_ref, LOWEST)
    redo_ref[0] = jnp.int32(0)

    def fold_pair(blocks, image, exact):
        width = image.shape[1]
        queries = [q_refs[0][at_block(block), :] for block in blocks]
        if parts > 1:
            first = table_ref[table_ref.shape[0] - 1] > 0
            queries = [jnp.where(first, one, q_refs[1][at_block(block), :]) for one, block in zip(queries, blocks)]
        queries = jnp.concatenate([stacked_heads(one) for one in queries], axis=0)
        chunks = chunks_of(width)

        def scores_of(start, stop):
            scores = nt_dot(image[0, start:stop, :], queries)
            if stop > key_count:
                body = stop - start - LANES
                tail = scores[body:, :]
                key_id = start + body + lax.broadcasted_iota(jnp.int32, tail.shape, 0)
                tail = jnp.where(key_id < key_count, tail, LOWEST)
                scores = jnp.concatenate([scores[:body, :], tail], axis=0) if body else tail
            return scores

        @pl.when(exact)
        def _():
            tops = [jnp.max(scores_of(*chunk), axis=0, keepdims=True) for chunk in chunks]
            peak_ref[0:1, :] = functools.reduce(jnp.maximum, tops)

        high = jnp.concatenate([high_ref[block][0:1] for block in blocks], axis=1)
        mixed = jnp.concatenate([mixed_ref[block] for block in blocks], axis=1)
        scores = scores_of(*chunks[0])
        seen = jnp.max(scores[0 : min(SHIFT_KEYS, scores.shape[0])], axis=0, keepdims=True)
        new_high = jnp.maximum(jnp.maximum(high, seen), peak_ref[0:1, :])
        shift = new_high * LOG2_SCALE
        mixed = mixed * jnp.exp2((high - new_high) * LOG2_SCALE)
        for index, (start, stop) in enumerate(chunks):
            following = scores_of(*chunks[index + 1]) if index + 1 < len(chunks) else None
            weights = jnp.exp2(scores * LOG2_SCALE - shift).astype(jnp.bfloat16)
            value_t = jnp.concatenate([image[1, c : c + LANES, :] for c in range(start, stop, LANES)], axis=1)
            mixed = mixed + jnp.dot(with_ones(value_t), weights, preferred_element_type=jnp.float32)
            scores = following
        for index, block in enumerate(blocks):
            own = slice(index * rows, (index + 1) * rows)
            high_ref[block] = jnp.broadcast_to(new_high[:, own], high_ref.shape[1:])
            mixed_ref[block] = mixed[:, own]

    def attempt(trial, carry):
        @pl.when((trial == 0) | (redo_ref[0] > 0))
        def _():
            if offset:
                high_ref[...] = before[0][...]
                mixed_ref[...] = before[1][...]
            else:
                high_ref[...] = jnp.full_like(high_ref, LOWEST)
                mixed_ref[...] = jnp.zeros_like(mixed_ref)
            for piece in range(pieces):
                base = (offset + piece) * (block_count + 1)
                count = table_ref[base]

                def pair_step(pair, carry, piece=piece, base=base, count=count):
                    blocks = [table_ref[base + 1 + 2 * pair], table_ref[base + jnp.minimum(2 * pair + 2, count)]]
                    fold_pair(blocks, images[piece], trial > 0)
                    return carry

                lax.fori_loop(0, (count + 1) // 2, pair_step, 0)
            most = functools.reduce(
                jnp.maximum, [mixed_ref[block, HEAD_SIZE : HEAD_SIZE + 1, :] for block in range(block_count)]
            )
            redo_ref[0] = 1 - jnp.min((most <= MOST_SUM).astype(jnp.int32))

        return carry

    lax.fori_loop(0, 2, attempt, 0)

    if last:
        lse_ref[...] = jnp.zeros_like(lse_ref)
        for block in range(block_count):
            total = mixed_ref[block, HEAD_SIZE : HEAD_SIZE + 1, :]
            out_ref[block * HEAD_SIZE : (block + 1) * HEAD_SIZE, :] = (
                mixed_ref[block, 0:HEAD_SIZE, :] / total
            ).astype(jnp.bfloat16)
            lse_ref[block : block + 1, :] = high_ref[block, 0:1, :] * LOG2_SCALE + jnp.log2(total)
        out_ref[block_count * HEAD_SIZE :, :] = lse_pieces(lse_ref[0:block_count, :], block_count)


def cross_part(table, queries, images, key_count, offset, last, before=()):
    tokens, columns = queries[0].shape
    block_count = tokens // MASK_BLOCK_TOKENS
    rows = columns // HEAD_SIZE * MASK_BLOCK_TOKENS
    state = [(block_count, 8, rows), (block_count, MIXED_ROWS, rows)]
    scratch = [pltpu.VMEM((8, 2 * rows), jnp.float32), pltpu.SMEM((1,), jnp.int32)]
    if last:
        out_shape = jax.ShapeDtypeStruct((block_count * HEAD_SIZE + lse_rows(block_count), rows), jnp.bfloat16)
        scratch = [pltpu.VMEM(shape, jnp.float32) for shape in state] + scratch
        scratch = [pltpu.VMEM((-(-block_count // 8) * 8, rows), jnp.float32)] + scratch
    else:
        out_shape = tuple(jax.ShapeDtypeStruct(shape, jnp.float32) for shape in state)
    return pl.pallas_call(
        functools.partial(cross_kernel, key_count, len(images), offset, last, len(queries)),
        out_shape=out_shape,
        in_specs=[SMEM] + [VMEM] * (len(queries) + len(images) + len(before)),
        out_specs=VMEM if last else (VMEM,) * 2,
        scratch_shapes=scratch,
        compiler_params=pltpu.CompilerParams(vmem_limit_bytes=VMEM_LIMIT),
        cost_estimate=MUCH,
        name="cross_last" if last else "cross_first",
    )(table, *queries, *images, *before)


def lse_of(ref, block_count):
    tail = ref[block_count * HEAD_SIZE :, :].astype(jnp.float32)
    return tail[0:block_count] + tail[block_count : 2 * block_count] + tail[2 * block_count : 3 * block_count]


def lse_pieces(lse, block_count):
    first = lse.astype(jnp.bfloat16).astype(jnp.float32)
    second = (lse - first).astype(jnp.bfloat16).astype(jnp.float32)
    pieces = [first, second, lse - first - second]
    spare = lse_rows(block_count) - 3 * block_count
    if spare:
        pieces.append(jnp.zeros((spare, lse.shape[1]), jnp.float32))
    return jnp.concatenate(pieces, axis=0).astype(jnp.bfloat16)


def mixed_block(part_refs, weights, block):
    at = slice(block * HEAD_SIZE, (block + 1) * HEAD_SIZE)
    terms = [weight[block : block + 1, :] * ref[at, :].astype(jnp.float32) for ref, weight in zip(part_refs, weights)]
    return functools.reduce(jnp.add, terms)


def combine_kernel(held, last, *refs):
    if held:
        mixed_ref, lse_ref, part_ref, *out_refs = refs
        block_count = lse_ref.shape[0]
        lse = [lse_ref[...], lse_of(part_ref, block_count)]
    else:
        mixed_ref, part_ref, *out_refs = refs
        block_count = packed_blocks(part_ref.shape[0])
        lse = [lse_of(mixed_ref, block_count), lse_of(part_ref, block_count)]
    highest = functools.reduce(jnp.maximum, lse)
    weights = [jnp.exp2(one - highest) for one in lse]
    total = functools.reduce(jnp.add, weights)
    weights = [one / total for one in weights]
    for block in range(block_count):
        mixed = mixed_block((mixed_ref, part_ref), weights, block)
        if last:
            store_heads(out_refs[0], block, mixed)
        else:
            out_refs[0][block * HEAD_SIZE : (block + 1) * HEAD_SIZE, :] = mixed
    if not last:
        out_refs[1][...] = highest + jnp.log2(total)


def store_heads(out_ref, block, mixed):
    at = slice(block * MASK_BLOCK_TOKENS, (block + 1) * MASK_BLOCK_TOKENS)
    for head in range(out_ref.shape[1] // HEAD_SIZE):
        piece = mixed[:, head * MASK_BLOCK_TOKENS : (head + 1) * MASK_BLOCK_TOKENS]
        out_ref[at, head * HEAD_SIZE : (head + 1) * HEAD_SIZE] = piece.T.astype(jnp.bfloat16)


def combined(so_far, part, shape, last):
    tokens, columns = shape
    held = len(so_far) == 2
    block_count = tokens // MASK_BLOCK_TOKENS
    rows = columns // HEAD_SIZE * MASK_BLOCK_TOKENS
    if last:
        out_shape = jax.ShapeDtypeStruct(shape, jnp.bfloat16)
    else:
        out_shape = (
            jax.ShapeDtypeStruct((block_count * HEAD_SIZE, rows), jnp.float32),
            jax.ShapeDtypeStruct((block_count, rows), jnp.float32),
        )
    return pl.pallas_call(
        functools.partial(combine_kernel, held, last),
        out_shape=out_shape,
        in_specs=[VMEM] * (len(so_far) + 1),
        out_specs=VMEM if last else (VMEM,) * 2,
        compiler_params=pltpu.CompilerParams(vmem_limit_bytes=VMEM_LIMIT),
        cost_estimate=MUCH,
        name="combine_last" if last else "combine",
    )(*so_far, part)


def pair_queries(q_ref, first, blocks):
    return jnp.concatenate(
        [
            stacked_heads(q_ref[block * MASK_BLOCK_TOKENS : (block + 1) * MASK_BLOCK_TOKENS, :])
            for block in range(first, first + blocks)
        ],
        axis=0,
    )


def self_first_kernel(group, q_ref, text_ref, high_ref, mixed_ref, value_ref):
    tokens, columns = q_ref.shape
    rows = columns // HEAD_SIZE * MASK_BLOCK_TOKENS
    value_ref[...] = text_ref[:, HEAD_SIZE:].T
    for index in range(tokens // MASK_BLOCK_TOKENS // group):
        first = index * group
        start, stop = first * MASK_BLOCK_TOKENS, (first + group) * MASK_BLOCK_TOKENS
        scores = nt_dot(text_ref[0:stop, 0:HEAD_SIZE], pair_queries(q_ref, first, group))
        tail = scores[start:, :]
        key_id = lax.broadcasted_iota(jnp.int32, tail.shape, 0)
        column = lax.broadcasted_iota(jnp.int32, tail.shape, 1)
        query_id = column // rows * MASK_BLOCK_TOKENS + column % MASK_BLOCK_TOKENS
        tail = jnp.where(key_id <= query_id, tail, LOWEST)
        scores = jnp.concatenate([scores[:start, :], tail], axis=0) if start else tail
        high = jnp.full((1, group * rows), LOWEST, jnp.float32)
        mixed = jnp.zeros((MIXED_ROWS, group * rows), jnp.float32)
        high, mixed = fold(high, mixed, scores, value_ref[:, 0:stop], True)
        high_ref[index] = jnp.broadcast_to(high, high_ref.shape[1:])
        mixed_ref[index] = mixed


def self_last_kernel(group, pieces, position_ref, q_ref, high_ref, mixed_ref, *refs):
    texts = refs[:pieces]
    out_ref, value_ref, new_high_ref, new_mixed_ref = refs[pieces:]
    rows = q_ref.shape[1] // HEAD_SIZE * MASK_BLOCK_TOKENS
    new_high_ref[...] = high_ref[...]
    new_mixed_ref[...] = mixed_ref[...]
    for piece in range(pieces):

        @pl.when(position_ref[0] >= piece + 1)
        def _(piece=piece):
            value_ref[...] = texts[piece][:, HEAD_SIZE:].T
            for index in range(high_ref.shape[0]):
                scores = nt_dot(texts[piece][:, 0:HEAD_SIZE], pair_queries(q_ref, index * group, group))
                high, mixed = fold(new_high_ref[index, 0:1, :], new_mixed_ref[index], scores, value_ref[...], True)
                new_high_ref[index] = jnp.broadcast_to(high, high_ref.shape[1:])
                new_mixed_ref[index] = mixed

    for index in range(high_ref.shape[0]):
        total = new_mixed_ref[index, HEAD_SIZE : HEAD_SIZE + 1, :]
        mixed = new_mixed_ref[index, 0:HEAD_SIZE, :] / total
        for block in range(group):
            store_heads(out_ref, index * group + block, mixed[:, block * rows : (block + 1) * rows])


def self_first(queries, text):
    tokens, columns = queries.shape
    block_count = tokens // MASK_BLOCK_TOKENS
    group = 1 if block_count % 2 else 2
    width = group * columns // HEAD_SIZE * MASK_BLOCK_TOKENS
    return pl.pallas_call(
        functools.partial(self_first_kernel, group),
        out_shape=(
            jax.ShapeDtypeStruct((block_count // group, 8, width), jnp.float32),
            jax.ShapeDtypeStruct((block_count // group, MIXED_ROWS, width), jnp.float32),
        ),
        in_specs=[VMEM] * 2,
        out_specs=(VMEM,) * 2,
        scratch_shapes=[pltpu.VMEM((HEAD_SIZE, tokens), jnp.bfloat16)],
        compiler_params=pltpu.CompilerParams(vmem_limit_bytes=VMEM_LIMIT),
        cost_estimate=LITTLE,
        name="self_first",
    )(queries, text)


def self_last(position, queries, state, texts):
    tokens, columns = queries.shape
    group = tokens // MASK_BLOCK_TOKENS // state[0].shape[0]
    return pl.pallas_call(
        functools.partial(self_last_kernel, group, len(texts)),
        out_shape=jax.ShapeDtypeStruct((tokens, columns), jnp.bfloat16),
        in_specs=[SMEM] + [VMEM] * (3 + len(texts)),
        out_specs=VMEM,
        scratch_shapes=[pltpu.VMEM((HEAD_SIZE, tokens), jnp.bfloat16)]
        + [pltpu.VMEM(one.shape, jnp.float32) for one in state],
        compiler_params=pltpu.CompilerParams(vmem_limit_bytes=VMEM_LIMIT),
        cost_estimate=LITTLE,
        name="self_last",
    )(position, queries, *state, *texts)


def shifted(value, axis, steps):
    count = lax.axis_size(axis)
    return lax.ppermute(value, axis, [(source, (source + steps) % count) for source in range(count)])


def swapped(value, axis, bits):
    return lax.ppermute(value, axis, [(source, source ^ bits) for source in range(lax.axis_size(axis))])


def after(value, earlier):
    return lax.optimization_barrier((value, earlier))[0]


def per_device(
    self_queries, text_kv, cross_queries, image_kv, block_images, image_owner
):
    rows = self_queries.shape[0]
    key_count = image_kv.shape[2]
    cycle = lax.axis_size("blk")
    ring = lax.axis_size("enc")
    place = lax.axis_index("enc")
    inside = (place > 0) & (place < ring - 1)
    position = jnp.stack([lax.axis_index("blk"), inside]).astype(jnp.int32)

    images = [prepare(image_kv[0])]
    for _ in range(1, cycle):
        images.append(shifted(images[-1], "blk", 1))
    if ring == 4:
        queries = {step: [swapped(cross_queries, "enc", step)] for step in (2, 1)}
        middle = lax.ppermute(cross_queries, "enc", [(0, 0), (1, 2), (2, 1), (3, 3)])
        queries[3] = [middle, swapped(queries[2][0], "enc", 1)]
    else:
        queries = {step: [shifted(cross_queries, "enc", ring - step)] for step in range(1, ring)}
    queries[0] = [cross_queries]
    table = seen_table(position, block_images, image_owner)

    text = text_kv.reshape(rows, 2 * HEAD_SIZE)
    texts = []
    onward = after(text, images[-1])
    for _ in range(1, cycle):
        onward = shifted(onward, "blk", 1)
        texts.append(onward)

    latest = [None]

    def in_turn(arrays):
        return arrays if latest[0] is None else [after(one, latest[0]) for one in arrays]

    def begun(step):
        latest[0] = cross_part(table, in_turn(queries[step]), images[:1], key_count, 0, False)
        return latest[0]

    def finished(step, state=None):
        used = images if state is None else images[1:]
        before = () if state is None else state
        offset = 0 if state is None else 1
        latest[0] = cross_part(table, in_turn(queries[step]), used, key_count, offset, True, before)
        return latest[0]

    split = cycle > 1
    self_state = latest[0] = self_first(self_queries, text)
    own = begun(0) if split else None
    steps = [2, 3, 1] if ring == 4 else list(range(1, ring))
    states = {step: begun(step) for step in steps[:1]} if split else {}
    received = []
    for step in steps:
        part = finished(step, states.get(step))
        received.append(swapped(part, "enc", step) if ring == 4 else shifted(part, "enc", step))
    own_part = finished(0, own)
    self_out = latest[0] = self_last(position, in_turn([self_queries])[0], self_state, texts)
    so_far = in_turn([own_part])
    for index, part in enumerate(received):
        so_far = combined(so_far, part, cross_queries.shape, index + 1 == len(received))
    return (self_out, so_far)


def solution(mesh):
    placed = (
        P("blk", ("tp", "enc")),
        P("blk", None, "tp"),
        P("blk", ("tp", "enc")),
        P("blk", None, "enc", "tp"),
        P("blk", None),
        P(),
    )
    return jax.shard_map(
        per_device,
        mesh=mesh,
        in_specs=placed,
        out_specs=(P("blk", ("tp", "enc")), P("blk", ("tp", "enc"))),
        check_vma=False,
    )
```

```python
import functools
import math

import jax
import jax.numpy as jnp
from jax import lax
from jax.experimental import pallas as pl
from jax.experimental.pallas import tpu as pltpu
from jax.sharding import PartitionSpec as P

HEAD_SIZE = 128
MASK_BLOCK_TOKENS = 128
LANES = 128
LOWEST = -1e30
MIXED_ROWS = HEAD_SIZE + 16
SHIFT_KEYS = 256
MOST_SUM = 2.0**100
LOG2_SCALE = math.log2(math.e) / math.sqrt(HEAD_SIZE)
VMEM_LIMIT = 48 * 1024 * 1024

LITTLE = pl.CostEstimate(flops=0, bytes_accessed=1024, transcendentals=0)
MUCH = pl.CostEstimate(flops=2_000_000_000, bytes_accessed=1024, transcendentals=0)

VMEM = pl.BlockSpec(memory_space=pltpu.VMEM)
SMEM = pl.BlockSpec(memory_space=pltpu.SMEM)


def padded(count):
    return -(-count // LANES) * LANES


def nt_dot(a, b):
    return lax.dot_general(a, b, (((1,), (1,)), ((), ())), preferred_element_type=jnp.float32)


def at_block(block, size=MASK_BLOCK_TOKENS):
    return pl.ds(pl.multiple_of(block * size, size), size)


def stacked_heads(rows):
    heads = rows.shape[1] // HEAD_SIZE
    return jnp.concatenate([rows[:, h * HEAD_SIZE : (h + 1) * HEAD_SIZE] for h in range(heads)], axis=0)


def with_ones(value_t):
    shape = (MIXED_ROWS - HEAD_SIZE, value_t.shape[1])
    ones = (lax.broadcasted_iota(jnp.int32, shape, 0) == 0).astype(jnp.bfloat16)
    return jnp.concatenate([value_t, ones], axis=0)


def fold(high, mixed, scores, value_t, exact):
    seen = scores if exact else scores[0 : min(SHIFT_KEYS, scores.shape[0]), :]
    new_high = jnp.maximum(high, jnp.max(seen, axis=0, keepdims=True))
    weights = jnp.exp2(scores * LOG2_SCALE - new_high * LOG2_SCALE).astype(jnp.bfloat16)
    fading = jnp.exp2((high - new_high) * LOG2_SCALE)
    mixed = mixed * fading + jnp.dot(with_ones(value_t), weights, preferred_element_type=jnp.float32)
    return new_high, mixed


def prepare_kernel(kv_ref, out_ref):
    count = kv_ref.shape[1]
    whole = count // LANES * LANES
    rest = count - whole
    out_ref[0, 0:whole, :] = kv_ref[0, 0:whole, :]
    for at in range(0, whole, LANES):
        out_ref[1, at : at + LANES, :] = kv_ref[1, at : at + LANES, :].T
    if rest:
        empty = jnp.zeros((LANES - rest, HEAD_SIZE), jnp.float32)
        tail_key = jnp.concatenate([kv_ref[0, whole:count, :].astype(jnp.float32), empty], axis=0)
        tail_value = jnp.concatenate([kv_ref[1, whole:count, :].astype(jnp.float32), empty], axis=0)
        out_ref[0, whole : whole + LANES, :] = tail_key.astype(jnp.bfloat16)
        out_ref[1, whole : whole + LANES, :] = tail_value.T.astype(jnp.bfloat16)


def prepare(kv):
    return pl.pallas_call(
        prepare_kernel,
        out_shape=jax.ShapeDtypeStruct((2, padded(kv.shape[1]), HEAD_SIZE), jnp.bfloat16),
        in_specs=[VMEM],
        out_specs=VMEM,
        compiler_params=pltpu.CompilerParams(vmem_limit_bytes=VMEM_LIMIT),
        cost_estimate=LITTLE,
        name="prepare",
    )(kv)


def lse_rows(block_count):
    return -(-3 * block_count // 16) * 16


def packed_blocks(rows):
    return next(count for count in range(1, rows) if count * HEAD_SIZE + lse_rows(count) == rows)


def table_kernel(position_ref, images_ref, owner_ref, table_ref):
    block_count, slots = images_ref.shape
    for piece in range(slots):
        slot = lax.rem(position_ref[0] + (slots - piece), slots)
        base = piece * (block_count + 1)
        count = jnp.int32(0)
        for block in range(block_count):
            table_ref[base + 1 + block] = jnp.int32(0)
        for block in range(block_count):
            seen = lax.fori_loop(
                0,
                slots,
                lambda image, sum, block=block, slot=slot: sum
                + jnp.where(owner_ref[image] == slot, images_ref[block, image], 0),
                jnp.int32(0),
            )

            @pl.when(seen > 0)
            def _(base=base, block=block, count=count):
                table_ref[base + 1 + count] = jnp.int32(block)

            count = count + jnp.where(seen > 0, 1, 0)
        table_ref[base] = count
    table_ref[slots * (block_count + 1)] = position_ref[1]


def seen_table(position, block_images, image_owner):
    block_count, slots = block_images.shape
    return pl.pallas_call(
        table_kernel,
        out_shape=jax.ShapeDtypeStruct((slots * (block_count + 1) + 1,), jnp.int32),
        in_specs=[SMEM] * 3,
        out_specs=SMEM,
        name="seen_table",
    )(position, block_images, image_owner)


def chunks_of(width):
    half = width // LANES // 2 * LANES
    return [(0, half), (half, width)] if half else [(0, width)]


def cross_kernel(key_count, pieces, offset, last, parts, table_ref, *refs):
    q_refs, images, refs = refs[:parts], refs[parts : parts + pieces], refs[parts + pieces :]
    if offset:
        before, refs = refs[:2], refs[2:]
    if last:
        out_ref, lse_ref, high_ref, mixed_ref, peak_ref, redo_ref = refs
    else:
        high_ref, mixed_ref, peak_ref, redo_ref = refs
    block_count = q_refs[0].shape[0] // MASK_BLOCK_TOKENS
    rows = q_refs[0].shape[1] // HEAD_SIZE * MASK_BLOCK_TOKENS
    peak_ref[...] = jnp.full_like(peak_ref, LOWEST)
    redo_ref[0] = jnp.int32(0)

    def fold_pair(blocks, image, exact, held):
        width = image.shape[1]
        queries = [q_refs[0][at_block(block), :] for block in blocks]
        if parts > 1:
            first = table_ref[table_ref.shape[0] - 1] > 0
            queries = [jnp.where(first, one, q_refs[1][at_block(block), :]) for one, block in zip(queries, blocks)]
        queries = jnp.concatenate([stacked_heads(one) for one in queries], axis=0)
        chunks = chunks_of(width)

        def scores_of(start, stop):
            scores = nt_dot(image[0, start:stop, :], queries)
            if stop > key_count:
                body = stop - start - LANES
                tail = scores[body:, :]
                key_id = start + body + lax.broadcasted_iota(jnp.int32, tail.shape, 0)
                tail = jnp.where(key_id < key_count, tail, LOWEST)
                scores = jnp.concatenate([scores[:body, :], tail], axis=0) if body else tail
            return scores

        @pl.when(exact)
        def _():
            tops = [jnp.max(scores_of(*chunk), axis=0, keepdims=True) for chunk in chunks]
            peak_ref[0:1, :] = functools.reduce(jnp.maximum, tops)

        if held is None:
            high = jnp.full((1, 2 * rows), LOWEST, jnp.float32)
            mixed = jnp.zeros((MIXED_ROWS, 2 * rows), jnp.float32)
        else:
            high = jnp.concatenate([held[0][block][0:1] for block in blocks], axis=1)
            mixed = jnp.concatenate([held[1][block] for block in blocks], axis=1)
        scores = scores_of(*chunks[0])
        seen = jnp.max(scores[0 : min(SHIFT_KEYS, scores.shape[0])], axis=0, keepdims=True)
        new_high = jnp.maximum(jnp.maximum(high, seen), peak_ref[0:1, :])
        shift = new_high * LOG2_SCALE
        mixed = mixed * jnp.exp2((high - new_high) * LOG2_SCALE)
        for index, (start, stop) in enumerate(chunks):
            following = scores_of(*chunks[index + 1]) if index + 1 < len(chunks) else None
            weights = jnp.exp2(scores * LOG2_SCALE - shift).astype(jnp.bfloat16)
            value_t = jnp.concatenate([image[1, c : c + LANES, :] for c in range(start, stop, LANES)], axis=1)
            mixed = mixed + jnp.dot(with_ones(value_t), weights, preferred_element_type=jnp.float32)
            scores = following
        for index, block in enumerate(blocks):
            own = slice(index * rows, (index + 1) * rows)
            high_ref[block] = jnp.broadcast_to(new_high[:, own], high_ref.shape[1:])
            mixed_ref[block] = mixed[:, own]

    def finish():
        for block in range(block_count):
            total = mixed_ref[block, HEAD_SIZE : HEAD_SIZE + 1, :]
            out_ref[block * HEAD_SIZE : (block + 1) * HEAD_SIZE, :] = (
                mixed_ref[block, 0:HEAD_SIZE, :] * (1.0 / total)
            ).astype(jnp.bfloat16)
            lse_ref[block : block + 1, :] = high_ref[block, 0:1, :] * LOG2_SCALE + jnp.log2(total)
        out_ref[block_count * HEAD_SIZE :, :] = lse_pieces(lse_ref[0:block_count, :], block_count)

    def attempt(trial, carry):
        @pl.when((trial == 0) | (redo_ref[0] > 0))
        def _():
            for piece in range(pieces):
                base = (offset + piece) * (block_count + 1)
                count = table_ref[base]
                if piece == 0:
                    held = before if offset else None
                    for block in range(block_count):
                        seen = functools.reduce(
                            jnp.logical_or,
                            [(count > index) & (table_ref[base + 1 + index] == block) for index in range(block_count)],
                        )

                        @pl.when(jnp.logical_not(seen))
                        def _(block=block):
                            if held is None:
                                high_ref[block] = jnp.full(high_ref.shape[1:], LOWEST, jnp.float32)
                                mixed_ref[block] = jnp.zeros(mixed_ref.shape[1:], jnp.float32)
                            else:
                                high_ref[block] = held[0][block]
                                mixed_ref[block] = held[1][block]

                else:
                    held = (high_ref, mixed_ref)

                def pair_step(pair, carry, piece=piece, base=base, count=count, held=held):
                    blocks = [table_ref[base + 1 + 2 * pair], table_ref[base + jnp.minimum(2 * pair + 2, count)]]
                    fold_pair(blocks, images[piece], trial > 0, held)
                    return carry

                lax.fori_loop(0, (count + 1) // 2, pair_step, 0)
            most = functools.reduce(
                jnp.maximum, [mixed_ref[block, HEAD_SIZE : HEAD_SIZE + 1, :] for block in range(block_count)]
            )
            if last:
                finish()
            redo_ref[0] = 1 - jnp.min((most <= MOST_SUM).astype(jnp.int32))

        return carry

    lax.fori_loop(0, 2, attempt, 0)


def cross_part(table, queries, images, key_count, offset, last, before=()):
    tokens, columns = queries[0].shape
    block_count = tokens // MASK_BLOCK_TOKENS
    rows = columns // HEAD_SIZE * MASK_BLOCK_TOKENS
    state = [(block_count, 8, rows), (block_count, MIXED_ROWS, rows)]
    scratch = [pltpu.VMEM((8, 2 * rows), jnp.float32), pltpu.SMEM((1,), jnp.int32)]
    if last:
        out_shape = jax.ShapeDtypeStruct((block_count * HEAD_SIZE + lse_rows(block_count), rows), jnp.bfloat16)
        scratch = [pltpu.VMEM(shape, jnp.float32) for shape in state] + scratch
        scratch = [pltpu.VMEM((-(-block_count // 8) * 8, rows), jnp.float32)] + scratch
    else:
        out_shape = tuple(jax.ShapeDtypeStruct(shape, jnp.float32) for shape in state)
    return pl.pallas_call(
        functools.partial(cross_kernel, key_count, len(images), offset, last, len(queries)),
        out_shape=out_shape,
        in_specs=[SMEM] + [VMEM] * (len(queries) + len(images) + len(before)),
        out_specs=VMEM if last else (VMEM,) * 2,
        scratch_shapes=scratch,
        compiler_params=pltpu.CompilerParams(vmem_limit_bytes=VMEM_LIMIT),
        cost_estimate=MUCH,
        name="cross_last" if last else "cross_first",
    )(table, *queries, *images, *before)


def lse_of(ref, block_count):
    tail = ref[block_count * HEAD_SIZE :, :].astype(jnp.float32)
    return tail[0:block_count] + tail[block_count : 2 * block_count] + tail[2 * block_count : 3 * block_count]


def lse_pieces(lse, block_count):
    first = lse.astype(jnp.bfloat16).astype(jnp.float32)
    second = (lse - first).astype(jnp.bfloat16).astype(jnp.float32)
    pieces = [first, second, lse - first - second]
    spare = lse_rows(block_count) - 3 * block_count
    if spare:
        pieces.append(jnp.zeros((spare, lse.shape[1]), jnp.float32))
    return jnp.concatenate(pieces, axis=0).astype(jnp.bfloat16)


def mixed_block(part_refs, weights, block):
    at = slice(block * HEAD_SIZE, (block + 1) * HEAD_SIZE)
    terms = [weight[block : block + 1, :] * ref[at, :].astype(jnp.float32) for ref, weight in zip(part_refs, weights)]
    return functools.reduce(jnp.add, terms)


def combine_kernel(held, last, *refs):
    if held:
        mixed_ref, lse_ref, part_ref, *out_refs = refs
        block_count = lse_ref.shape[0]
        lse = [lse_ref[...], lse_of(part_ref, block_count)]
    else:
        mixed_ref, part_ref, *out_refs = refs
        block_count = packed_blocks(part_ref.shape[0])
        lse = [lse_of(mixed_ref, block_count), lse_of(part_ref, block_count)]
    highest = functools.reduce(jnp.maximum, lse)
    weights = [jnp.exp2(one - highest) for one in lse]
    total = functools.reduce(jnp.add, weights)
    weights = [one / total for one in weights]
    for block in range(block_count):
        mixed = mixed_block((mixed_ref, part_ref), weights, block)
        if last:
            store_heads(out_refs[0], block, mixed)
        else:
            out_refs[0][block * HEAD_SIZE : (block + 1) * HEAD_SIZE, :] = mixed
    if not last:
        out_refs[1][...] = highest + jnp.log2(total)


def store_heads(out_ref, block, mixed):
    at = slice(block * MASK_BLOCK_TOKENS, (block + 1) * MASK_BLOCK_TOKENS)
    for head in range(out_ref.shape[1] // HEAD_SIZE):
        piece = mixed[:, head * MASK_BLOCK_TOKENS : (head + 1) * MASK_BLOCK_TOKENS]
        out_ref[at, head * HEAD_SIZE : (head + 1) * HEAD_SIZE] = piece.T.astype(jnp.bfloat16)


def combined(so_far, part, shape, last):
    tokens, columns = shape
    held = len(so_far) == 2
    block_count = tokens // MASK_BLOCK_TOKENS
    rows = columns // HEAD_SIZE * MASK_BLOCK_TOKENS
    if last:
        out_shape = jax.ShapeDtypeStruct(shape, jnp.bfloat16)
    else:
        out_shape = (
            jax.ShapeDtypeStruct((block_count * HEAD_SIZE, rows), jnp.float32),
            jax.ShapeDtypeStruct((block_count, rows), jnp.float32),
        )
    return pl.pallas_call(
        functools.partial(combine_kernel, held, last),
        out_shape=out_shape,
        in_specs=[VMEM] * (len(so_far) + 1),
        out_specs=VMEM if last else (VMEM,) * 2,
        compiler_params=pltpu.CompilerParams(vmem_limit_bytes=VMEM_LIMIT),
        cost_estimate=MUCH,
        name="combine_last" if last else "combine",
    )(*so_far, part)


def pair_queries(q_ref, first, blocks):
    return jnp.concatenate(
        [
            stacked_heads(q_ref[block * MASK_BLOCK_TOKENS : (block + 1) * MASK_BLOCK_TOKENS, :])
            for block in range(first, first + blocks)
        ],
        axis=0,
    )


def self_first_kernel(group, q_ref, text_ref, high_ref, mixed_ref, value_ref):
    tokens, columns = q_ref.shape
    rows = columns // HEAD_SIZE * MASK_BLOCK_TOKENS
    value_ref[...] = text_ref[:, HEAD_SIZE:].T
    for index in range(tokens // MASK_BLOCK_TOKENS // group):
        first = index * group
        start, stop = first * MASK_BLOCK_TOKENS, (first + group) * MASK_BLOCK_TOKENS
        scores = nt_dot(text_ref[0:stop, 0:HEAD_SIZE], pair_queries(q_ref, first, group))
        tail = scores[start:, :]
        key_id = lax.broadcasted_iota(jnp.int32, tail.shape, 0)
        column = lax.broadcasted_iota(jnp.int32, tail.shape, 1)
        query_id = column // rows * MASK_BLOCK_TOKENS + column % MASK_BLOCK_TOKENS
        tail = jnp.where(key_id <= query_id, tail, LOWEST)
        scores = jnp.concatenate([scores[:start, :], tail], axis=0) if start else tail
        high = jnp.full((1, group * rows), LOWEST, jnp.float32)
        mixed = jnp.zeros((MIXED_ROWS, group * rows), jnp.float32)
        high, mixed = fold(high, mixed, scores, value_ref[:, 0:stop], True)
        high_ref[index] = jnp.broadcast_to(high, high_ref.shape[1:])
        mixed_ref[index] = mixed


def self_last_kernel(group, pieces, position_ref, q_ref, high_ref, mixed_ref, *refs):
    texts = refs[:pieces]
    out_ref, value_ref, new_high_ref, new_mixed_ref = refs[pieces:]
    rows = q_ref.shape[1] // HEAD_SIZE * MASK_BLOCK_TOKENS
    new_high_ref[...] = high_ref[...]
    new_mixed_ref[...] = mixed_ref[...]
    for piece in range(pieces):

        @pl.when(position_ref[0] >= piece + 1)
        def _(piece=piece):
            value_ref[...] = texts[piece][:, HEAD_SIZE:].T
            for index in range(high_ref.shape[0]):
                scores = nt_dot(texts[piece][:, 0:HEAD_SIZE], pair_queries(q_ref, index * group, group))
                high, mixed = fold(new_high_ref[index, 0:1, :], new_mixed_ref[index], scores, value_ref[...], True)
                new_high_ref[index] = jnp.broadcast_to(high, high_ref.shape[1:])
                new_mixed_ref[index] = mixed

    for index in range(high_ref.shape[0]):
        total = new_mixed_ref[index, HEAD_SIZE : HEAD_SIZE + 1, :]
        mixed = new_mixed_ref[index, 0:HEAD_SIZE, :] / total
        for block in range(group):
            store_heads(out_ref, index * group + block, mixed[:, block * rows : (block + 1) * rows])


def self_first(queries, text):
    tokens, columns = queries.shape
    block_count = tokens // MASK_BLOCK_TOKENS
    group = 1 if block_count % 2 else 2
    width = group * columns // HEAD_SIZE * MASK_BLOCK_TOKENS
    return pl.pallas_call(
        functools.partial(self_first_kernel, group),
        out_shape=(
            jax.ShapeDtypeStruct((block_count // group, 8, width), jnp.float32),
            jax.ShapeDtypeStruct((block_count // group, MIXED_ROWS, width), jnp.float32),
        ),
        in_specs=[VMEM] * 2,
        out_specs=(VMEM,) * 2,
        scratch_shapes=[pltpu.VMEM((HEAD_SIZE, tokens), jnp.bfloat16)],
        compiler_params=pltpu.CompilerParams(vmem_limit_bytes=VMEM_LIMIT),
        cost_estimate=LITTLE,
        name="self_first",
    )(queries, text)


def self_last(position, queries, state, texts):
    tokens, columns = queries.shape
    group = tokens // MASK_BLOCK_TOKENS // state[0].shape[0]
    return pl.pallas_call(
        functools.partial(self_last_kernel, group, len(texts)),
        out_shape=jax.ShapeDtypeStruct((tokens, columns), jnp.bfloat16),
        in_specs=[SMEM] + [VMEM] * (3 + len(texts)),
        out_specs=VMEM,
        scratch_shapes=[pltpu.VMEM((HEAD_SIZE, tokens), jnp.bfloat16)]
        + [pltpu.VMEM(one.shape, jnp.float32) for one in state],
        compiler_params=pltpu.CompilerParams(vmem_limit_bytes=VMEM_LIMIT),
        cost_estimate=LITTLE,
        name="self_last",
    )(position, queries, *state, *texts)


def shifted(value, axis, steps):
    count = lax.axis_size(axis)
    return lax.ppermute(value, axis, [(source, (source + steps) % count) for source in range(count)])


def swapped(value, axis, bits):
    return lax.ppermute(value, axis, [(source, source ^ bits) for source in range(lax.axis_size(axis))])


def after(value, earlier):
    return lax.optimization_barrier((value, earlier))[0]


def per_device(
    self_queries, text_kv, cross_queries, image_kv, block_images, image_owner
):
    rows = self_queries.shape[0]
    key_count = image_kv.shape[2]
    cycle = lax.axis_size("blk")
    ring = lax.axis_size("enc")
    place = lax.axis_index("enc")
    inside = (place > 0) & (place < ring - 1)
    position = jnp.stack([lax.axis_index("blk"), inside]).astype(jnp.int32)

    images = [prepare(image_kv[0])]
    for _ in range(1, cycle):
        images.append(shifted(images[-1], "blk", 1))
    if ring == 4:
        queries = {step: [swapped(cross_queries, "enc", step)] for step in (2, 1)}
        middle = lax.ppermute(cross_queries, "enc", [(0, 0), (1, 2), (2, 1), (3, 3)])
        queries[3] = [middle, swapped(queries[2][0], "enc", 1)]
    else:
        queries = {step: [shifted(cross_queries, "enc", ring - step)] for step in range(1, ring)}
    queries[0] = [cross_queries]
    table = seen_table(position, block_images, image_owner)

    text = text_kv.reshape(rows, 2 * HEAD_SIZE)
    texts = []
    onward = after(text, images[-1])
    for _ in range(1, cycle):
        onward = shifted(onward, "blk", 1)
        texts.append(onward)

    latest = [None]

    def in_turn(arrays):
        return arrays if latest[0] is None else [after(one, latest[0]) for one in arrays]

    def begun(step):
        latest[0] = cross_part(table, in_turn(queries[step]), images[:1], key_count, 0, False)
        return latest[0]

    def finished(step, state=None):
        used = images if state is None else images[1:]
        before = () if state is None else state
        offset = 0 if state is None else 1
        latest[0] = cross_part(table, in_turn(queries[step]), used, key_count, offset, True, before)
        return latest[0]

    split = cycle > 1
    self_state = latest[0] = self_first(self_queries, text)
    own = begun(0) if split else None
    steps = [2, 3, 1] if ring == 4 else list(range(1, ring))
    states = {step: begun(step) for step in steps[:1]} if split else {}
    received = []
    for step in steps:
        part = finished(step, states.get(step))
        received.append(swapped(part, "enc", step) if ring == 4 else shifted(part, "enc", step))
    own_part = finished(0, own)
    self_out = latest[0] = self_last(position, in_turn([self_queries])[0], self_state, texts)
    so_far = in_turn([own_part])
    for index, part in enumerate(received):
        so_far = combined(so_far, part, cross_queries.shape, index + 1 == len(received))
    return (self_out, so_far)


def solution(mesh):
    placed = (
        P("blk", ("tp", "enc")),
        P("blk", None, "tp"),
        P("blk", ("tp", "enc")),
        P("blk", None, "enc", "tp"),
        P("blk", None),
        P(),
    )
    return jax.shard_map(
        per_device,
        mesh=mesh,
        in_specs=placed,
        out_specs=(P("blk", ("tp", "enc")), P("blk", ("tp", "enc"))),
        check_vma=False,
    )
```

```python
import functools
import math

import jax
import jax.numpy as jnp
from jax import lax
from jax.experimental import pallas as pl
from jax.experimental.pallas import tpu as pltpu
from jax.sharding import PartitionSpec as P

HEAD_SIZE = 128
MASK_BLOCK_TOKENS = 128
LANES = 128
LOWEST = -1e30
MIXED_ROWS = HEAD_SIZE + 16
SHIFT_KEYS = 256
MOST_SUM = 2.0**100
LOG2_SCALE = math.log2(math.e) / math.sqrt(HEAD_SIZE)
VMEM_LIMIT = 48 * 1024 * 1024

LITTLE = pl.CostEstimate(flops=0, bytes_accessed=1024, transcendentals=0)
MUCH = pl.CostEstimate(flops=2_000_000_000, bytes_accessed=1024, transcendentals=0)

VMEM = pl.BlockSpec(memory_space=pltpu.VMEM)
SMEM = pl.BlockSpec(memory_space=pltpu.SMEM)


def padded(count):
    return -(-count // LANES) * LANES


def nt_dot(a, b):
    return lax.dot_general(a, b, (((1,), (1,)), ((), ())), preferred_element_type=jnp.float32)


def at_block(block, size=MASK_BLOCK_TOKENS):
    return pl.ds(pl.multiple_of(block * size, size), size)


def stacked_heads(rows):
    heads = rows.shape[1] // HEAD_SIZE
    return jnp.concatenate([rows[:, h * HEAD_SIZE : (h + 1) * HEAD_SIZE] for h in range(heads)], axis=0)


def with_ones(value_t):
    shape = (MIXED_ROWS - HEAD_SIZE, value_t.shape[1])
    ones = (lax.broadcasted_iota(jnp.int32, shape, 0) == 0).astype(jnp.bfloat16)
    return jnp.concatenate([value_t, ones], axis=0)


def fold(high, mixed, scores, value_t, exact):
    seen = scores if exact else scores[0 : min(SHIFT_KEYS, scores.shape[0]), :]
    new_high = jnp.maximum(high, jnp.max(seen, axis=0, keepdims=True))
    weights = jnp.exp2(scores * LOG2_SCALE - new_high * LOG2_SCALE).astype(jnp.bfloat16)
    fading = jnp.exp2((high - new_high) * LOG2_SCALE)
    mixed = mixed * fading + jnp.dot(with_ones(value_t), weights, preferred_element_type=jnp.float32)
    return new_high, mixed


def prepare_kernel(kv_ref, out_ref):
    count = kv_ref.shape[1]
    whole = count // LANES * LANES
    rest = count - whole
    out_ref[0, 0:whole, :] = kv_ref[0, 0:whole, :]
    for at in range(0, whole, LANES):
        out_ref[1, at : at + LANES, :] = kv_ref[1, at : at + LANES, :].T
    if rest:
        empty = jnp.zeros((LANES - rest, HEAD_SIZE), jnp.float32)
        tail_key = jnp.concatenate([kv_ref[0, whole:count, :].astype(jnp.float32), empty], axis=0)
        tail_value = jnp.concatenate([kv_ref[1, whole:count, :].astype(jnp.float32), empty], axis=0)
        out_ref[0, whole : whole + LANES, :] = tail_key.astype(jnp.bfloat16)
        out_ref[1, whole : whole + LANES, :] = tail_value.T.astype(jnp.bfloat16)


def prepare(kv):
    return pl.pallas_call(
        prepare_kernel,
        out_shape=jax.ShapeDtypeStruct((2, padded(kv.shape[1]), HEAD_SIZE), jnp.bfloat16),
        in_specs=[VMEM],
        out_specs=VMEM,
        compiler_params=pltpu.CompilerParams(vmem_limit_bytes=VMEM_LIMIT),
        cost_estimate=LITTLE,
        name="prepare",
    )(kv)


def lse_rows(block_count):
    return -(-3 * block_count // 16) * 16


def packed_blocks(rows):
    return next(count for count in range(1, rows) if count * HEAD_SIZE + lse_rows(count) == rows)


def table_kernel(position_ref, inside_ref, images_ref, owner_ref, table_ref):
    slots, block_count = images_ref.shape
    for piece in range(slots):
        slot = lax.rem(position_ref[0] + (slots - piece), slots)
        base = piece * (block_count + 1)
        count = jnp.int32(0)
        for block in range(block_count):
            table_ref[base + 1 + block] = jnp.int32(0)
        for block in range(block_count):
            seen = lax.fori_loop(
                0,
                slots,
                lambda image, sum, block=block, slot=slot: sum
                + jnp.where(owner_ref[image] == slot, images_ref[image, block], 0),
                jnp.int32(0),
            )

            @pl.when(seen > 0)
            def _(base=base, block=block, count=count):
                table_ref[base + 1 + count] = jnp.int32(block)

            count = count + jnp.where(seen > 0, 1, 0)
        table_ref[base] = count
    table_ref[slots * (block_count + 1)] = inside_ref[0]


def seen_table(position, inside, block_images, image_owner):
    block_count, slots = block_images.shape
    return pl.pallas_call(
        table_kernel,
        out_shape=jax.ShapeDtypeStruct((slots * (block_count + 1) + 1,), jnp.int32),
        in_specs=[SMEM] * 4,
        out_specs=SMEM,
        name="seen_table",
    )(position, inside, block_images.T, image_owner)


def chunks_of(width):
    half = width // LANES // 2 * LANES
    return [(0, half), (half, width)] if half else [(0, width)]


def cross_kernel(key_count, pieces, offset, last, parts, table_ref, *refs):
    q_refs, images, refs = refs[:parts], refs[parts : parts + pieces], refs[parts + pieces :]
    if offset:
        before, refs = refs[:2], refs[2:]
    if last:
        out_ref, lse_ref, high_ref, mixed_ref, peak_ref, redo_ref = refs
    else:
        high_ref, mixed_ref, peak_ref, redo_ref = refs
    block_count = q_refs[0].shape[0] // MASK_BLOCK_TOKENS
    rows = q_refs[0].shape[1] // HEAD_SIZE * MASK_BLOCK_TOKENS
    peak_ref[...] = jnp.full_like(peak_ref, LOWEST)
    redo_ref[0] = jnp.int32(0)

    def fold_pair(blocks, image, exact, held):
        width = image.shape[1]
        queries = [q_refs[0][at_block(block), :] for block in blocks]
        if parts > 1:
            first = table_ref[table_ref.shape[0] - 1] > 0
            queries = [jnp.where(first, one, q_refs[1][at_block(block), :]) for one, block in zip(queries, blocks)]
        queries = jnp.concatenate([stacked_heads(one) for one in queries], axis=0)
        chunks = chunks_of(width)

        def scores_of(start, stop):
            scores = nt_dot(image[0, start:stop, :], queries)
            if stop > key_count:
                body = stop - start - LANES
                tail = scores[body:, :]
                key_id = start + body + lax.broadcasted_iota(jnp.int32, tail.shape, 0)
                tail = jnp.where(key_id < key_count, tail, LOWEST)
                scores = jnp.concatenate([scores[:body, :], tail], axis=0) if body else tail
            return scores

        @pl.when(exact)
        def _():
            tops = [jnp.max(scores_of(*chunk), axis=0, keepdims=True) for chunk in chunks]
            peak_ref[0:1, :] = functools.reduce(jnp.maximum, tops)

        if held is None:
            high = jnp.full((1, 2 * rows), LOWEST, jnp.float32)
            mixed = jnp.zeros((MIXED_ROWS, 2 * rows), jnp.float32)
        else:
            high = jnp.concatenate([held[0][block][0:1] for block in blocks], axis=1)
            mixed = jnp.concatenate([held[1][block] for block in blocks], axis=1)
        scores = scores_of(*chunks[0])
        seen = jnp.max(scores[0 : min(SHIFT_KEYS, scores.shape[0])], axis=0, keepdims=True)
        new_high = jnp.maximum(jnp.maximum(high, seen), peak_ref[0:1, :])
        shift = new_high * LOG2_SCALE
        mixed = mixed * jnp.exp2((high - new_high) * LOG2_SCALE)
        for index, (start, stop) in enumerate(chunks):
            following = scores_of(*chunks[index + 1]) if index + 1 < len(chunks) else None
            weights = jnp.exp2(scores * LOG2_SCALE - shift).astype(jnp.bfloat16)
            value_t = jnp.concatenate([image[1, c : c + LANES, :] for c in range(start, stop, LANES)], axis=1)
            mixed = mixed + jnp.dot(with_ones(value_t), weights, preferred_element_type=jnp.float32)
            scores = following
        for index, block in enumerate(blocks):
            own = slice(index * rows, (index + 1) * rows)
            high_ref[block] = jnp.broadcast_to(new_high[:, own], high_ref.shape[1:])
            mixed_ref[block] = mixed[:, own]

    def finish():
        for block in range(block_count):
            total = mixed_ref[block, HEAD_SIZE : HEAD_SIZE + 1, :]
            out_ref[block * HEAD_SIZE : (block + 1) * HEAD_SIZE, :] = (
                mixed_ref[block, 0:HEAD_SIZE, :] * (1.0 / total)
            ).astype(jnp.bfloat16)
            lse_ref[block : block + 1, :] = high_ref[block, 0:1, :] * LOG2_SCALE + jnp.log2(total)
        out_ref[block_count * HEAD_SIZE :, :] = lse_pieces(lse_ref[0:block_count, :], block_count)

    def attempt(trial, carry):
        @pl.when((trial == 0) | (redo_ref[0] > 0))
        def _():
            for piece in range(pieces):
                base = (offset + piece) * (block_count + 1)
                count = table_ref[base]
                if piece == 0:
                    held = before if offset else None
                    for block in range(block_count):
                        seen = functools.reduce(
                            jnp.logical_or,
                            [(count > index) & (table_ref[base + 1 + index] == block) for index in range(block_count)],
                        )

                        @pl.when(jnp.logical_not(seen))
                        def _(block=block):
                            if held is None:
                                high_ref[block] = jnp.full(high_ref.shape[1:], LOWEST, jnp.float32)
                                mixed_ref[block] = jnp.zeros(mixed_ref.shape[1:], jnp.float32)
                            else:
                                high_ref[block] = held[0][block]
                                mixed_ref[block] = held[1][block]

                else:
                    held = (high_ref, mixed_ref)

                def pair_step(pair, carry, piece=piece, base=base, count=count, held=held):
                    blocks = [table_ref[base + 1 + 2 * pair], table_ref[base + jnp.minimum(2 * pair + 2, count)]]
                    fold_pair(blocks, images[piece], trial > 0, held)
                    return carry

                lax.fori_loop(0, (count + 1) // 2, pair_step, 0)
            most = functools.reduce(
                jnp.maximum, [mixed_ref[block, HEAD_SIZE : HEAD_SIZE + 1, :] for block in range(block_count)]
            )
            if last:
                finish()
            redo_ref[0] = 1 - jnp.min((most <= MOST_SUM).astype(jnp.int32))

        return carry

    lax.fori_loop(0, 2, attempt, 0)


def cross_part(table, queries, images, key_count, offset, last, before=()):
    tokens, columns = queries[0].shape
    block_count = tokens // MASK_BLOCK_TOKENS
    rows = columns // HEAD_SIZE * MASK_BLOCK_TOKENS
    state = [(block_count, 8, rows), (block_count, MIXED_ROWS, rows)]
    scratch = [pltpu.VMEM((8, 2 * rows), jnp.float32), pltpu.SMEM((1,), jnp.int32)]
    if last:
        out_shape = jax.ShapeDtypeStruct((block_count * HEAD_SIZE + lse_rows(block_count), rows), jnp.bfloat16)
        scratch = [pltpu.VMEM(shape, jnp.float32) for shape in state] + scratch
        scratch = [pltpu.VMEM((-(-block_count // 8) * 8, rows), jnp.float32)] + scratch
    else:
        out_shape = tuple(jax.ShapeDtypeStruct(shape, jnp.float32) for shape in state)
    return pl.pallas_call(
        functools.partial(cross_kernel, key_count, len(images), offset, last, len(queries)),
        out_shape=out_shape,
        in_specs=[SMEM] + [VMEM] * (len(queries) + len(images) + len(before)),
        out_specs=VMEM if last else (VMEM,) * 2,
        scratch_shapes=scratch,
        compiler_params=pltpu.CompilerParams(vmem_limit_bytes=VMEM_LIMIT),
        cost_estimate=MUCH,
        name="cross_last" if last else "cross_first",
    )(table, *queries, *images, *before)


def lse_of(ref, block_count):
    tail = ref[block_count * HEAD_SIZE :, :].astype(jnp.float32)
    return tail[0:block_count] + tail[block_count : 2 * block_count] + tail[2 * block_count : 3 * block_count]


def lse_pieces(lse, block_count):
    first = lse.astype(jnp.bfloat16).astype(jnp.float32)
    second = (lse - first).astype(jnp.bfloat16).astype(jnp.float32)
    pieces = [first, second, lse - first - second]
    spare = lse_rows(block_count) - 3 * block_count
    if spare:
        pieces.append(jnp.zeros((spare, lse.shape[1]), jnp.float32))
    return jnp.concatenate(pieces, axis=0).astype(jnp.bfloat16)


def mixed_block(part_refs, weights, block):
    at = slice(block * HEAD_SIZE, (block + 1) * HEAD_SIZE)
    terms = [weight[block : block + 1, :] * ref[at, :].astype(jnp.float32) for ref, weight in zip(part_refs, weights)]
    return functools.reduce(jnp.add, terms)


def combine_kernel(held, last, *refs):
    if held:
        mixed_ref, lse_ref, part_ref, *out_refs = refs
        block_count = lse_ref.shape[0]
        lse = [lse_ref[...], lse_of(part_ref, block_count)]
    else:
        mixed_ref, part_ref, *out_refs = refs
        block_count = packed_blocks(part_ref.shape[0])
        lse = [lse_of(mixed_ref, block_count), lse_of(part_ref, block_count)]
    highest = functools.reduce(jnp.maximum, lse)
    weights = [jnp.exp2(one - highest) for one in lse]
    total = functools.reduce(jnp.add, weights)
    weights = [one / total for one in weights]
    for block in range(block_count):
        mixed = mixed_block((mixed_ref, part_ref), weights, block)
        if last:
            store_heads(out_refs[0], block, mixed)
        else:
            out_refs[0][block * HEAD_SIZE : (block + 1) * HEAD_SIZE, :] = mixed
    if not last:
        out_refs[1][...] = highest + jnp.log2(total)


def store_heads(out_ref, block, mixed):
    at = slice(block * MASK_BLOCK_TOKENS, (block + 1) * MASK_BLOCK_TOKENS)
    for head in range(out_ref.shape[1] // HEAD_SIZE):
        piece = mixed[:, head * MASK_BLOCK_TOKENS : (head + 1) * MASK_BLOCK_TOKENS]
        out_ref[at, head * HEAD_SIZE : (head + 1) * HEAD_SIZE] = piece.T.astype(jnp.bfloat16)


def combined(so_far, part, shape, last):
    tokens, columns = shape
    held = len(so_far) == 2
    block_count = tokens // MASK_BLOCK_TOKENS
    rows = columns // HEAD_SIZE * MASK_BLOCK_TOKENS
    if last:
        out_shape = jax.ShapeDtypeStruct(shape, jnp.bfloat16)
    else:
        out_shape = (
            jax.ShapeDtypeStruct((block_count * HEAD_SIZE, rows), jnp.float32),
            jax.ShapeDtypeStruct((block_count, rows), jnp.float32),
        )
    return pl.pallas_call(
        functools.partial(combine_kernel, held, last),
        out_shape=out_shape,
        in_specs=[VMEM] * (len(so_far) + 1),
        out_specs=VMEM if last else (VMEM,) * 2,
        compiler_params=pltpu.CompilerParams(vmem_limit_bytes=VMEM_LIMIT),
        cost_estimate=MUCH,
        name="combine_last" if last else "combine",
    )(*so_far, part)


def pair_queries(q_ref, first, blocks):
    return jnp.concatenate(
        [
            stacked_heads(q_ref[block * MASK_BLOCK_TOKENS : (block + 1) * MASK_BLOCK_TOKENS, :])
            for block in range(first, first + blocks)
        ],
        axis=0,
    )


def self_first_kernel(group, q_ref, text_ref, high_ref, mixed_ref, value_ref):
    tokens, columns = q_ref.shape
    rows = columns // HEAD_SIZE * MASK_BLOCK_TOKENS
    value_ref[...] = text_ref[:, HEAD_SIZE:].T
    for index in range(tokens // MASK_BLOCK_TOKENS // group):
        first = index * group
        start, stop = first * MASK_BLOCK_TOKENS, (first + group) * MASK_BLOCK_TOKENS
        scores = nt_dot(text_ref[0:stop, 0:HEAD_SIZE], pair_queries(q_ref, first, group))
        tail = scores[start:, :]
        key_id = lax.broadcasted_iota(jnp.int32, tail.shape, 0)
        column = lax.broadcasted_iota(jnp.int32, tail.shape, 1)
        query_id = column // rows * MASK_BLOCK_TOKENS + column % MASK_BLOCK_TOKENS
        tail = jnp.where(key_id <= query_id, tail, LOWEST)
        scores = jnp.concatenate([scores[:start, :], tail], axis=0) if start else tail
        high = jnp.full((1, group * rows), LOWEST, jnp.float32)
        mixed = jnp.zeros((MIXED_ROWS, group * rows), jnp.float32)
        high, mixed = fold(high, mixed, scores, value_ref[:, 0:stop], True)
        high_ref[index] = jnp.broadcast_to(high, high_ref.shape[1:])
        mixed_ref[index] = mixed


def self_last_kernel(group, pieces, position_ref, q_ref, high_ref, mixed_ref, *refs):
    texts = refs[:pieces]
    out_ref, value_ref, new_high_ref, new_mixed_ref = refs[pieces:]
    rows = q_ref.shape[1] // HEAD_SIZE * MASK_BLOCK_TOKENS
    new_high_ref[...] = high_ref[...]
    new_mixed_ref[...] = mixed_ref[...]
    for piece in range(pieces):

        @pl.when(position_ref[0] >= piece + 1)
        def _(piece=piece):
            value_ref[...] = texts[piece][:, HEAD_SIZE:].T
            for index in range(high_ref.shape[0]):
                scores = nt_dot(texts[piece][:, 0:HEAD_SIZE], pair_queries(q_ref, index * group, group))
                high, mixed = fold(new_high_ref[index, 0:1, :], new_mixed_ref[index], scores, value_ref[...], True)
                new_high_ref[index] = jnp.broadcast_to(high, high_ref.shape[1:])
                new_mixed_ref[index] = mixed

    for index in range(high_ref.shape[0]):
        total = new_mixed_ref[index, HEAD_SIZE : HEAD_SIZE + 1, :]
        mixed = new_mixed_ref[index, 0:HEAD_SIZE, :] / total
        for block in range(group):
            store_heads(out_ref, index * group + block, mixed[:, block * rows : (block + 1) * rows])


def self_first(queries, text):
    tokens, columns = queries.shape
    block_count = tokens // MASK_BLOCK_TOKENS
    group = 1 if block_count % 2 else 2
    width = group * columns // HEAD_SIZE * MASK_BLOCK_TOKENS
    return pl.pallas_call(
        functools.partial(self_first_kernel, group),
        out_shape=(
            jax.ShapeDtypeStruct((block_count // group, 8, width), jnp.float32),
            jax.ShapeDtypeStruct((block_count // group, MIXED_ROWS, width), jnp.float32),
        ),
        in_specs=[VMEM] * 2,
        out_specs=(VMEM,) * 2,
        scratch_shapes=[pltpu.VMEM((HEAD_SIZE, tokens), jnp.bfloat16)],
        compiler_params=pltpu.CompilerParams(vmem_limit_bytes=VMEM_LIMIT),
        cost_estimate=LITTLE,
        name="self_first",
    )(queries, text)


def self_last(position, queries, state, texts):
    tokens, columns = queries.shape
    group = tokens // MASK_BLOCK_TOKENS // state[0].shape[0]
    return pl.pallas_call(
        functools.partial(self_last_kernel, group, len(texts)),
        out_shape=jax.ShapeDtypeStruct((tokens, columns), jnp.bfloat16),
        in_specs=[SMEM] + [VMEM] * (3 + len(texts)),
        out_specs=VMEM,
        scratch_shapes=[pltpu.VMEM((HEAD_SIZE, tokens), jnp.bfloat16)]
        + [pltpu.VMEM(one.shape, jnp.float32) for one in state],
        compiler_params=pltpu.CompilerParams(vmem_limit_bytes=VMEM_LIMIT),
        cost_estimate=LITTLE,
        name="self_last",
    )(position, queries, *state, *texts)


def shifted(value, axis, steps):
    count = lax.axis_size(axis)
    return lax.ppermute(value, axis, [(source, (source + steps) % count) for source in range(count)])


def swapped(value, axis, bits):
    return lax.ppermute(value, axis, [(source, source ^ bits) for source in range(lax.axis_size(axis))])


def after(value, earlier):
    return lax.optimization_barrier((value, earlier))[0]


def per_device(
    self_queries, text_kv, cross_queries, image_kv, block_images, image_owner
):
    rows = self_queries.shape[0]
    key_count = image_kv.shape[2]
    cycle = lax.axis_size("blk")
    ring = lax.axis_size("enc")
    place = lax.axis_index("enc")
    inside = ((place > 0) & (place < ring - 1)).astype(jnp.int32)[None]
    position = lax.axis_index("blk").astype(jnp.int32)[None]

    images = [prepare(image_kv[0])]
    for _ in range(1, cycle):
        images.append(shifted(images[-1], "blk", 1))
    if ring == 4:
        queries = {step: [swapped(cross_queries, "enc", step)] for step in (2, 1)}
        middle = lax.ppermute(cross_queries, "enc", [(0, 0), (1, 2), (2, 1), (3, 3)])
        queries[3] = [middle, swapped(queries[2][0], "enc", 1)]
    else:
        queries = {step: [shifted(cross_queries, "enc", ring - step)] for step in range(1, ring)}
    queries[0] = [cross_queries]
    table = seen_table(position, inside, block_images, image_owner)

    latest = [None]

    def in_turn(arrays):
        return arrays if latest[0] is None else [after(one, latest[0]) for one in arrays]

    def begun(step):
        latest[0] = cross_part(table, in_turn(queries[step]), images[:1], key_count, 0, False)
        return latest[0]

    def finished(step, state=None):
        used = images if state is None else images[1:]
        before = () if state is None else state
        offset = 0 if state is None else 1
        latest[0] = cross_part(table, in_turn(queries[step]), used, key_count, offset, True, before)
        return latest[0]

    split = cycle > 1
    own = begun(0) if split else None
    steps = [2, 3, 1] if ring == 4 else list(range(1, ring))
    states = {step: begun(step) for step in steps[:1]} if split else {}
    received, texts = [], []
    for step in steps:
        part = finished(step, states.get(step))
        if not texts:
            texts.append(after(text_kv, part).reshape(rows, 2 * HEAD_SIZE))
            for _ in range(1, cycle):
                texts.append(shifted(texts[-1], "blk", 1))
        received.append(swapped(part, "enc", step) if ring == 4 else shifted(part, "enc", step))
    own_part = finished(0, own)
    self_state = latest[0] = self_first(in_turn([self_queries])[0], texts[0])
    self_out = latest[0] = self_last(position, in_turn([self_queries])[0], self_state, texts[1:])
    so_far = in_turn([own_part])
    for index, part in enumerate(received):
        so_far = combined(so_far, part, cross_queries.shape, index + 1 == len(received))
    return (self_out, so_far)


def solution(mesh):
    placed = (
        P("blk", ("tp", "enc")),
        P("blk", None, "tp"),
        P("blk", ("tp", "enc")),
        P("blk", None, "enc", "tp"),
        P("blk", None),
        P(),
    )
    return jax.shard_map(
        per_device,
        mesh=mesh,
        in_specs=placed,
        out_specs=(P("blk", ("tp", "enc")), P("blk", ("tp", "enc"))),
        check_vma=False,
    )
```

```python
import functools
import math

import jax
import jax.numpy as jnp
from jax import lax
from jax.experimental import pallas as pl
from jax.experimental.pallas import tpu as pltpu
from jax.sharding import PartitionSpec as P

HEAD_SIZE = 128
MASK_BLOCK_TOKENS = 128
LANES = 128
LOWEST = -1e30
MIXED_ROWS = HEAD_SIZE + 16
SHIFT_KEYS = 256
MOST_SUM = 2.0**100
LOG2_SCALE = math.log2(math.e) / math.sqrt(HEAD_SIZE)
VMEM_LIMIT = 48 * 1024 * 1024

LITTLE = pl.CostEstimate(flops=0, bytes_accessed=1024, transcendentals=0)
MUCH = pl.CostEstimate(flops=2_000_000_000, bytes_accessed=1024, transcendentals=0)

VMEM = pl.BlockSpec(memory_space=pltpu.VMEM)
SMEM = pl.BlockSpec(memory_space=pltpu.SMEM)


def padded(count):
    return -(-count // LANES) * LANES


def nt_dot(a, b):
    return lax.dot_general(a, b, (((1,), (1,)), ((), ())), preferred_element_type=jnp.float32)


def at_block(block, size=MASK_BLOCK_TOKENS):
    return pl.ds(pl.multiple_of(block * size, size), size)


def stacked_heads(rows):
    heads = rows.shape[1] // HEAD_SIZE
    return jnp.concatenate([rows[:, h * HEAD_SIZE : (h + 1) * HEAD_SIZE] for h in range(heads)], axis=0)


def with_ones(value_t):
    shape = (MIXED_ROWS - HEAD_SIZE, value_t.shape[1])
    ones = (lax.broadcasted_iota(jnp.int32, shape, 0) == 0).astype(jnp.bfloat16)
    return jnp.concatenate([value_t, ones], axis=0)


def fold(high, mixed, scores, value_t, exact):
    seen = scores if exact else scores[0 : min(SHIFT_KEYS, scores.shape[0]), :]
    new_high = jnp.maximum(high, jnp.max(seen, axis=0, keepdims=True))
    weights = jnp.exp2(scores * LOG2_SCALE - new_high * LOG2_SCALE).astype(jnp.bfloat16)
    fading = jnp.exp2((high - new_high) * LOG2_SCALE)
    mixed = mixed * fading + jnp.dot(with_ones(value_t), weights, preferred_element_type=jnp.float32)
    return new_high, mixed


def prepare_kernel(kv_ref, out_ref):
    count = kv_ref.shape[1]
    whole = count // LANES * LANES
    rest = count - whole
    out_ref[0, 0:whole, :] = kv_ref[0, 0:whole, :]
    for at in range(0, whole, LANES):
        out_ref[1, at : at + LANES, :] = kv_ref[1, at : at + LANES, :].T
    if rest:
        empty = jnp.zeros((LANES - rest, HEAD_SIZE), jnp.float32)
        tail_key = jnp.concatenate([kv_ref[0, whole:count, :].astype(jnp.float32), empty], axis=0)
        tail_value = jnp.concatenate([kv_ref[1, whole:count, :].astype(jnp.float32), empty], axis=0)
        out_ref[0, whole : whole + LANES, :] = tail_key.astype(jnp.bfloat16)
        out_ref[1, whole : whole + LANES, :] = tail_value.T.astype(jnp.bfloat16)


def prepare(kv):
    return pl.pallas_call(
        prepare_kernel,
        out_shape=jax.ShapeDtypeStruct((2, padded(kv.shape[1]), HEAD_SIZE), jnp.bfloat16),
        in_specs=[VMEM],
        out_specs=VMEM,
        compiler_params=pltpu.CompilerParams(vmem_limit_bytes=VMEM_LIMIT),
        cost_estimate=LITTLE,
        name="prepare",
    )(kv)


def lse_rows(block_count):
    return -(-3 * block_count // 16) * 16


def packed_blocks(rows):
    return next(count for count in range(1, rows) if count * HEAD_SIZE + lse_rows(count) == rows)


def table_kernel(position_ref, inside_ref, images_ref, owner_ref, table_ref):
    slots, block_count = images_ref.shape
    for piece in range(slots):
        slot = lax.rem(position_ref[0] + (slots - piece), slots)
        base = piece * (block_count + 1)
        count = jnp.int32(0)
        for block in range(block_count):
            table_ref[base + 1 + block] = jnp.int32(0)
        for block in range(block_count):
            seen = lax.fori_loop(
                0,
                slots,
                lambda image, sum, block=block, slot=slot: sum
                + jnp.where(owner_ref[image] == slot, images_ref[image, block], 0),
                jnp.int32(0),
            )

            @pl.when(seen > 0)
            def _(base=base, block=block, count=count):
                table_ref[base + 1 + count] = jnp.int32(block)

            count = count + jnp.where(seen > 0, 1, 0)
        table_ref[base] = count
    table_ref[slots * (block_count + 1)] = inside_ref[0]


def seen_table(position, inside, block_images, image_owner):
    block_count, slots = block_images.shape
    return pl.pallas_call(
        table_kernel,
        out_shape=jax.ShapeDtypeStruct((slots * (block_count + 1) + 1,), jnp.int32),
        in_specs=[SMEM] * 4,
        out_specs=SMEM,
        name="seen_table",
    )(position, inside, block_images.T, image_owner)


def halves_of(count):
    half = padded(count) // LANES // 2 * LANES
    return [(0, half), (half, count)] if half else [(0, count)]


def cross_kernel(layout, held_before, last, parts, table_ref, *refs):
    q_refs, refs = refs[:parts], refs[parts:]
    images = []
    for step, counts in layout:
        images.append((step, list(zip(refs[: len(counts)], counts))))
        refs = refs[len(counts) :]
    before = None
    if held_before:
        before, refs = refs[:2], refs[2:]
    if last:
        out_ref, lse_ref, high_ref, mixed_ref, peak_ref, redo_ref = refs
    else:
        high_ref, mixed_ref, peak_ref, redo_ref = refs
    block_count = q_refs[0].shape[0] // MASK_BLOCK_TOKENS
    rows = q_refs[0].shape[1] // HEAD_SIZE * MASK_BLOCK_TOKENS
    peak_ref[...] = jnp.full_like(peak_ref, LOWEST)
    redo_ref[0] = jnp.int32(0)

    def fold_pair(blocks, chunks, exact, held):
        queries = [q_refs[0][at_block(block), :] for block in blocks]
        if parts > 1:
            first = table_ref[table_ref.shape[0] - 1] > 0
            queries = [jnp.where(first, one, q_refs[1][at_block(block), :]) for one, block in zip(queries, blocks)]
        queries = jnp.concatenate([stacked_heads(one) for one in queries], axis=0)

        def scores_of(keys, count):
            scores = nt_dot(keys[0], queries)
            width = keys.shape[1]
            if width > count:
                body = width - LANES
                tail = scores[body:, :]
                key_id = body + lax.broadcasted_iota(jnp.int32, tail.shape, 0)
                tail = jnp.where(key_id < count, tail, LOWEST)
                scores = jnp.concatenate([scores[:body, :], tail], axis=0) if body else tail
            return scores

        @pl.when(exact)
        def _():
            tops = [jnp.max(scores_of(*chunk), axis=0, keepdims=True) for chunk in chunks]
            peak_ref[0:1, :] = functools.reduce(jnp.maximum, tops)

        if held is None:
            high = jnp.full((1, 2 * rows), LOWEST, jnp.float32)
            mixed = jnp.zeros((MIXED_ROWS, 2 * rows), jnp.float32)
        else:
            high = jnp.concatenate([held[0][block][0:1] for block in blocks], axis=1)
            mixed = jnp.concatenate([held[1][block] for block in blocks], axis=1)
        scores = scores_of(*chunks[0])
        seen = jnp.max(scores[0 : min(SHIFT_KEYS, scores.shape[0])], axis=0, keepdims=True)
        new_high = jnp.maximum(jnp.maximum(high, seen), peak_ref[0:1, :])
        shift = new_high * LOG2_SCALE
        mixed = mixed * jnp.exp2((high - new_high) * LOG2_SCALE)
        for index, (keys, _) in enumerate(chunks):
            following = scores_of(*chunks[index + 1]) if index + 1 < len(chunks) else None
            weights = jnp.exp2(scores * LOG2_SCALE - shift).astype(jnp.bfloat16)
            value_t = jnp.concatenate([keys[1, c : c + LANES, :] for c in range(0, keys.shape[1], LANES)], axis=1)
            mixed = mixed + jnp.dot(with_ones(value_t), weights, preferred_element_type=jnp.float32)
            scores = following
        for index, block in enumerate(blocks):
            own = slice(index * rows, (index + 1) * rows)
            high_ref[block] = jnp.broadcast_to(new_high[:, own], high_ref.shape[1:])
            mixed_ref[block] = mixed[:, own]

    def finish():
        for block in range(block_count):
            total = mixed_ref[block, HEAD_SIZE : HEAD_SIZE + 1, :]
            out_ref[block * HEAD_SIZE : (block + 1) * HEAD_SIZE, :] = (
                mixed_ref[block, 0:HEAD_SIZE, :] * (1.0 / total)
            ).astype(jnp.bfloat16)
            lse_ref[block : block + 1, :] = high_ref[block, 0:1, :] * LOG2_SCALE + jnp.log2(total)
        out_ref[block_count * HEAD_SIZE :, :] = lse_pieces(lse_ref[0:block_count, :], block_count)

    def attempt(trial, carry):
        @pl.when((trial == 0) | (redo_ref[0] > 0))
        def _():
            for piece, (step, chunks) in enumerate(images):
                base = step * (block_count + 1)
                count = table_ref[base]
                if piece == 0:
                    held = before
                    for block in range(block_count):
                        seen = functools.reduce(
                            jnp.logical_or,
                            [(count > index) & (table_ref[base + 1 + index] == block) for index in range(block_count)],
                        )

                        @pl.when(jnp.logical_not(seen))
                        def _(block=block):
                            if held is None:
                                high_ref[block] = jnp.full(high_ref.shape[1:], LOWEST, jnp.float32)
                                mixed_ref[block] = jnp.zeros(mixed_ref.shape[1:], jnp.float32)
                            else:
                                high_ref[block] = held[0][block]
                                mixed_ref[block] = held[1][block]

                else:
                    held = (high_ref, mixed_ref)

                def pair_step(pair, carry, chunks=chunks, base=base, count=count, held=held):
                    blocks = [table_ref[base + 1 + 2 * pair], table_ref[base + jnp.minimum(2 * pair + 2, count)]]
                    fold_pair(blocks, chunks, trial > 0, held)
                    return carry

                lax.fori_loop(0, (count + 1) // 2, pair_step, 0)
            most = functools.reduce(
                jnp.maximum, [mixed_ref[block, HEAD_SIZE : HEAD_SIZE + 1, :] for block in range(block_count)]
            )
            if last:
                finish()
            redo_ref[0] = 1 - jnp.min((most <= MOST_SUM).astype(jnp.int32))

        return carry

    lax.fori_loop(0, 2, attempt, 0)


def cross_part(table, queries, images, last, before=()):
    tokens, columns = queries[0].shape
    block_count = tokens // MASK_BLOCK_TOKENS
    rows = columns // HEAD_SIZE * MASK_BLOCK_TOKENS
    state = [(block_count, 8, rows), (block_count, MIXED_ROWS, rows)]
    scratch = [pltpu.VMEM((8, 2 * rows), jnp.float32), pltpu.SMEM((1,), jnp.int32)]
    if last:
        out_shape = jax.ShapeDtypeStruct((block_count * HEAD_SIZE + lse_rows(block_count), rows), jnp.bfloat16)
        scratch = [pltpu.VMEM(shape, jnp.float32) for shape in state] + scratch
        scratch = [pltpu.VMEM((-(-block_count // 8) * 8, rows), jnp.float32)] + scratch
    else:
        out_shape = tuple(jax.ShapeDtypeStruct(shape, jnp.float32) for shape in state)
    layout = tuple((step, tuple(count for _, count in parts)) for step, parts in images)
    arrays = [part for _, parts in images for part, _ in parts]
    return pl.pallas_call(
        functools.partial(cross_kernel, layout, bool(before), last, len(queries)),
        out_shape=out_shape,
        in_specs=[SMEM] + [VMEM] * (len(queries) + len(arrays) + len(before)),
        out_specs=VMEM if last else (VMEM,) * 2,
        scratch_shapes=scratch,
        compiler_params=pltpu.CompilerParams(vmem_limit_bytes=VMEM_LIMIT),
        cost_estimate=MUCH,
        name="cross_last" if last else "cross_first",
    )(table, *queries, *arrays, *before)


def lse_of(ref, block_count):
    tail = ref[block_count * HEAD_SIZE :, :].astype(jnp.float32)
    return tail[0:block_count] + tail[block_count : 2 * block_count] + tail[2 * block_count : 3 * block_count]


def lse_pieces(lse, block_count):
    first = lse.astype(jnp.bfloat16).astype(jnp.float32)
    second = (lse - first).astype(jnp.bfloat16).astype(jnp.float32)
    pieces = [first, second, lse - first - second]
    spare = lse_rows(block_count) - 3 * block_count
    if spare:
        pieces.append(jnp.zeros((spare, lse.shape[1]), jnp.float32))
    return jnp.concatenate(pieces, axis=0).astype(jnp.bfloat16)


def mixed_block(part_refs, weights, block):
    at = slice(block * HEAD_SIZE, (block + 1) * HEAD_SIZE)
    terms = [weight[block : block + 1, :] * ref[at, :].astype(jnp.float32) for ref, weight in zip(part_refs, weights)]
    return functools.reduce(jnp.add, terms)


def combine_kernel(held, last, *refs):
    if held:
        mixed_ref, lse_ref, part_ref, *out_refs = refs
        block_count = lse_ref.shape[0]
        lse = [lse_ref[...], lse_of(part_ref, block_count)]
    else:
        mixed_ref, part_ref, *out_refs = refs
        block_count = packed_blocks(part_ref.shape[0])
        lse = [lse_of(mixed_ref, block_count), lse_of(part_ref, block_count)]
    highest = functools.reduce(jnp.maximum, lse)
    weights = [jnp.exp2(one - highest) for one in lse]
    total = functools.reduce(jnp.add, weights)
    weights = [one / total for one in weights]
    for block in range(block_count):
        mixed = mixed_block((mixed_ref, part_ref), weights, block)
        if last:
            store_heads(out_refs[0], block, mixed)
        else:
            out_refs[0][block * HEAD_SIZE : (block + 1) * HEAD_SIZE, :] = mixed
    if not last:
        out_refs[1][...] = highest + jnp.log2(total)


def store_heads(out_ref, block, mixed):
    at = slice(block * MASK_BLOCK_TOKENS, (block + 1) * MASK_BLOCK_TOKENS)
    for head in range(out_ref.shape[1] // HEAD_SIZE):
        piece = mixed[:, head * MASK_BLOCK_TOKENS : (head + 1) * MASK_BLOCK_TOKENS]
        out_ref[at, head * HEAD_SIZE : (head + 1) * HEAD_SIZE] = piece.T.astype(jnp.bfloat16)


def combined(so_far, part, shape, last):
    tokens, columns = shape
    held = len(so_far) == 2
    block_count = tokens // MASK_BLOCK_TOKENS
    rows = columns // HEAD_SIZE * MASK_BLOCK_TOKENS
    if last:
        out_shape = jax.ShapeDtypeStruct(shape, jnp.bfloat16)
    else:
        out_shape = (
            jax.ShapeDtypeStruct((block_count * HEAD_SIZE, rows), jnp.float32),
            jax.ShapeDtypeStruct((block_count, rows), jnp.float32),
        )
    return pl.pallas_call(
        functools.partial(combine_kernel, held, last),
        out_shape=out_shape,
        in_specs=[VMEM] * (len(so_far) + 1),
        out_specs=VMEM if last else (VMEM,) * 2,
        compiler_params=pltpu.CompilerParams(vmem_limit_bytes=VMEM_LIMIT),
        cost_estimate=MUCH,
        name="combine_last" if last else "combine",
    )(*so_far, part)


def pair_queries(q_ref, first, blocks):
    return jnp.concatenate(
        [
            stacked_heads(q_ref[block * MASK_BLOCK_TOKENS : (block + 1) * MASK_BLOCK_TOKENS, :])
            for block in range(first, first + blocks)
        ],
        axis=0,
    )


def self_first_kernel(group, q_ref, text_ref, high_ref, mixed_ref, value_ref):
    tokens, columns = q_ref.shape
    rows = columns // HEAD_SIZE * MASK_BLOCK_TOKENS
    value_ref[...] = text_ref[:, HEAD_SIZE:].T
    for index in range(tokens // MASK_BLOCK_TOKENS // group):
        first = index * group
        start, stop = first * MASK_BLOCK_TOKENS, (first + group) * MASK_BLOCK_TOKENS
        scores = nt_dot(text_ref[0:stop, 0:HEAD_SIZE], pair_queries(q_ref, first, group))
        tail = scores[start:, :]
        key_id = lax.broadcasted_iota(jnp.int32, tail.shape, 0)
        column = lax.broadcasted_iota(jnp.int32, tail.shape, 1)
        query_id = column // rows * MASK_BLOCK_TOKENS + column % MASK_BLOCK_TOKENS
        tail = jnp.where(key_id <= query_id, tail, LOWEST)
        scores = jnp.concatenate([scores[:start, :], tail], axis=0) if start else tail
        high = jnp.full((1, group * rows), LOWEST, jnp.float32)
        mixed = jnp.zeros((MIXED_ROWS, group * rows), jnp.float32)
        high, mixed = fold(high, mixed, scores, value_ref[:, 0:stop], True)
        high_ref[index] = jnp.broadcast_to(high, high_ref.shape[1:])
        mixed_ref[index] = mixed


def self_last_kernel(group, pieces, position_ref, q_ref, high_ref, mixed_ref, *refs):
    texts = refs[:pieces]
    out_ref, value_ref, new_high_ref, new_mixed_ref = refs[pieces:]
    rows = q_ref.shape[1] // HEAD_SIZE * MASK_BLOCK_TOKENS
    new_high_ref[...] = high_ref[...]
    new_mixed_ref[...] = mixed_ref[...]
    for piece in range(pieces):

        @pl.when(position_ref[0] >= piece + 1)
        def _(piece=piece):
            value_ref[...] = texts[piece][:, HEAD_SIZE:].T
            for index in range(high_ref.shape[0]):
                scores = nt_dot(texts[piece][:, 0:HEAD_SIZE], pair_queries(q_ref, index * group, group))
                high, mixed = fold(new_high_ref[index, 0:1, :], new_mixed_ref[index], scores, value_ref[...], True)
                new_high_ref[index] = jnp.broadcast_to(high, high_ref.shape[1:])
                new_mixed_ref[index] = mixed

    for index in range(high_ref.shape[0]):
        total = new_mixed_ref[index, HEAD_SIZE : HEAD_SIZE + 1, :]
        mixed = new_mixed_ref[index, 0:HEAD_SIZE, :] / total
        for block in range(group):
            store_heads(out_ref, index * group + block, mixed[:, block * rows : (block + 1) * rows])


def self_first(queries, text):
    tokens, columns = queries.shape
    block_count = tokens // MASK_BLOCK_TOKENS
    group = 1 if block_count % 2 else 2
    width = group * columns // HEAD_SIZE * MASK_BLOCK_TOKENS
    return pl.pallas_call(
        functools.partial(self_first_kernel, group),
        out_shape=(
            jax.ShapeDtypeStruct((block_count // group, 8, width), jnp.float32),
            jax.ShapeDtypeStruct((block_count // group, MIXED_ROWS, width), jnp.float32),
        ),
        in_specs=[VMEM] * 2,
        out_specs=(VMEM,) * 2,
        scratch_shapes=[pltpu.VMEM((HEAD_SIZE, tokens), jnp.bfloat16)],
        compiler_params=pltpu.CompilerParams(vmem_limit_bytes=VMEM_LIMIT),
        cost_estimate=LITTLE,
        name="self_first",
    )(queries, text)


def self_last(position, queries, state, texts):
    tokens, columns = queries.shape
    group = tokens // MASK_BLOCK_TOKENS // state[0].shape[0]
    return pl.pallas_call(
        functools.partial(self_last_kernel, group, len(texts)),
        out_shape=jax.ShapeDtypeStruct((tokens, columns), jnp.bfloat16),
        in_specs=[SMEM] + [VMEM] * (3 + len(texts)),
        out_specs=VMEM,
        scratch_shapes=[pltpu.VMEM((HEAD_SIZE, tokens), jnp.bfloat16)]
        + [pltpu.VMEM(one.shape, jnp.float32) for one in state],
        compiler_params=pltpu.CompilerParams(vmem_limit_bytes=VMEM_LIMIT),
        cost_estimate=LITTLE,
        name="self_last",
    )(position, queries, *state, *texts)


def shifted(value, axis, steps):
    count = lax.axis_size(axis)
    return lax.ppermute(value, axis, [(source, (source + steps) % count) for source in range(count)])


def swapped(value, axis, bits):
    return lax.ppermute(value, axis, [(source, source ^ bits) for source in range(lax.axis_size(axis))])


def after(value, earlier):
    return lax.optimization_barrier((value, earlier))[0]


def per_device(
    self_queries, text_kv, cross_queries, image_kv, block_images, image_owner
):
    rows = self_queries.shape[0]
    key_count = image_kv.shape[2]
    cycle = lax.axis_size("blk")
    ring = lax.axis_size("enc")
    place = lax.axis_index("enc")
    inside = ((place > 0) & (place < ring - 1)).astype(jnp.int32)[None]
    position = lax.axis_index("blk").astype(jnp.int32)[None]

    halves = halves_of(key_count)
    images = [[(prepare(image_kv[0, :, start:stop, :]), stop - start) for start, stop in halves]]
    for _ in range(1, cycle):
        images.append([(shifted(part, "blk", 1), count) for part, count in images[-1]])
    images = list(enumerate(images))
    if ring == 4:
        queries = {step: [swapped(cross_queries, "enc", step)] for step in (2, 1)}
        middle = lax.ppermute(cross_queries, "enc", [(0, 0), (1, 2), (2, 1), (3, 3)])
        queries[3] = [middle, swapped(queries[2][0], "enc", 1)]
    else:
        queries = {step: [shifted(cross_queries, "enc", ring - step)] for step in range(1, ring)}
    queries[0] = [cross_queries]
    table = seen_table(position, inside, block_images, image_owner)

    latest = [None]

    def in_turn(arrays):
        return arrays if latest[0] is None else [after(one, latest[0]) for one in arrays]

    def begun(step, given):
        latest[0] = cross_part(table, in_turn(queries[step]), given, False)
        return latest[0]

    def finished(step, given, state=()):
        latest[0] = cross_part(table, in_turn(queries[step]), given, True, state)
        return latest[0]

    split = cycle > 1
    own = begun(0, images[:1]) if split else ()
    steps = [2, 3, 1] if ring == 4 else list(range(1, ring))
    early, late = (), images
    if split:
        halfway = (1, images[1][1][:-1])
        early = begun(steps[0], images[:1] + ([halfway] if halfway[1] else []))
        late = [(1, images[1][1][-1:])] + images[2:]
    received, texts = [], []
    for step in steps:
        part = finished(step, late, early) if step == steps[0] else finished(step, images)
        if not texts and (step != steps[0] or len(steps) == 1):
            texts.append(after(text_kv, part).reshape(rows, 2 * HEAD_SIZE))
            for _ in range(1, cycle):
                texts.append(shifted(texts[-1], "blk", 1))
        received.append(swapped(part, "enc", step) if ring == 4 else shifted(part, "enc", step))
    own_part = finished(0, images[1:] if split else images, own)
    self_state = latest[0] = self_first(in_turn([self_queries])[0], texts[0])
    self_out = latest[0] = self_last(position, in_turn([self_queries])[0], self_state, texts[1:])
    so_far = in_turn([own_part])
    for index, part in enumerate(received):
        so_far = combined(so_far, part, cross_queries.shape, index + 1 == len(received))
    return (self_out, so_far)


def solution(mesh):
    placed = (
        P("blk", ("tp", "enc")),
        P("blk", None, "tp"),
        P("blk", ("tp", "enc")),
        P("blk", None, "enc", "tp"),
        P("blk", None),
        P(),
    )
    return jax.shard_map(
        per_device,
        mesh=mesh,
        in_specs=placed,
        out_specs=(P("blk", ("tp", "enc")), P("blk", ("tp", "enc"))),
        check_vma=False,
    )
```

```python
import functools
import math

import jax
import jax.numpy as jnp
from jax import lax
from jax.experimental import pallas as pl
from jax.experimental.pallas import tpu as pltpu
from jax.sharding import PartitionSpec as P

HEAD_SIZE = 128
MASK_BLOCK_TOKENS = 128
LANES = 128
LOWEST = -1e30
MIXED_ROWS = HEAD_SIZE + 16
SHIFT_KEYS = 256
MOST_SUM = 2.0**100
LOG2_SCALE = math.log2(math.e) / math.sqrt(HEAD_SIZE)
VMEM_LIMIT = 48 * 1024 * 1024

LITTLE = pl.CostEstimate(flops=0, bytes_accessed=1024, transcendentals=0)
MUCH = pl.CostEstimate(flops=2_000_000_000, bytes_accessed=1024, transcendentals=0)

VMEM = pl.BlockSpec(memory_space=pltpu.VMEM)
SMEM = pl.BlockSpec(memory_space=pltpu.SMEM)


def padded(count):
    return -(-count // LANES) * LANES


def nt_dot(a, b):
    return lax.dot_general(a, b, (((1,), (1,)), ((), ())), preferred_element_type=jnp.float32)


def at_block(block, size=MASK_BLOCK_TOKENS):
    return pl.ds(pl.multiple_of(block * size, size), size)


def stacked_heads(rows):
    heads = rows.shape[1] // HEAD_SIZE
    return jnp.concatenate([rows[:, h * HEAD_SIZE : (h + 1) * HEAD_SIZE] for h in range(heads)], axis=0)


def scaled_pieces(queries):
    scaled = queries.astype(jnp.float32) * LOG2_SCALE
    first = scaled.astype(jnp.bfloat16)
    rest = (scaled - first.astype(jnp.float32)).astype(jnp.bfloat16)
    return jnp.concatenate([first, rest], axis=1)


def with_ones(value_t):
    shape = (MIXED_ROWS - HEAD_SIZE, value_t.shape[1])
    ones = (lax.broadcasted_iota(jnp.int32, shape, 0) == 0).astype(jnp.bfloat16)
    return jnp.concatenate([value_t, ones], axis=0)


def fold(high, mixed, scores, value_t, exact):
    seen = scores if exact else scores[0 : min(SHIFT_KEYS, scores.shape[0]), :]
    new_high = jnp.maximum(high, jnp.max(seen, axis=0, keepdims=True))
    weights = jnp.exp2(scores * LOG2_SCALE - new_high * LOG2_SCALE).astype(jnp.bfloat16)
    fading = jnp.exp2((high - new_high) * LOG2_SCALE)
    mixed = mixed * fading + jnp.dot(with_ones(value_t), weights, preferred_element_type=jnp.float32)
    return new_high, mixed


def prepare_kernel(kv_ref, out_ref):
    count = kv_ref.shape[1]
    whole = count // LANES * LANES
    rest = count - whole
    out_ref[0, 0:whole, :] = kv_ref[0, 0:whole, :]
    for at in range(0, whole, LANES):
        out_ref[1, at : at + LANES, :] = kv_ref[1, at : at + LANES, :].T
    if rest:
        empty = jnp.zeros((LANES - rest, HEAD_SIZE), jnp.float32)
        tail_key = jnp.concatenate([kv_ref[0, whole:count, :].astype(jnp.float32), empty], axis=0)
        tail_value = jnp.concatenate([kv_ref[1, whole:count, :].astype(jnp.float32), empty], axis=0)
        out_ref[0, whole : whole + LANES, :] = tail_key.astype(jnp.bfloat16)
        out_ref[1, whole : whole + LANES, :] = tail_value.T.astype(jnp.bfloat16)


def prepare(kv):
    return pl.pallas_call(
        prepare_kernel,
        out_shape=jax.ShapeDtypeStruct((2, padded(kv.shape[1]), HEAD_SIZE), jnp.bfloat16),
        in_specs=[VMEM],
        out_specs=VMEM,
        compiler_params=pltpu.CompilerParams(vmem_limit_bytes=VMEM_LIMIT),
        cost_estimate=LITTLE,
        name="prepare",
    )(kv)


def lse_rows(block_count):
    return -(-3 * block_count // 16) * 16


def packed_blocks(rows):
    return next(count for count in range(1, rows) if count * HEAD_SIZE + lse_rows(count) == rows)


def table_kernel(position_ref, inside_ref, images_ref, owner_ref, table_ref):
    slots, block_count = images_ref.shape
    for piece in range(slots):
        slot = lax.rem(position_ref[0] + (slots - piece), slots)
        base = piece * (block_count + 1)
        count = jnp.int32(0)
        for block in range(block_count):
            table_ref[base + 1 + block] = jnp.int32(0)
        for block in range(block_count):
            seen = lax.fori_loop(
                0,
                slots,
                lambda image, sum, block=block, slot=slot: sum
                + jnp.where(owner_ref[image] == slot, images_ref[image, block], 0),
                jnp.int32(0),
            )

            @pl.when(seen > 0)
            def _(base=base, block=block, count=count):
                table_ref[base + 1 + count] = jnp.int32(block)

            count = count + jnp.where(seen > 0, 1, 0)
        table_ref[base] = count
    table_ref[slots * (block_count + 1)] = inside_ref[0]


def seen_table(position, inside, block_images, image_owner):
    block_count, slots = block_images.shape
    return pl.pallas_call(
        table_kernel,
        out_shape=jax.ShapeDtypeStruct((slots * (block_count + 1) + 1,), jnp.int32),
        in_specs=[SMEM] * 4,
        out_specs=SMEM,
        name="seen_table",
    )(position, inside, block_images.T, image_owner)


def chunks_of(width):
    half = width // LANES // 2 * LANES
    return [(0, half), (half, width)] if half else [(0, width)]


def cross_kernel(key_count, pieces, offset, last, parts, table_ref, *refs):
    q_refs, images, refs = refs[:parts], refs[parts : parts + pieces], refs[parts + pieces :]
    if offset:
        before, refs = refs[:2], refs[2:]
    if last:
        out_ref, lse_ref, high_ref, mixed_ref, peak_ref, redo_ref = refs
    else:
        high_ref, mixed_ref, peak_ref, redo_ref = refs
    block_count = q_refs[0].shape[0] // MASK_BLOCK_TOKENS
    rows = q_refs[0].shape[1] // HEAD_SIZE * MASK_BLOCK_TOKENS
    peak_ref[...] = jnp.full_like(peak_ref, LOWEST)
    redo_ref[0] = jnp.int32(0)

    def fold_pair(blocks, image, exact, held):
        width = image.shape[1]
        queries = [q_refs[0][at_block(block), :] for block in blocks]
        if parts > 1:
            first = table_ref[table_ref.shape[0] - 1] > 0
            queries = [jnp.where(first, one, q_refs[1][at_block(block), :]) for one, block in zip(queries, blocks)]
        queries = scaled_pieces(jnp.concatenate([stacked_heads(one) for one in queries], axis=0))
        chunks = chunks_of(width)

        def scores_of(start, stop):
            keys = image[0, start:stop, :]
            scores = nt_dot(jnp.concatenate([keys, keys], axis=1), queries)
            if stop > key_count:
                body = stop - start - LANES
                tail = scores[body:, :]
                key_id = start + body + lax.broadcasted_iota(jnp.int32, tail.shape, 0)
                tail = jnp.where(key_id < key_count, tail, LOWEST)
                scores = jnp.concatenate([scores[:body, :], tail], axis=0) if body else tail
            return scores

        @pl.when(exact)
        def _():
            tops = [jnp.max(scores_of(*chunk), axis=0, keepdims=True) for chunk in chunks]
            peak_ref[0:1, :] = functools.reduce(jnp.maximum, tops)

        if held is None:
            high = jnp.full((1, 2 * rows), LOWEST, jnp.float32)
            mixed = jnp.zeros((MIXED_ROWS, 2 * rows), jnp.float32)
        else:
            high = jnp.concatenate([held[0][block][0:1] for block in blocks], axis=1)
            mixed = jnp.concatenate([held[1][block] for block in blocks], axis=1)
        scores = scores_of(*chunks[0])
        seen = jnp.max(scores[0 : min(SHIFT_KEYS, scores.shape[0])], axis=0, keepdims=True)
        new_high = jnp.maximum(jnp.maximum(high, seen), peak_ref[0:1, :])
        mixed = mixed * jnp.exp2(high - new_high)
        for index, (start, stop) in enumerate(chunks):
            following = scores_of(*chunks[index + 1]) if index + 1 < len(chunks) else None
            weights = jnp.exp2(scores - new_high).astype(jnp.bfloat16)
            value_t = jnp.concatenate([image[1, c : c + LANES, :] for c in range(start, stop, LANES)], axis=1)
            mixed = mixed + jnp.dot(with_ones(value_t), weights, preferred_element_type=jnp.float32)
            scores = following
        for index, block in enumerate(blocks):
            own = slice(index * rows, (index + 1) * rows)
            high_ref[block] = jnp.broadcast_to(new_high[:, own], high_ref.shape[1:])
            mixed_ref[block] = mixed[:, own]

    def finish():
        for block in range(block_count):
            total = mixed_ref[block, HEAD_SIZE : HEAD_SIZE + 1, :]
            out_ref[block * HEAD_SIZE : (block + 1) * HEAD_SIZE, :] = (
                mixed_ref[block, 0:HEAD_SIZE, :] * (1.0 / total)
            ).astype(jnp.bfloat16)
            lse_ref[block : block + 1, :] = high_ref[block, 0:1, :] + jnp.log2(total)
        out_ref[block_count * HEAD_SIZE :, :] = lse_pieces(lse_ref[0:block_count, :], block_count)

    def attempt(trial, carry):
        @pl.when((trial == 0) | (redo_ref[0] > 0))
        def _():
            for piece in range(pieces):
                base = (offset + piece) * (block_count + 1)
                count = table_ref[base]
                if piece == 0:
                    held = before if offset else None
                    for block in range(block_count):
                        seen = functools.reduce(
                            jnp.logical_or,
                            [(count > index) & (table_ref[base + 1 + index] == block) for index in range(block_count)],
                        )

                        @pl.when(jnp.logical_not(seen))
                        def _(block=block):
                            if held is None:
                                high_ref[block] = jnp.full(high_ref.shape[1:], LOWEST, jnp.float32)
                                mixed_ref[block] = jnp.zeros(mixed_ref.shape[1:], jnp.float32)
                            else:
                                high_ref[block] = held[0][block]
                                mixed_ref[block] = held[1][block]

                else:
                    held = (high_ref, mixed_ref)

                def pair_step(pair, carry, piece=piece, base=base, count=count, held=held):
                    blocks = [table_ref[base + 1 + 2 * pair], table_ref[base + jnp.minimum(2 * pair + 2, count)]]
                    fold_pair(blocks, images[piece], trial > 0, held)
                    return carry

                lax.fori_loop(0, (count + 1) // 2, pair_step, 0)
            most = functools.reduce(
                jnp.maximum, [mixed_ref[block, HEAD_SIZE : HEAD_SIZE + 1, :] for block in range(block_count)]
            )
            if last:
                finish()
            redo_ref[0] = 1 - jnp.min((most <= MOST_SUM).astype(jnp.int32))

        return carry

    lax.fori_loop(0, 2, attempt, 0)


def cross_part(table, queries, images, key_count, offset, last, before=()):
    tokens, columns = queries[0].shape
    block_count = tokens // MASK_BLOCK_TOKENS
    rows = columns // HEAD_SIZE * MASK_BLOCK_TOKENS
    state = [(block_count, 8, rows), (block_count, MIXED_ROWS, rows)]
    scratch = [pltpu.VMEM((8, 2 * rows), jnp.float32), pltpu.SMEM((1,), jnp.int32)]
    if last:
        out_shape = jax.ShapeDtypeStruct((block_count * HEAD_SIZE + lse_rows(block_count), rows), jnp.bfloat16)
        scratch = [pltpu.VMEM(shape, jnp.float32) for shape in state] + scratch
        scratch = [pltpu.VMEM((-(-block_count // 8) * 8, rows), jnp.float32)] + scratch
    else:
        out_shape = tuple(jax.ShapeDtypeStruct(shape, jnp.float32) for shape in state)
    return pl.pallas_call(
        functools.partial(cross_kernel, key_count, len(images), offset, last, len(queries)),
        out_shape=out_shape,
        in_specs=[SMEM] + [VMEM] * (len(queries) + len(images) + len(before)),
        out_specs=VMEM if last else (VMEM,) * 2,
        scratch_shapes=scratch,
        compiler_params=pltpu.CompilerParams(vmem_limit_bytes=VMEM_LIMIT),
        cost_estimate=MUCH,
        name="cross_last" if last else "cross_first",
    )(table, *queries, *images, *before)


def lse_of(ref, block_count):
    tail = ref[block_count * HEAD_SIZE :, :].astype(jnp.float32)
    return tail[0:block_count] + tail[block_count : 2 * block_count] + tail[2 * block_count : 3 * block_count]


def lse_pieces(lse, block_count):
    first = lse.astype(jnp.bfloat16).astype(jnp.float32)
    second = (lse - first).astype(jnp.bfloat16).astype(jnp.float32)
    pieces = [first, second, lse - first - second]
    spare = lse_rows(block_count) - 3 * block_count
    if spare:
        pieces.append(jnp.zeros((spare, lse.shape[1]), jnp.float32))
    return jnp.concatenate(pieces, axis=0).astype(jnp.bfloat16)


def mixed_block(part_refs, weights, block):
    at = slice(block * HEAD_SIZE, (block + 1) * HEAD_SIZE)
    terms = [weight[block : block + 1, :] * ref[at, :].astype(jnp.float32) for ref, weight in zip(part_refs, weights)]
    return functools.reduce(jnp.add, terms)


def combine_kernel(held, last, *refs):
    if held:
        mixed_ref, lse_ref, part_ref, *out_refs = refs
        block_count = lse_ref.shape[0]
        lse = [lse_ref[...], lse_of(part_ref, block_count)]
    else:
        mixed_ref, part_ref, *out_refs = refs
        block_count = packed_blocks(part_ref.shape[0])
        lse = [lse_of(mixed_ref, block_count), lse_of(part_ref, block_count)]
    highest = functools.reduce(jnp.maximum, lse)
    weights = [jnp.exp2(one - highest) for one in lse]
    total = functools.reduce(jnp.add, weights)
    weights = [one / total for one in weights]
    for block in range(block_count):
        mixed = mixed_block((mixed_ref, part_ref), weights, block)
        if last:
            store_heads(out_refs[0], block, mixed)
        else:
            out_refs[0][block * HEAD_SIZE : (block + 1) * HEAD_SIZE, :] = mixed
    if not last:
        out_refs[1][...] = highest + jnp.log2(total)


def store_heads(out_ref, block, mixed):
    at = slice(block * MASK_BLOCK_TOKENS, (block + 1) * MASK_BLOCK_TOKENS)
    for head in range(out_ref.shape[1] // HEAD_SIZE):
        piece = mixed[:, head * MASK_BLOCK_TOKENS : (head + 1) * MASK_BLOCK_TOKENS]
        out_ref[at, head * HEAD_SIZE : (head + 1) * HEAD_SIZE] = piece.T.astype(jnp.bfloat16)


def combined(so_far, part, shape, last):
    tokens, columns = shape
    held = len(so_far) == 2
    block_count = tokens // MASK_BLOCK_TOKENS
    rows = columns // HEAD_SIZE * MASK_BLOCK_TOKENS
    if last:
        out_shape = jax.ShapeDtypeStruct(shape, jnp.bfloat16)
    else:
        out_shape = (
            jax.ShapeDtypeStruct((block_count * HEAD_SIZE, rows), jnp.float32),
            jax.ShapeDtypeStruct((block_count, rows), jnp.float32),
        )
    return pl.pallas_call(
        functools.partial(combine_kernel, held, last),
        out_shape=out_shape,
        in_specs=[VMEM] * (len(so_far) + 1),
        out_specs=VMEM if last else (VMEM,) * 2,
        compiler_params=pltpu.CompilerParams(vmem_limit_bytes=VMEM_LIMIT),
        cost_estimate=MUCH,
        name="combine_last" if last else "combine",
    )(*so_far, part)


def pair_queries(q_ref, first, blocks):
    return jnp.concatenate(
        [
            stacked_heads(q_ref[block * MASK_BLOCK_TOKENS : (block + 1) * MASK_BLOCK_TOKENS, :])
            for block in range(first, first + blocks)
        ],
        axis=0,
    )


def self_first_kernel(group, q_ref, text_ref, high_ref, mixed_ref, value_ref):
    tokens, columns = q_ref.shape
    rows = columns // HEAD_SIZE * MASK_BLOCK_TOKENS
    value_ref[...] = text_ref[:, HEAD_SIZE:].T
    for index in range(tokens // MASK_BLOCK_TOKENS // group):
        first = index * group
        start, stop = first * MASK_BLOCK_TOKENS, (first + group) * MASK_BLOCK_TOKENS
        scores = nt_dot(text_ref[0:stop, 0:HEAD_SIZE], pair_queries(q_ref, first, group))
        tail = scores[start:, :]
        key_id = lax.broadcasted_iota(jnp.int32, tail.shape, 0)
        column = lax.broadcasted_iota(jnp.int32, tail.shape, 1)
        query_id = column // rows * MASK_BLOCK_TOKENS + column % MASK_BLOCK_TOKENS
        tail = jnp.where(key_id <= query_id, tail, LOWEST)
        scores = jnp.concatenate([scores[:start, :], tail], axis=0) if start else tail
        high = jnp.full((1, group * rows), LOWEST, jnp.float32)
        mixed = jnp.zeros((MIXED_ROWS, group * rows), jnp.float32)
        high, mixed = fold(high, mixed, scores, value_ref[:, 0:stop], True)
        high_ref[index] = jnp.broadcast_to(high, high_ref.shape[1:])
        mixed_ref[index] = mixed


def self_last_kernel(group, pieces, position_ref, q_ref, high_ref, mixed_ref, *refs):
    texts = refs[:pieces]
    out_ref, value_ref, new_high_ref, new_mixed_ref = refs[pieces:]
    rows = q_ref.shape[1] // HEAD_SIZE * MASK_BLOCK_TOKENS
    new_high_ref[...] = high_ref[...]
    new_mixed_ref[...] = mixed_ref[...]
    for piece in range(pieces):

        @pl.when(position_ref[0] >= piece + 1)
        def _(piece=piece):
            value_ref[...] = texts[piece][:, HEAD_SIZE:].T
            for index in range(high_ref.shape[0]):
                scores = nt_dot(texts[piece][:, 0:HEAD_SIZE], pair_queries(q_ref, index * group, group))
                high, mixed = fold(new_high_ref[index, 0:1, :], new_mixed_ref[index], scores, value_ref[...], True)
                new_high_ref[index] = jnp.broadcast_to(high, high_ref.shape[1:])
                new_mixed_ref[index] = mixed

    for index in range(high_ref.shape[0]):
        total = new_mixed_ref[index, HEAD_SIZE : HEAD_SIZE + 1, :]
        mixed = new_mixed_ref[index, 0:HEAD_SIZE, :] / total
        for block in range(group):
            store_heads(out_ref, index * group + block, mixed[:, block * rows : (block + 1) * rows])


def self_first(queries, text):
    tokens, columns = queries.shape
    block_count = tokens // MASK_BLOCK_TOKENS
    group = 1 if block_count % 2 else 2
    width = group * columns // HEAD_SIZE * MASK_BLOCK_TOKENS
    return pl.pallas_call(
        functools.partial(self_first_kernel, group),
        out_shape=(
            jax.ShapeDtypeStruct((block_count // group, 8, width), jnp.float32),
            jax.ShapeDtypeStruct((block_count // group, MIXED_ROWS, width), jnp.float32),
        ),
        in_specs=[VMEM] * 2,
        out_specs=(VMEM,) * 2,
        scratch_shapes=[pltpu.VMEM((HEAD_SIZE, tokens), jnp.bfloat16)],
        compiler_params=pltpu.CompilerParams(vmem_limit_bytes=VMEM_LIMIT),
        cost_estimate=LITTLE,
        name="self_first",
    )(queries, text)


def self_last(position, queries, state, texts):
    tokens, columns = queries.shape
    group = tokens // MASK_BLOCK_TOKENS // state[0].shape[0]
    return pl.pallas_call(
        functools.partial(self_last_kernel, group, len(texts)),
        out_shape=jax.ShapeDtypeStruct((tokens, columns), jnp.bfloat16),
        in_specs=[SMEM] + [VMEM] * (3 + len(texts)),
        out_specs=VMEM,
        scratch_shapes=[pltpu.VMEM((HEAD_SIZE, tokens), jnp.bfloat16)]
        + [pltpu.VMEM(one.shape, jnp.float32) for one in state],
        compiler_params=pltpu.CompilerParams(vmem_limit_bytes=VMEM_LIMIT),
        cost_estimate=LITTLE,
        name="self_last",
    )(position, queries, *state, *texts)


def shifted(value, axis, steps):
    count = lax.axis_size(axis)
    return lax.ppermute(value, axis, [(source, (source + steps) % count) for source in range(count)])


def swapped(value, axis, bits):
    return lax.ppermute(value, axis, [(source, source ^ bits) for source in range(lax.axis_size(axis))])


def after(value, earlier):
    return lax.optimization_barrier((value, earlier))[0]


def per_device(
    self_queries, text_kv, cross_queries, image_kv, block_images, image_owner
):
    rows = self_queries.shape[0]
    key_count = image_kv.shape[2]
    cycle = lax.axis_size("blk")
    ring = lax.axis_size("enc")
    place = lax.axis_index("enc")
    inside = ((place > 0) & (place < ring - 1)).astype(jnp.int32)[None]
    position = lax.axis_index("blk").astype(jnp.int32)[None]

    images = [prepare(image_kv[0])]
    for _ in range(1, cycle):
        images.append(shifted(images[-1], "blk", 1))
    if ring == 4:
        queries = {step: [swapped(cross_queries, "enc", step)] for step in (2, 1)}
        middle = lax.ppermute(cross_queries, "enc", [(0, 0), (1, 2), (2, 1), (3, 3)])
        queries[3] = [middle, swapped(queries[2][0], "enc", 1)]
    else:
        queries = {step: [shifted(cross_queries, "enc", ring - step)] for step in range(1, ring)}
    queries[0] = [cross_queries]
    table = seen_table(position, inside, block_images, image_owner)

    latest = [None]

    def in_turn(arrays):
        return arrays if latest[0] is None else [after(one, latest[0]) for one in arrays]

    def begun(step):
        latest[0] = cross_part(table, in_turn(queries[step]), images[:1], key_count, 0, False)
        return latest[0]

    def finished(step, state=None):
        used = images if state is None else images[1:]
        before = () if state is None else state
        offset = 0 if state is None else 1
        latest[0] = cross_part(table, in_turn(queries[step]), used, key_count, offset, True, before)
        return latest[0]

    split = cycle > 1
    own = begun(0) if split else None
    steps = [2, 3, 1] if ring == 4 else list(range(1, ring))
    states = {step: begun(step) for step in steps[:1]} if split else {}
    received, texts = [], []
    for step in steps:
        part = finished(step, states.get(step))
        if not texts:
            texts.append(after(text_kv, part).reshape(rows, 2 * HEAD_SIZE))
            for _ in range(1, cycle):
                texts.append(shifted(texts[-1], "blk", 1))
        received.append(swapped(part, "enc", step) if ring == 4 else shifted(part, "enc", step))
    own_part = finished(0, own)
    self_state = latest[0] = self_first(in_turn([self_queries])[0], texts[0])
    self_out = latest[0] = self_last(position, in_turn([self_queries])[0], self_state, texts[1:])
    so_far = in_turn([own_part])
    for index, part in enumerate(received):
        so_far = combined(so_far, part, cross_queries.shape, index + 1 == len(received))
    return (self_out, so_far)


def solution(mesh):
    placed = (
        P("blk", ("tp", "enc")),
        P("blk", None, "tp"),
        P("blk", ("tp", "enc")),
        P("blk", None, "enc", "tp"),
        P("blk", None),
        P(),
    )
    return jax.shard_map(
        per_device,
        mesh=mesh,
        in_specs=placed,
        out_specs=(P("blk", ("tp", "enc")), P("blk", ("tp", "enc"))),
        check_vma=False,
    )
```

```python
import functools
import math

import jax
import jax.numpy as jnp
from jax import lax
from jax.experimental import pallas as pl
from jax.experimental.pallas import tpu as pltpu
from jax.sharding import PartitionSpec as P

HEAD_SIZE = 128
MASK_BLOCK_TOKENS = 128
LANES = 128
LOWEST = -1e30
MIXED_ROWS = HEAD_SIZE + 16
SHIFT_KEYS = 256
MOST_SUM = 2.0**100
LOG2_SCALE = math.log2(math.e) / math.sqrt(HEAD_SIZE)
VMEM_LIMIT = 48 * 1024 * 1024

LITTLE = pl.CostEstimate(flops=0, bytes_accessed=1024, transcendentals=0)
MUCH = pl.CostEstimate(flops=2_000_000_000, bytes_accessed=1024, transcendentals=0)

VMEM = pl.BlockSpec(memory_space=pltpu.VMEM)
SMEM = pl.BlockSpec(memory_space=pltpu.SMEM)


def padded(count):
    return -(-count // LANES) * LANES


def nt_dot(a, b):
    return lax.dot_general(a, b, (((1,), (1,)), ((), ())), preferred_element_type=jnp.float32)


def at_block(block, size=MASK_BLOCK_TOKENS):
    return pl.ds(pl.multiple_of(block * size, size), size)


def stacked_heads(rows):
    heads = rows.shape[1] // HEAD_SIZE
    return jnp.concatenate([rows[:, h * HEAD_SIZE : (h + 1) * HEAD_SIZE] for h in range(heads)], axis=0)


def with_ones(value_t):
    shape = (MIXED_ROWS - HEAD_SIZE, value_t.shape[1])
    ones = (lax.broadcasted_iota(jnp.int32, shape, 0) == 0).astype(jnp.bfloat16)
    return jnp.concatenate([value_t, ones], axis=0)


def fold(high, mixed, scores, value_t, exact):
    seen = scores if exact else scores[0 : min(SHIFT_KEYS, scores.shape[0]), :]
    new_high = jnp.maximum(high, jnp.max(seen, axis=0, keepdims=True))
    weights = jnp.exp2(scores * LOG2_SCALE - new_high * LOG2_SCALE).astype(jnp.bfloat16)
    fading = jnp.exp2((high - new_high) * LOG2_SCALE)
    mixed = mixed * fading + jnp.dot(with_ones(value_t), weights, preferred_element_type=jnp.float32)
    return new_high, mixed


def prepare_kernel(kv_ref, out_ref):
    count = kv_ref.shape[1]
    whole = count // LANES * LANES
    rest = count - whole
    out_ref[0, 0:whole, :] = kv_ref[0, 0:whole, :]
    for at in range(0, whole, LANES):
        out_ref[1, at : at + LANES, :] = kv_ref[1, at : at + LANES, :].T
    if rest:
        empty = jnp.zeros((LANES - rest, HEAD_SIZE), jnp.float32)
        tail_key = jnp.concatenate([kv_ref[0, whole:count, :].astype(jnp.float32), empty], axis=0)
        tail_value = jnp.concatenate([kv_ref[1, whole:count, :].astype(jnp.float32), empty], axis=0)
        out_ref[0, whole : whole + LANES, :] = tail_key.astype(jnp.bfloat16)
        out_ref[1, whole : whole + LANES, :] = tail_value.T.astype(jnp.bfloat16)


def prepare(kv):
    return pl.pallas_call(
        prepare_kernel,
        out_shape=jax.ShapeDtypeStruct((2, padded(kv.shape[1]), HEAD_SIZE), jnp.bfloat16),
        in_specs=[VMEM],
        out_specs=VMEM,
        compiler_params=pltpu.CompilerParams(vmem_limit_bytes=VMEM_LIMIT),
        cost_estimate=LITTLE,
        name="prepare",
    )(kv)


def lse_rows(block_count):
    return -(-3 * block_count // 16) * 16


def packed_blocks(rows):
    return next(count for count in range(1, rows) if count * HEAD_SIZE + lse_rows(count) == rows)


def table_kernel(position_ref, inside_ref, images_ref, owner_ref, table_ref):
    slots, block_count = images_ref.shape
    for piece in range(slots):
        slot = lax.rem(position_ref[0] + (slots - piece), slots)
        base = piece * (block_count + 1)
        count = jnp.int32(0)
        for block in range(block_count):
            table_ref[base + 1 + block] = jnp.int32(0)
        for block in range(block_count):
            seen = lax.fori_loop(
                0,
                slots,
                lambda image, sum, block=block, slot=slot: sum
                + jnp.where(owner_ref[image] == slot, images_ref[image, block], 0),
                jnp.int32(0),
            )

            @pl.when(seen > 0)
            def _(base=base, block=block, count=count):
                table_ref[base + 1 + count] = jnp.int32(block)

            count = count + jnp.where(seen > 0, 1, 0)
        table_ref[base] = count
    table_ref[slots * (block_count + 1)] = inside_ref[0]


def seen_table(position, inside, block_images, image_owner):
    block_count, slots = block_images.shape
    return pl.pallas_call(
        table_kernel,
        out_shape=jax.ShapeDtypeStruct((slots * (block_count + 1) + 1,), jnp.int32),
        in_specs=[SMEM] * 4,
        out_specs=SMEM,
        name="seen_table",
    )(position, inside, block_images.T, image_owner)


def chunks_of(width):
    half = width // LANES // 2 * LANES
    return [(0, half), (half, width)] if half else [(0, width)]


def cross_kernel(key_count, pieces, offset, last, parts, table_ref, *refs):
    q_refs, images, refs = refs[:parts], refs[parts : parts + pieces], refs[parts + pieces :]
    if offset:
        before, refs = refs[:2], refs[2:]
    if last:
        out_ref, lse_ref, high_ref, mixed_ref, peak_ref, redo_ref = refs
    else:
        high_ref, mixed_ref, peak_ref, redo_ref = refs
    block_count = q_refs[0].shape[0] // MASK_BLOCK_TOKENS
    rows = q_refs[0].shape[1] // HEAD_SIZE * MASK_BLOCK_TOKENS
    peak_ref[...] = jnp.full_like(peak_ref, LOWEST)
    redo_ref[0] = jnp.int32(0)

    def fold_pair(blocks, image, exact, held):
        width = image.shape[1]
        queries = [q_refs[0][at_block(block), :] for block in blocks]
        if parts > 1:
            first = table_ref[table_ref.shape[0] - 1] > 0
            queries = [jnp.where(first, one, q_refs[1][at_block(block), :]) for one, block in zip(queries, blocks)]
        queries = jnp.concatenate([stacked_heads(one) for one in queries], axis=0)
        chunks = chunks_of(width)

        def scores_of(start, stop):
            scores = nt_dot(image[0, start:stop, :], queries)
            if stop > key_count:
                body = stop - start - LANES
                tail = scores[body:, :]
                key_id = start + body + lax.broadcasted_iota(jnp.int32, tail.shape, 0)
                tail = jnp.where(key_id < key_count, tail, LOWEST)
                scores = jnp.concatenate([scores[:body, :], tail], axis=0) if body else tail
            return scores

        @pl.when(exact)
        def _():
            tops = [jnp.max(scores_of(*chunk), axis=0, keepdims=True) for chunk in chunks]
            peak_ref[0:1, :] = functools.reduce(jnp.maximum, tops)

        if held is None:
            high = jnp.full((1, 2 * rows), LOWEST, jnp.float32)
            mixed = jnp.zeros((MIXED_ROWS, 2 * rows), jnp.float32)
        else:
            high = jnp.concatenate([held[0][block][0:1] for block in blocks], axis=1)
            mixed = jnp.concatenate([held[1][block] for block in blocks], axis=1)
        scores = scores_of(*chunks[0])
        seen = jnp.max(scores[0 : min(SHIFT_KEYS, scores.shape[0])], axis=0, keepdims=True)
        new_high = jnp.maximum(jnp.maximum(high, seen), peak_ref[0:1, :])
        shift = new_high * LOG2_SCALE
        mixed = mixed * jnp.exp2((high - new_high) * LOG2_SCALE)
        for index, (start, stop) in enumerate(chunks):
            following = scores_of(*chunks[index + 1]) if index + 1 < len(chunks) else None
            weights = jnp.exp2(scores * LOG2_SCALE - shift).astype(jnp.bfloat16)
            value_t = jnp.concatenate([image[1, c : c + LANES, :] for c in range(start, stop, LANES)], axis=1)
            mixed = mixed + jnp.dot(with_ones(value_t), weights, preferred_element_type=jnp.float32)
            scores = following
        for index, block in enumerate(blocks):
            own = slice(index * rows, (index + 1) * rows)
            high_ref[block] = jnp.broadcast_to(new_high[:, own], high_ref.shape[1:])
            mixed_ref[block] = mixed[:, own]

    def finish():
        for block in range(block_count):
            total = mixed_ref[block, HEAD_SIZE : HEAD_SIZE + 1, :]
            out_ref[block * HEAD_SIZE : (block + 1) * HEAD_SIZE, :] = (
                mixed_ref[block, 0:HEAD_SIZE, :] * (1.0 / total)
            ).astype(jnp.bfloat16)
            lse_ref[block : block + 1, :] = high_ref[block, 0:1, :] * LOG2_SCALE + jnp.log2(total)
        out_ref[block_count * HEAD_SIZE :, :] = lse_pieces(lse_ref[0:block_count, :], block_count)

    def attempt(trial, carry):
        @pl.when((trial == 0) | (redo_ref[0] > 0))
        def _():
            for piece in range(pieces):
                base = (offset + piece) * (block_count + 1)
                count = table_ref[base]
                if piece == 0:
                    held = before if offset else None
                    for block in range(block_count):
                        seen = functools.reduce(
                            jnp.logical_or,
                            [(count > index) & (table_ref[base + 1 + index] == block) for index in range(block_count)],
                        )

                        @pl.when(jnp.logical_not(seen))
                        def _(block=block):
                            if held is None:
                                high_ref[block] = jnp.full(high_ref.shape[1:], LOWEST, jnp.float32)
                                mixed_ref[block] = jnp.zeros(mixed_ref.shape[1:], jnp.float32)
                            else:
                                high_ref[block] = held[0][block]
                                mixed_ref[block] = held[1][block]

                else:
                    held = (high_ref, mixed_ref)

                def pair_step(pair, carry, piece=piece, base=base, count=count, held=held):
                    blocks = [table_ref[base + 1 + 2 * pair], table_ref[base + jnp.minimum(2 * pair + 2, count)]]
                    fold_pair(blocks, images[piece], trial > 0, held)
                    return carry

                lax.fori_loop(0, (count + 1) // 2, pair_step, 0)
            most = functools.reduce(
                jnp.maximum, [mixed_ref[block, HEAD_SIZE : HEAD_SIZE + 1, :] for block in range(block_count)]
            )
            if last:
                finish()
            redo_ref[0] = 1 - jnp.min((most <= MOST_SUM).astype(jnp.int32))

        return carry

    lax.fori_loop(0, 2, attempt, 0)


def cross_part(table, queries, images, key_count, offset, last, before=()):
    tokens, columns = queries[0].shape
    block_count = tokens // MASK_BLOCK_TOKENS
    rows = columns // HEAD_SIZE * MASK_BLOCK_TOKENS
    state = [(block_count, 8, rows), (block_count, MIXED_ROWS, rows)]
    scratch = [pltpu.VMEM((8, 2 * rows), jnp.float32), pltpu.SMEM((1,), jnp.int32)]
    if last:
        out_shape = jax.ShapeDtypeStruct((block_count * HEAD_SIZE + lse_rows(block_count), rows), jnp.bfloat16)
        scratch = [pltpu.VMEM(shape, jnp.float32) for shape in state] + scratch
        scratch = [pltpu.VMEM((-(-block_count // 8) * 8, rows), jnp.float32)] + scratch
    else:
        out_shape = tuple(jax.ShapeDtypeStruct(shape, jnp.float32) for shape in state)
    return pl.pallas_call(
        functools.partial(cross_kernel, key_count, len(images), offset, last, len(queries)),
        out_shape=out_shape,
        in_specs=[SMEM] + [VMEM] * (len(queries) + len(images) + len(before)),
        out_specs=VMEM if last else (VMEM,) * 2,
        scratch_shapes=scratch,
        compiler_params=pltpu.CompilerParams(vmem_limit_bytes=VMEM_LIMIT),
        cost_estimate=MUCH,
        name="cross_last" if last else "cross_first",
    )(table, *queries, *images, *before)


def lse_of(ref, block_count):
    tail = ref[block_count * HEAD_SIZE :, :].astype(jnp.float32)
    return tail[0:block_count] + tail[block_count : 2 * block_count] + tail[2 * block_count : 3 * block_count]


def lse_pieces(lse, block_count):
    first = lse.astype(jnp.bfloat16).astype(jnp.float32)
    second = (lse - first).astype(jnp.bfloat16).astype(jnp.float32)
    pieces = [first, second, lse - first - second]
    spare = lse_rows(block_count) - 3 * block_count
    if spare:
        pieces.append(jnp.zeros((spare, lse.shape[1]), jnp.float32))
    return jnp.concatenate(pieces, axis=0).astype(jnp.bfloat16)


def mixed_block(part_refs, weights, block):
    at = slice(block * HEAD_SIZE, (block + 1) * HEAD_SIZE)
    terms = [weight[block : block + 1, :] * ref[at, :].astype(jnp.float32) for ref, weight in zip(part_refs, weights)]
    return functools.reduce(jnp.add, terms)


def combine_kernel(held, last, *refs):
    if held:
        mixed_ref, lse_ref, part_ref, *out_refs = refs
        block_count = lse_ref.shape[0]
        lse = [lse_ref[...], lse_of(part_ref, block_count)]
    else:
        mixed_ref, part_ref, *out_refs = refs
        block_count = packed_blocks(part_ref.shape[0])
        lse = [lse_of(mixed_ref, block_count), lse_of(part_ref, block_count)]
    highest = functools.reduce(jnp.maximum, lse)
    weights = [jnp.exp2(one - highest) for one in lse]
    total = functools.reduce(jnp.add, weights)
    weights = [one / total for one in weights]
    for block in range(block_count):
        mixed = mixed_block((mixed_ref, part_ref), weights, block)
        if last:
            store_heads(out_refs[0], block, mixed)
        else:
            out_refs[0][block * HEAD_SIZE : (block + 1) * HEAD_SIZE, :] = mixed
    if not last:
        out_refs[1][...] = highest + jnp.log2(total)


def store_heads(out_ref, block, mixed):
    at = slice(block * MASK_BLOCK_TOKENS, (block + 1) * MASK_BLOCK_TOKENS)
    for head in range(out_ref.shape[1] // HEAD_SIZE):
        piece = mixed[:, head * MASK_BLOCK_TOKENS : (head + 1) * MASK_BLOCK_TOKENS]
        out_ref[at, head * HEAD_SIZE : (head + 1) * HEAD_SIZE] = piece.T.astype(jnp.bfloat16)


def combined(so_far, part, shape, last):
    tokens, columns = shape
    held = len(so_far) == 2
    block_count = tokens // MASK_BLOCK_TOKENS
    rows = columns // HEAD_SIZE * MASK_BLOCK_TOKENS
    if last:
        out_shape = jax.ShapeDtypeStruct(shape, jnp.bfloat16)
    else:
        out_shape = (
            jax.ShapeDtypeStruct((block_count * HEAD_SIZE, rows), jnp.float32),
            jax.ShapeDtypeStruct((block_count, rows), jnp.float32),
        )
    return pl.pallas_call(
        functools.partial(combine_kernel, held, last),
        out_shape=out_shape,
        in_specs=[VMEM] * (len(so_far) + 1),
        out_specs=VMEM if last else (VMEM,) * 2,
        compiler_params=pltpu.CompilerParams(vmem_limit_bytes=VMEM_LIMIT),
        cost_estimate=MUCH,
        name="combine_last" if last else "combine",
    )(*so_far, part)


def pair_queries(q_ref, first, blocks):
    return jnp.concatenate(
        [
            stacked_heads(q_ref[block * MASK_BLOCK_TOKENS : (block + 1) * MASK_BLOCK_TOKENS, :])
            for block in range(first, first + blocks)
        ],
        axis=0,
    )


def self_first_kernel(group, q_ref, text_ref, high_ref, mixed_ref, value_ref):
    tokens, columns = q_ref.shape
    rows = columns // HEAD_SIZE * MASK_BLOCK_TOKENS
    value_ref[...] = text_ref[:, HEAD_SIZE:].T
    for index in range(tokens // MASK_BLOCK_TOKENS // group):
        first = index * group
        start, stop = first * MASK_BLOCK_TOKENS, (first + group) * MASK_BLOCK_TOKENS
        scores = nt_dot(text_ref[0:stop, 0:HEAD_SIZE], pair_queries(q_ref, first, group))
        tail = scores[start:, :]
        key_id = lax.broadcasted_iota(jnp.int32, tail.shape, 0)
        column = lax.broadcasted_iota(jnp.int32, tail.shape, 1)
        query_id = column // rows * MASK_BLOCK_TOKENS + column % MASK_BLOCK_TOKENS
        tail = jnp.where(key_id <= query_id, tail, LOWEST)
        scores = jnp.concatenate([scores[:start, :], tail], axis=0) if start else tail
        high = jnp.full((1, group * rows), LOWEST, jnp.float32)
        mixed = jnp.zeros((MIXED_ROWS, group * rows), jnp.float32)
        high, mixed = fold(high, mixed, scores, value_ref[:, 0:stop], True)
        high_ref[index] = jnp.broadcast_to(high, high_ref.shape[1:])
        mixed_ref[index] = mixed


def self_last_kernel(group, pieces, position_ref, q_ref, high_ref, mixed_ref, *refs):
    texts = refs[:pieces]
    out_ref, value_ref, new_high_ref, new_mixed_ref = refs[pieces:]
    rows = q_ref.shape[1] // HEAD_SIZE * MASK_BLOCK_TOKENS
    new_high_ref[...] = high_ref[...]
    new_mixed_ref[...] = mixed_ref[...]
    for piece in range(pieces):

        @pl.when(position_ref[0] >= piece + 1)
        def _(piece=piece):
            value_ref[...] = texts[piece][:, HEAD_SIZE:].T
            for index in range(high_ref.shape[0]):
                scores = nt_dot(texts[piece][:, 0:HEAD_SIZE], pair_queries(q_ref, index * group, group))
                high, mixed = fold(new_high_ref[index, 0:1, :], new_mixed_ref[index], scores, value_ref[...], True)
                new_high_ref[index] = jnp.broadcast_to(high, high_ref.shape[1:])
                new_mixed_ref[index] = mixed

    for index in range(high_ref.shape[0]):
        total = new_mixed_ref[index, HEAD_SIZE : HEAD_SIZE + 1, :]
        mixed = new_mixed_ref[index, 0:HEAD_SIZE, :] / total
        for block in range(group):
            store_heads(out_ref, index * group + block, mixed[:, block * rows : (block + 1) * rows])


def self_first(queries, text):
    tokens, columns = queries.shape
    block_count = tokens // MASK_BLOCK_TOKENS
    group = 1 if block_count % 2 else 2
    width = group * columns // HEAD_SIZE * MASK_BLOCK_TOKENS
    return pl.pallas_call(
        functools.partial(self_first_kernel, group),
        out_shape=(
            jax.ShapeDtypeStruct((block_count // group, 8, width), jnp.float32),
            jax.ShapeDtypeStruct((block_count // group, MIXED_ROWS, width), jnp.float32),
        ),
        in_specs=[VMEM] * 2,
        out_specs=(VMEM,) * 2,
        scratch_shapes=[pltpu.VMEM((HEAD_SIZE, tokens), jnp.bfloat16)],
        compiler_params=pltpu.CompilerParams(vmem_limit_bytes=VMEM_LIMIT),
        cost_estimate=LITTLE,
        name="self_first",
    )(queries, text)


def self_last(position, queries, state, texts):
    tokens, columns = queries.shape
    group = tokens // MASK_BLOCK_TOKENS // state[0].shape[0]
    return pl.pallas_call(
        functools.partial(self_last_kernel, group, len(texts)),
        out_shape=jax.ShapeDtypeStruct((tokens, columns), jnp.bfloat16),
        in_specs=[SMEM] + [VMEM] * (3 + len(texts)),
        out_specs=VMEM,
        scratch_shapes=[pltpu.VMEM((HEAD_SIZE, tokens), jnp.bfloat16)]
        + [pltpu.VMEM(one.shape, jnp.float32) for one in state],
        compiler_params=pltpu.CompilerParams(vmem_limit_bytes=VMEM_LIMIT),
        cost_estimate=LITTLE,
        name="self_last",
    )(position, queries, *state, *texts)


def shifted(value, axis, steps):
    count = lax.axis_size(axis)
    return lax.ppermute(value, axis, [(source, (source + steps) % count) for source in range(count)])


def swapped(value, axis, bits):
    return lax.ppermute(value, axis, [(source, source ^ bits) for source in range(lax.axis_size(axis))])


def after(value, earlier):
    return lax.optimization_barrier((value, earlier))[0]


def per_device(
    self_queries, text_kv, cross_queries, image_kv, block_images, image_owner
):
    rows = self_queries.shape[0]
    key_count = image_kv.shape[2]
    cycle = lax.axis_size("blk")
    ring = lax.axis_size("enc")
    place = lax.axis_index("enc")
    inside = ((place > 0) & (place < ring - 1)).astype(jnp.int32)[None]
    position = lax.axis_index("blk").astype(jnp.int32)[None]

    raw = [image_kv]
    for _ in range(1, cycle):
        raw.append(shifted(raw[-1], "blk", 1))
    images = [prepare(image[0]) for image in raw]
    if ring == 4:
        queries = {step: [swapped(cross_queries, "enc", step)] for step in (2, 1)}
        middle = lax.ppermute(cross_queries, "enc", [(0, 0), (1, 2), (2, 1), (3, 3)])
        queries[3] = [middle, swapped(queries[2][0], "enc", 1)]
    else:
        queries = {step: [shifted(cross_queries, "enc", ring - step)] for step in range(1, ring)}
    queries[0] = [cross_queries]
    table = seen_table(position, inside, block_images, image_owner)

    latest = [None]

    def in_turn(arrays):
        return arrays if latest[0] is None else [after(one, latest[0]) for one in arrays]

    def begun(step):
        latest[0] = cross_part(table, in_turn(queries[step]), images[:1], key_count, 0, False)
        return latest[0]

    def finished(step, state=None):
        used = images if state is None else images[1:]
        before = () if state is None else state
        offset = 0 if state is None else 1
        latest[0] = cross_part(table, in_turn(queries[step]), used, key_count, offset, True, before)
        return latest[0]

    split = cycle > 1
    own = begun(0) if split else None
    steps = [2, 3, 1] if ring == 4 else list(range(1, ring))
    states = {step: begun(step) for step in steps[:1]} if split else {}
    received, texts = [], []
    for step in steps:
        part = finished(step, states.get(step))
        if not texts:
            texts.append(after(text_kv, part).reshape(rows, 2 * HEAD_SIZE))
            for _ in range(1, cycle):
                texts.append(shifted(texts[-1], "blk", 1))
        received.append(swapped(part, "enc", step) if ring == 4 else shifted(part, "enc", step))
    own_part = finished(0, own)
    self_state = latest[0] = self_first(in_turn([self_queries])[0], texts[0])
    self_out = latest[0] = self_last(position, in_turn([self_queries])[0], self_state, texts[1:])
    so_far = in_turn([own_part])
    for index, part in enumerate(received):
        so_far = combined(so_far, part, cross_queries.shape, index + 1 == len(received))
    return (self_out, so_far)


def solution(mesh):
    placed = (
        P("blk", ("tp", "enc")),
        P("blk", None, "tp"),
        P("blk", ("tp", "enc")),
        P("blk", None, "enc", "tp"),
        P("blk", None),
        P(),
    )
    return jax.shard_map(
        per_device,
        mesh=mesh,
        in_specs=placed,
        out_specs=(P("blk", ("tp", "enc")), P("blk", ("tp", "enc"))),
        check_vma=False,
    )
```

```python
import functools
import math

import jax
import jax.numpy as jnp
from jax import lax
from jax.experimental import pallas as pl
from jax.experimental.pallas import tpu as pltpu
from jax.sharding import PartitionSpec as P

HEAD_SIZE = 128
MASK_BLOCK_TOKENS = 128
LANES = 128
LOWEST = -1e30
MIXED_ROWS = HEAD_SIZE + 16
SHIFT_KEYS = 256
MOST_SUM = 2.0**100
LOG2_SCALE = math.log2(math.e) / math.sqrt(HEAD_SIZE)
VMEM_LIMIT = 48 * 1024 * 1024

LITTLE = pl.CostEstimate(flops=0, bytes_accessed=1024, transcendentals=0)
MUCH = pl.CostEstimate(flops=2_000_000_000, bytes_accessed=1024, transcendentals=0)

VMEM = pl.BlockSpec(memory_space=pltpu.VMEM)
SMEM = pl.BlockSpec(memory_space=pltpu.SMEM)


def padded(count):
    return -(-count // LANES) * LANES


def nt_dot(a, b):
    return lax.dot_general(a, b, (((1,), (1,)), ((), ())), preferred_element_type=jnp.float32)


def at_block(block, size=MASK_BLOCK_TOKENS):
    return pl.ds(pl.multiple_of(block * size, size), size)


def stacked_heads(rows):
    heads = rows.shape[1] // HEAD_SIZE
    return jnp.concatenate([rows[:, h * HEAD_SIZE : (h + 1) * HEAD_SIZE] for h in range(heads)], axis=0)


def with_ones(value_t):
    shape = (MIXED_ROWS - HEAD_SIZE, value_t.shape[1])
    ones = (lax.broadcasted_iota(jnp.int32, shape, 0) == 0).astype(jnp.bfloat16)
    return jnp.concatenate([value_t, ones], axis=0)


def fold(high, mixed, scores, value_t, exact):
    seen = scores if exact else scores[0 : min(SHIFT_KEYS, scores.shape[0]), :]
    new_high = jnp.maximum(high, jnp.max(seen, axis=0, keepdims=True))
    weights = jnp.exp2(scores * LOG2_SCALE - new_high * LOG2_SCALE).astype(jnp.bfloat16)
    fading = jnp.exp2((high - new_high) * LOG2_SCALE)
    mixed = mixed * fading + jnp.dot(with_ones(value_t), weights, preferred_element_type=jnp.float32)
    return new_high, mixed


def prepare_kernel(kv_ref, out_ref):
    count = kv_ref.shape[1]
    whole = count // LANES * LANES
    rest = count - whole
    out_ref[0, 0:whole, :] = kv_ref[0, 0:whole, :]
    for at in range(0, whole, LANES):
        out_ref[1, at : at + LANES, :] = kv_ref[1, at : at + LANES, :].T
    if rest:
        empty = jnp.zeros((LANES - rest, HEAD_SIZE), jnp.float32)
        tail_key = jnp.concatenate([kv_ref[0, whole:count, :].astype(jnp.float32), empty], axis=0)
        tail_value = jnp.concatenate([kv_ref[1, whole:count, :].astype(jnp.float32), empty], axis=0)
        out_ref[0, whole : whole + LANES, :] = tail_key.astype(jnp.bfloat16)
        out_ref[1, whole : whole + LANES, :] = tail_value.T.astype(jnp.bfloat16)


def prepare(kv):
    return pl.pallas_call(
        prepare_kernel,
        out_shape=jax.ShapeDtypeStruct((2, padded(kv.shape[1]), HEAD_SIZE), jnp.bfloat16),
        in_specs=[VMEM],
        out_specs=VMEM,
        compiler_params=pltpu.CompilerParams(vmem_limit_bytes=VMEM_LIMIT),
        cost_estimate=LITTLE,
        name="prepare",
    )(kv)


def lse_rows(block_count):
    return -(-3 * block_count // 16) * 16


def packed_blocks(rows):
    return next(count for count in range(1, rows) if count * HEAD_SIZE + lse_rows(count) == rows)


def table_kernel(position_ref, inside_ref, images_ref, owner_ref, out_ref, table_ref):
    slots, block_count = images_ref.shape
    for piece in range(slots):
        slot = lax.rem(position_ref[0] + (slots - piece), slots)
        base = piece * (block_count + 1)
        count = jnp.int32(0)
        for block in range(block_count):
            table_ref[base + 1 + block] = jnp.int32(0)
        for block in range(block_count):
            seen = lax.fori_loop(
                0,
                slots,
                lambda image, sum, block=block, slot=slot: sum
                + jnp.where(owner_ref[image] == slot, images_ref[image, block], 0),
                jnp.int32(0),
            )

            @pl.when(seen > 0)
            def _(base=base, block=block, count=count):
                table_ref[base + 1 + count] = jnp.int32(block)

            count = count + jnp.where(seen > 0, 1, 0)
        table_ref[base] = count
    lane = lax.broadcasted_iota(jnp.int32, out_ref.shape, 1)
    table = jnp.where(lane == out_ref.shape[1] - 1, inside_ref[0], 0)
    for index in range(table_ref.shape[0]):
        table = jnp.where(lane == index, table_ref[index], table)
    out_ref[...] = table


def seen_table(position, inside, block_images, image_owner):
    block_count, slots = block_images.shape
    size = slots * (block_count + 1)
    return pl.pallas_call(
        table_kernel,
        out_shape=jax.ShapeDtypeStruct((1, padded(size + 1)), jnp.int32),
        in_specs=[SMEM] * 4,
        out_specs=VMEM,
        scratch_shapes=[pltpu.SMEM((size,), jnp.int32)],
        name="seen_table",
    )(position, inside, block_images.T, image_owner)


def chunks_of(width):
    half = width // LANES // 2 * LANES
    return [(0, half), (half, width)] if half else [(0, width)]


def cross_kernel(key_count, pieces, offset, last, parts, table_ref, *refs):
    q_refs, images, refs = refs[:parts], refs[parts : parts + pieces], refs[parts + pieces :]
    if offset:
        before, refs = refs[:2], refs[2:]
    if last:
        out_ref, lse_ref, high_ref, mixed_ref, peak_ref, redo_ref = refs
    else:
        high_ref, mixed_ref, peak_ref, redo_ref = refs
    block_count = q_refs[0].shape[0] // MASK_BLOCK_TOKENS
    rows = q_refs[0].shape[1] // HEAD_SIZE * MASK_BLOCK_TOKENS
    peak_ref[...] = jnp.full_like(peak_ref, LOWEST)
    redo_ref[0] = jnp.int32(0)

    def fold_pair(blocks, image, exact, held):
        width = image.shape[1]
        queries = [q_refs[0][at_block(block), :] for block in blocks]
        if parts > 1:
            first = table_ref[0, table_ref.shape[1] - 1] > 0
            queries = [jnp.where(first, one, q_refs[1][at_block(block), :]) for one, block in zip(queries, blocks)]
        queries = jnp.concatenate([stacked_heads(one) for one in queries], axis=0)
        chunks = chunks_of(width)

        def scores_of(start, stop):
            scores = nt_dot(image[0, start:stop, :], queries)
            if stop > key_count:
                body = stop - start - LANES
                tail = scores[body:, :]
                key_id = start + body + lax.broadcasted_iota(jnp.int32, tail.shape, 0)
                tail = jnp.where(key_id < key_count, tail, LOWEST)
                scores = jnp.concatenate([scores[:body, :], tail], axis=0) if body else tail
            return scores

        @pl.when(exact)
        def _():
            tops = [jnp.max(scores_of(*chunk), axis=0, keepdims=True) for chunk in chunks]
            peak_ref[0:1, :] = functools.reduce(jnp.maximum, tops)

        if held is None:
            high = jnp.full((1, 2 * rows), LOWEST, jnp.float32)
            mixed = jnp.zeros((MIXED_ROWS, 2 * rows), jnp.float32)
        else:
            high = jnp.concatenate([held[0][block][0:1] for block in blocks], axis=1)
            mixed = jnp.concatenate([held[1][block] for block in blocks], axis=1)
        scores = scores_of(*chunks[0])
        seen = jnp.max(scores[0 : min(SHIFT_KEYS, scores.shape[0])], axis=0, keepdims=True)
        new_high = jnp.maximum(jnp.maximum(high, seen), peak_ref[0:1, :])
        shift = new_high * LOG2_SCALE
        mixed = mixed * jnp.exp2((high - new_high) * LOG2_SCALE)
        for index, (start, stop) in enumerate(chunks):
            following = scores_of(*chunks[index + 1]) if index + 1 < len(chunks) else None
            weights = jnp.exp2(scores * LOG2_SCALE - shift).astype(jnp.bfloat16)
            value_t = jnp.concatenate([image[1, c : c + LANES, :] for c in range(start, stop, LANES)], axis=1)
            mixed = mixed + jnp.dot(with_ones(value_t), weights, preferred_element_type=jnp.float32)
            scores = following
        for index, block in enumerate(blocks):
            own = slice(index * rows, (index + 1) * rows)
            high_ref[block] = jnp.broadcast_to(new_high[:, own], high_ref.shape[1:])
            mixed_ref[block] = mixed[:, own]

    def finish():
        for block in range(block_count):
            total = mixed_ref[block, HEAD_SIZE : HEAD_SIZE + 1, :]
            out_ref[block * HEAD_SIZE : (block + 1) * HEAD_SIZE, :] = (
                mixed_ref[block, 0:HEAD_SIZE, :] * (1.0 / total)
            ).astype(jnp.bfloat16)
            lse_ref[block : block + 1, :] = high_ref[block, 0:1, :] * LOG2_SCALE + jnp.log2(total)
        out_ref[block_count * HEAD_SIZE :, :] = lse_pieces(lse_ref[0:block_count, :], block_count)

    def attempt(trial, carry):
        @pl.when((trial == 0) | (redo_ref[0] > 0))
        def _():
            for piece in range(pieces):
                base = (offset + piece) * (block_count + 1)
                count = table_ref[0, base]
                if piece == 0:
                    held = before if offset else None
                    for block in range(block_count):
                        seen = functools.reduce(
                            jnp.logical_or,
                            [(count > index) & (table_ref[0, base + 1 + index] == block) for index in range(block_count)],
                        )

                        @pl.when(jnp.logical_not(seen))
                        def _(block=block):
                            if held is None:
                                high_ref[block] = jnp.full(high_ref.shape[1:], LOWEST, jnp.float32)
                                mixed_ref[block] = jnp.zeros(mixed_ref.shape[1:], jnp.float32)
                            else:
                                high_ref[block] = held[0][block]
                                mixed_ref[block] = held[1][block]

                else:
                    held = (high_ref, mixed_ref)

                def pair_step(pair, carry, piece=piece, base=base, count=count, held=held):
                    blocks = [table_ref[0, base + 1 + 2 * pair], table_ref[0, base + jnp.minimum(2 * pair + 2, count)]]
                    fold_pair(blocks, images[piece], trial > 0, held)
                    return carry

                lax.fori_loop(0, (count + 1) // 2, pair_step, 0)
            most = functools.reduce(
                jnp.maximum, [mixed_ref[block, HEAD_SIZE : HEAD_SIZE + 1, :] for block in range(block_count)]
            )
            if last:
                finish()
            redo_ref[0] = 1 - jnp.min((most <= MOST_SUM).astype(jnp.int32))

        return carry

    lax.fori_loop(0, 2, attempt, 0)


def cross_part(table, queries, images, key_count, offset, last, before=()):
    tokens, columns = queries[0].shape
    block_count = tokens // MASK_BLOCK_TOKENS
    rows = columns // HEAD_SIZE * MASK_BLOCK_TOKENS
    state = [(block_count, 8, rows), (block_count, MIXED_ROWS, rows)]
    scratch = [pltpu.VMEM((8, 2 * rows), jnp.float32), pltpu.SMEM((1,), jnp.int32)]
    if last:
        out_shape = jax.ShapeDtypeStruct((block_count * HEAD_SIZE + lse_rows(block_count), rows), jnp.bfloat16)
        scratch = [pltpu.VMEM(shape, jnp.float32) for shape in state] + scratch
        scratch = [pltpu.VMEM((-(-block_count // 8) * 8, rows), jnp.float32)] + scratch
    else:
        out_shape = tuple(jax.ShapeDtypeStruct(shape, jnp.float32) for shape in state)
    return pl.pallas_call(
        functools.partial(cross_kernel, key_count, len(images), offset, last, len(queries)),
        out_shape=out_shape,
        in_specs=[SMEM] + [VMEM] * (len(queries) + len(images) + len(before)),
        out_specs=VMEM if last else (VMEM,) * 2,
        scratch_shapes=scratch,
        compiler_params=pltpu.CompilerParams(vmem_limit_bytes=VMEM_LIMIT),
        cost_estimate=MUCH,
        name="cross_last" if last else "cross_first",
    )(table, *queries, *images, *before)


def lse_of(ref, block_count):
    tail = ref[block_count * HEAD_SIZE :, :].astype(jnp.float32)
    return tail[0:block_count] + tail[block_count : 2 * block_count] + tail[2 * block_count : 3 * block_count]


def lse_pieces(lse, block_count):
    first = lse.astype(jnp.bfloat16).astype(jnp.float32)
    second = (lse - first).astype(jnp.bfloat16).astype(jnp.float32)
    pieces = [first, second, lse - first - second]
    spare = lse_rows(block_count) - 3 * block_count
    if spare:
        pieces.append(jnp.zeros((spare, lse.shape[1]), jnp.float32))
    return jnp.concatenate(pieces, axis=0).astype(jnp.bfloat16)


def mixed_block(part_refs, weights, block):
    at = slice(block * HEAD_SIZE, (block + 1) * HEAD_SIZE)
    terms = [weight[block : block + 1, :] * ref[at, :].astype(jnp.float32) for ref, weight in zip(part_refs, weights)]
    return functools.reduce(jnp.add, terms)


def combine_kernel(held, last, *refs):
    if held:
        mixed_ref, lse_ref, part_ref, *out_refs = refs
        block_count = lse_ref.shape[0]
        lse = [lse_ref[...], lse_of(part_ref, block_count)]
    else:
        mixed_ref, part_ref, *out_refs = refs
        block_count = packed_blocks(part_ref.shape[0])
        lse = [lse_of(mixed_ref, block_count), lse_of(part_ref, block_count)]
    highest = functools.reduce(jnp.maximum, lse)
    weights = [jnp.exp2(one - highest) for one in lse]
    total = functools.reduce(jnp.add, weights)
    weights = [one / total for one in weights]
    for block in range(block_count):
        mixed = mixed_block((mixed_ref, part_ref), weights, block)
        if last:
            store_heads(out_refs[0], block, mixed)
        else:
            out_refs[0][block * HEAD_SIZE : (block + 1) * HEAD_SIZE, :] = mixed
    if not last:
        out_refs[1][...] = highest + jnp.log2(total)


def store_heads(out_ref, block, mixed):
    at = slice(block * MASK_BLOCK_TOKENS, (block + 1) * MASK_BLOCK_TOKENS)
    for head in range(out_ref.shape[1] // HEAD_SIZE):
        piece = mixed[:, head * MASK_BLOCK_TOKENS : (head + 1) * MASK_BLOCK_TOKENS]
        out_ref[at, head * HEAD_SIZE : (head + 1) * HEAD_SIZE] = piece.T.astype(jnp.bfloat16)


def combined(so_far, part, shape, last):
    tokens, columns = shape
    held = len(so_far) == 2
    block_count = tokens // MASK_BLOCK_TOKENS
    rows = columns // HEAD_SIZE * MASK_BLOCK_TOKENS
    if last:
        out_shape = jax.ShapeDtypeStruct(shape, jnp.bfloat16)
    else:
        out_shape = (
            jax.ShapeDtypeStruct((block_count * HEAD_SIZE, rows), jnp.float32),
            jax.ShapeDtypeStruct((block_count, rows), jnp.float32),
        )
    return pl.pallas_call(
        functools.partial(combine_kernel, held, last),
        out_shape=out_shape,
        in_specs=[VMEM] * (len(so_far) + 1),
        out_specs=VMEM if last else (VMEM,) * 2,
        compiler_params=pltpu.CompilerParams(vmem_limit_bytes=VMEM_LIMIT),
        cost_estimate=MUCH,
        name="combine_last" if last else "combine",
    )(*so_far, part)


def pair_queries(q_ref, first, blocks):
    return jnp.concatenate(
        [
            stacked_heads(q_ref[block * MASK_BLOCK_TOKENS : (block + 1) * MASK_BLOCK_TOKENS, :])
            for block in range(first, first + blocks)
        ],
        axis=0,
    )


def self_first_kernel(group, q_ref, text_ref, high_ref, mixed_ref, value_ref):
    tokens, columns = q_ref.shape
    rows = columns // HEAD_SIZE * MASK_BLOCK_TOKENS
    value_ref[...] = text_ref[:, HEAD_SIZE:].T
    for index in range(tokens // MASK_BLOCK_TOKENS // group):
        first = index * group
        start, stop = first * MASK_BLOCK_TOKENS, (first + group) * MASK_BLOCK_TOKENS
        scores = nt_dot(text_ref[0:stop, 0:HEAD_SIZE], pair_queries(q_ref, first, group))
        tail = scores[start:, :]
        key_id = lax.broadcasted_iota(jnp.int32, tail.shape, 0)
        column = lax.broadcasted_iota(jnp.int32, tail.shape, 1)
        query_id = column // rows * MASK_BLOCK_TOKENS + column % MASK_BLOCK_TOKENS
        tail = jnp.where(key_id <= query_id, tail, LOWEST)
        scores = jnp.concatenate([scores[:start, :], tail], axis=0) if start else tail
        high = jnp.full((1, group * rows), LOWEST, jnp.float32)
        mixed = jnp.zeros((MIXED_ROWS, group * rows), jnp.float32)
        high, mixed = fold(high, mixed, scores, value_ref[:, 0:stop], True)
        high_ref[index] = jnp.broadcast_to(high, high_ref.shape[1:])
        mixed_ref[index] = mixed


def self_last_kernel(group, pieces, position_ref, q_ref, high_ref, mixed_ref, *refs):
    texts = refs[:pieces]
    out_ref, value_ref, new_high_ref, new_mixed_ref = refs[pieces:]
    rows = q_ref.shape[1] // HEAD_SIZE * MASK_BLOCK_TOKENS
    new_high_ref[...] = high_ref[...]
    new_mixed_ref[...] = mixed_ref[...]
    for piece in range(pieces):

        @pl.when(position_ref[0] >= piece + 1)
        def _(piece=piece):
            value_ref[...] = texts[piece][:, HEAD_SIZE:].T
            for index in range(high_ref.shape[0]):
                scores = nt_dot(texts[piece][:, 0:HEAD_SIZE], pair_queries(q_ref, index * group, group))
                high, mixed = fold(new_high_ref[index, 0:1, :], new_mixed_ref[index], scores, value_ref[...], True)
                new_high_ref[index] = jnp.broadcast_to(high, high_ref.shape[1:])
                new_mixed_ref[index] = mixed

    for index in range(high_ref.shape[0]):
        total = new_mixed_ref[index, HEAD_SIZE : HEAD_SIZE + 1, :]
        mixed = new_mixed_ref[index, 0:HEAD_SIZE, :] / total
        for block in range(group):
            store_heads(out_ref, index * group + block, mixed[:, block * rows : (block + 1) * rows])


def self_first(queries, text):
    tokens, columns = queries.shape
    block_count = tokens // MASK_BLOCK_TOKENS
    group = 1 if block_count % 2 else 2
    width = group * columns // HEAD_SIZE * MASK_BLOCK_TOKENS
    return pl.pallas_call(
        functools.partial(self_first_kernel, group),
        out_shape=(
            jax.ShapeDtypeStruct((block_count // group, 8, width), jnp.float32),
            jax.ShapeDtypeStruct((block_count // group, MIXED_ROWS, width), jnp.float32),
        ),
        in_specs=[VMEM] * 2,
        out_specs=(VMEM,) * 2,
        scratch_shapes=[pltpu.VMEM((HEAD_SIZE, tokens), jnp.bfloat16)],
        compiler_params=pltpu.CompilerParams(vmem_limit_bytes=VMEM_LIMIT),
        cost_estimate=LITTLE,
        name="self_first",
    )(queries, text)


def self_last(position, queries, state, texts):
    tokens, columns = queries.shape
    group = tokens // MASK_BLOCK_TOKENS // state[0].shape[0]
    return pl.pallas_call(
        functools.partial(self_last_kernel, group, len(texts)),
        out_shape=jax.ShapeDtypeStruct((tokens, columns), jnp.bfloat16),
        in_specs=[SMEM] + [VMEM] * (3 + len(texts)),
        out_specs=VMEM,
        scratch_shapes=[pltpu.VMEM((HEAD_SIZE, tokens), jnp.bfloat16)]
        + [pltpu.VMEM(one.shape, jnp.float32) for one in state],
        compiler_params=pltpu.CompilerParams(vmem_limit_bytes=VMEM_LIMIT),
        cost_estimate=LITTLE,
        name="self_last",
    )(position, queries, *state, *texts)


def shifted(value, axis, steps):
    count = lax.axis_size(axis)
    return lax.ppermute(value, axis, [(source, (source + steps) % count) for source in range(count)])


def swapped(value, axis, bits):
    return lax.ppermute(value, axis, [(source, source ^ bits) for source in range(lax.axis_size(axis))])


def after(value, earlier):
    return lax.optimization_barrier((value, earlier))[0]


def per_device(
    self_queries, text_kv, cross_queries, image_kv, block_images, image_owner
):
    rows = self_queries.shape[0]
    key_count = image_kv.shape[2]
    cycle = lax.axis_size("blk")
    ring = lax.axis_size("enc")
    place = lax.axis_index("enc")
    inside = ((place > 0) & (place < ring - 1)).astype(jnp.int32)[None]
    position = lax.axis_index("blk").astype(jnp.int32)[None]

    raw = [image_kv]
    for _ in range(1, cycle):
        raw.append(shifted(raw[-1], "blk", 1))
    images = [prepare(image[0]) for image in raw]
    if ring == 4:
        queries = {step: [swapped(cross_queries, "enc", step)] for step in (2, 1)}
        middle = lax.ppermute(cross_queries, "enc", [(0, 0), (1, 2), (2, 1), (3, 3)])
        queries[3] = [middle, swapped(queries[2][0], "enc", 1)]
    else:
        queries = {step: [shifted(cross_queries, "enc", ring - step)] for step in range(1, ring)}
    queries[0] = [cross_queries]
    table = seen_table(position, inside, block_images, image_owner)

    latest = [None]

    def in_turn(arrays):
        return arrays if latest[0] is None else [after(one, latest[0]) for one in arrays]

    def begun(step):
        latest[0] = cross_part(table, in_turn(queries[step]), images[:1], key_count, 0, False)
        return latest[0]

    def finished(step, state=None):
        used = images if state is None else images[1:]
        before = () if state is None else state
        offset = 0 if state is None else 1
        latest[0] = cross_part(table, in_turn(queries[step]), used, key_count, offset, True, before)
        return latest[0]

    split = cycle > 1
    own = begun(0) if split else None
    steps = [2, 3, 1] if ring == 4 else list(range(1, ring))
    states = {step: begun(step) for step in steps[:1]} if split else {}
    received, texts = [], []
    for step in steps:
        part = finished(step, states.get(step))
        if not texts:
            texts.append(after(text_kv, part).reshape(rows, 2 * HEAD_SIZE))
            for _ in range(1, cycle):
                texts.append(shifted(texts[-1], "blk", 1))
        received.append(swapped(part, "enc", step) if ring == 4 else shifted(part, "enc", step))
    own_part = finished(0, own)
    self_state = latest[0] = self_first(in_turn([self_queries])[0], texts[0])
    self_out = latest[0] = self_last(position, in_turn([self_queries])[0], self_state, texts[1:])
    so_far = in_turn([own_part])
    for index, part in enumerate(received):
        so_far = combined(so_far, part, cross_queries.shape, index + 1 == len(received))
    return (self_out, so_far)


def solution(mesh):
    placed = (
        P("blk", ("tp", "enc")),
        P("blk", None, "tp"),
        P("blk", ("tp", "enc")),
        P("blk", None, "enc", "tp"),
        P("blk", None),
        P(),
    )
    return jax.shard_map(
        per_device,
        mesh=mesh,
        in_specs=placed,
        out_specs=(P("blk", ("tp", "enc")), P("blk", ("tp", "enc"))),
        check_vma=False,
    )
```

```python
import functools
import math

import jax
import jax.numpy as jnp
from jax import lax
from jax.experimental import pallas as pl
from jax.experimental.pallas import tpu as pltpu
from jax.sharding import PartitionSpec as P

HEAD_SIZE = 128
MASK_BLOCK_TOKENS = 128
LANES = 128
LOWEST = -1e30
MIXED_ROWS = HEAD_SIZE + 16
SHIFT_KEYS = 256
MOST_SUM = 2.0**100
LOG2_SCALE = math.log2(math.e) / math.sqrt(HEAD_SIZE)
VMEM_LIMIT = 48 * 1024 * 1024

LITTLE = pl.CostEstimate(flops=0, bytes_accessed=1024, transcendentals=0)
MUCH = pl.CostEstimate(flops=2_000_000_000, bytes_accessed=1024, transcendentals=0)

VMEM = pl.BlockSpec(memory_space=pltpu.VMEM)
SMEM = pl.BlockSpec(memory_space=pltpu.SMEM)


def padded(count):
    return -(-count // LANES) * LANES


def nt_dot(a, b):
    return lax.dot_general(a, b, (((1,), (1,)), ((), ())), preferred_element_type=jnp.float32)


def at_block(block, size=MASK_BLOCK_TOKENS):
    return pl.ds(pl.multiple_of(block * size, size), size)


def stacked_heads(rows):
    heads = rows.shape[1] // HEAD_SIZE
    return jnp.concatenate([rows[:, h * HEAD_SIZE : (h + 1) * HEAD_SIZE] for h in range(heads)], axis=0)


def with_ones(value_t):
    shape = (MIXED_ROWS - HEAD_SIZE, value_t.shape[1])
    ones = (lax.broadcasted_iota(jnp.int32, shape, 0) == 0).astype(jnp.bfloat16)
    return jnp.concatenate([value_t, ones], axis=0)


def fold(high, mixed, scores, value_t, exact):
    seen = scores if exact else scores[0 : min(SHIFT_KEYS, scores.shape[0]), :]
    new_high = jnp.maximum(high, jnp.max(seen, axis=0, keepdims=True))
    weights = jnp.exp2(scores * LOG2_SCALE - new_high * LOG2_SCALE).astype(jnp.bfloat16)
    fading = jnp.exp2((high - new_high) * LOG2_SCALE)
    mixed = mixed * fading + jnp.dot(with_ones(value_t), weights, preferred_element_type=jnp.float32)
    return new_high, mixed


def prepare_kernel(kv_ref, out_ref):
    count = kv_ref.shape[1]
    whole = count // LANES * LANES
    rest = count - whole
    out_ref[0, 0:whole, :] = kv_ref[0, 0:whole, :]
    for at in range(0, whole, LANES):
        out_ref[1, at : at + LANES, :] = kv_ref[1, at : at + LANES, :].T
    if rest:
        empty = jnp.zeros((LANES - rest, HEAD_SIZE), jnp.float32)
        tail_key = jnp.concatenate([kv_ref[0, whole:count, :].astype(jnp.float32), empty], axis=0)
        tail_value = jnp.concatenate([kv_ref[1, whole:count, :].astype(jnp.float32), empty], axis=0)
        out_ref[0, whole : whole + LANES, :] = tail_key.astype(jnp.bfloat16)
        out_ref[1, whole : whole + LANES, :] = tail_value.T.astype(jnp.bfloat16)


def prepare(kv):
    return pl.pallas_call(
        prepare_kernel,
        out_shape=jax.ShapeDtypeStruct((2, padded(kv.shape[1]), HEAD_SIZE), jnp.bfloat16),
        in_specs=[VMEM],
        out_specs=VMEM,
        compiler_params=pltpu.CompilerParams(vmem_limit_bytes=VMEM_LIMIT),
        cost_estimate=LITTLE,
        name="prepare",
    )(kv)


def lse_rows(block_count):
    return -(-3 * block_count // 16) * 16


def packed_blocks(rows):
    return next(count for count in range(1, rows) if count * HEAD_SIZE + lse_rows(count) == rows)


def table_kernel(position_ref, inside_ref, images_ref, owner_ref, out_ref, table_ref):
    slots, block_count = images_ref.shape
    for piece in range(slots):
        slot = lax.rem(position_ref[0] + (slots - piece), slots)
        base = piece * (block_count + 1)
        count = jnp.int32(0)
        for block in range(block_count):
            table_ref[base + 1 + block] = jnp.int32(0)
        for block in range(block_count):
            seen = lax.fori_loop(
                0,
                slots,
                lambda image, sum, block=block, slot=slot: sum
                + jnp.where(owner_ref[image] == slot, images_ref[image, block], 0),
                jnp.int32(0),
            )

            @pl.when(seen > 0)
            def _(base=base, block=block, count=count):
                table_ref[base + 1 + count] = jnp.int32(block)

            count = count + jnp.where(seen > 0, 1, 0)
        table_ref[base] = count
    lane = lax.broadcasted_iota(jnp.int32, out_ref.shape, 1)
    table = jnp.where(lane == out_ref.shape[1] - 1, inside_ref[0], 0)
    for index in range(table_ref.shape[0]):
        table = jnp.where(lane == index, table_ref[index], table)
    out_ref[...] = table


def seen_table(position, inside, block_images, image_owner):
    block_count, slots = block_images.shape
    size = slots * (block_count + 1)
    return pl.pallas_call(
        table_kernel,
        out_shape=jax.ShapeDtypeStruct((1, padded(size + 1)), jnp.int32),
        in_specs=[SMEM] * 4,
        out_specs=VMEM,
        scratch_shapes=[pltpu.SMEM((size,), jnp.int32)],
        compiler_params=pltpu.CompilerParams(vmem_limit_bytes=VMEM_LIMIT),
        name="seen_table",
    )(position, inside, block_images.T, image_owner)


def chunks_of(width):
    half = width // LANES // 2 * LANES
    return [(0, half), (half, width)] if half else [(0, width)]


def cross_kernel(key_count, pieces, offset, last, parts, table_ref, *refs):
    q_refs, images, refs = refs[:parts], refs[parts : parts + pieces], refs[parts + pieces :]
    if offset:
        before, refs = refs[:2], refs[2:]
    if last:
        out_ref, lse_ref, high_ref, mixed_ref, peak_ref, redo_ref = refs
    else:
        high_ref, mixed_ref, peak_ref, redo_ref = refs
    block_count = q_refs[0].shape[0] // MASK_BLOCK_TOKENS
    rows = q_refs[0].shape[1] // HEAD_SIZE * MASK_BLOCK_TOKENS
    peak_ref[...] = jnp.full_like(peak_ref, LOWEST)
    redo_ref[0] = jnp.int32(0)

    def fold_pair(blocks, image, exact, held):
        width = image.shape[1]
        queries = [q_refs[0][at_block(block), :] for block in blocks]
        if parts > 1:
            first = table_ref[0, table_ref.shape[1] - 1] > 0
            queries = [jnp.where(first, one, q_refs[1][at_block(block), :]) for one, block in zip(queries, blocks)]
        queries = jnp.concatenate([stacked_heads(one) for one in queries], axis=0)
        chunks = chunks_of(width)

        def scores_of(start, stop):
            scores = nt_dot(image[0, start:stop, :], queries)
            if stop > key_count:
                body = stop - start - LANES
                tail = scores[body:, :]
                key_id = start + body + lax.broadcasted_iota(jnp.int32, tail.shape, 0)
                tail = jnp.where(key_id < key_count, tail, LOWEST)
                scores = jnp.concatenate([scores[:body, :], tail], axis=0) if body else tail
            return scores

        @pl.when(exact)
        def _():
            tops = [jnp.max(scores_of(*chunk), axis=0, keepdims=True) for chunk in chunks]
            peak_ref[0:1, :] = functools.reduce(jnp.maximum, tops)

        if held is None:
            high = jnp.full((1, 2 * rows), LOWEST, jnp.float32)
            mixed = jnp.zeros((MIXED_ROWS, 2 * rows), jnp.float32)
        else:
            high = jnp.concatenate([held[0][block][0:1] for block in blocks], axis=1)
            mixed = jnp.concatenate([held[1][block] for block in blocks], axis=1)
        scores = scores_of(*chunks[0])
        seen = jnp.max(scores[0 : min(SHIFT_KEYS, scores.shape[0])], axis=0, keepdims=True)
        new_high = jnp.maximum(jnp.maximum(high, seen), peak_ref[0:1, :])
        shift = new_high * LOG2_SCALE
        mixed = mixed * jnp.exp2((high - new_high) * LOG2_SCALE)
        for index, (start, stop) in enumerate(chunks):
            following = scores_of(*chunks[index + 1]) if index + 1 < len(chunks) else None
            weights = jnp.exp2(scores * LOG2_SCALE - shift).astype(jnp.bfloat16)
            value_t = jnp.concatenate([image[1, c : c + LANES, :] for c in range(start, stop, LANES)], axis=1)
            mixed = mixed + jnp.dot(with_ones(value_t), weights, preferred_element_type=jnp.float32)
            scores = following
        for index, block in enumerate(blocks):
            own = slice(index * rows, (index + 1) * rows)
            high_ref[block] = jnp.broadcast_to(new_high[:, own], high_ref.shape[1:])
            mixed_ref[block] = mixed[:, own]

    def finish():
        for block in range(block_count):
            total = mixed_ref[block, HEAD_SIZE : HEAD_SIZE + 1, :]
            out_ref[block * HEAD_SIZE : (block + 1) * HEAD_SIZE, :] = (
                mixed_ref[block, 0:HEAD_SIZE, :] * (1.0 / total)
            ).astype(jnp.bfloat16)
            lse_ref[block : block + 1, :] = high_ref[block, 0:1, :] * LOG2_SCALE + jnp.log2(total)
        out_ref[block_count * HEAD_SIZE :, :] = lse_pieces(lse_ref[0:block_count, :], block_count)

    def attempt(trial, carry):
        @pl.when((trial == 0) | (redo_ref[0] > 0))
        def _():
            for piece in range(pieces):
                base = (offset + piece) * (block_count + 1)
                count = table_ref[0, base]
                if piece == 0:
                    held = before if offset else None
                    for block in range(block_count):
                        seen = functools.reduce(
                            jnp.logical_or,
                            [(count > index) & (table_ref[0, base + 1 + index] == block) for index in range(block_count)],
                        )

                        @pl.when(jnp.logical_not(seen))
                        def _(block=block):
                            if held is None:
                                high_ref[block] = jnp.full(high_ref.shape[1:], LOWEST, jnp.float32)
                                mixed_ref[block] = jnp.zeros(mixed_ref.shape[1:], jnp.float32)
                            else:
                                high_ref[block] = held[0][block]
                                mixed_ref[block] = held[1][block]

                else:
                    held = (high_ref, mixed_ref)

                def pair_step(pair, carry, piece=piece, base=base, count=count, held=held):
                    blocks = [table_ref[0, base + 1 + 2 * pair], table_ref[0, base + jnp.minimum(2 * pair + 2, count)]]
                    fold_pair(blocks, images[piece], trial > 0, held)
                    return carry

                lax.fori_loop(0, (count + 1) // 2, pair_step, 0)
            most = functools.reduce(
                jnp.maximum, [mixed_ref[block, HEAD_SIZE : HEAD_SIZE + 1, :] for block in range(block_count)]
            )
            if last:
                finish()
            redo_ref[0] = 1 - jnp.min((most <= MOST_SUM).astype(jnp.int32))

        return carry

    lax.fori_loop(0, 2, attempt, 0)


def cross_part(table, queries, images, key_count, offset, last, before=()):
    tokens, columns = queries[0].shape
    block_count = tokens // MASK_BLOCK_TOKENS
    rows = columns // HEAD_SIZE * MASK_BLOCK_TOKENS
    state = [(block_count, 8, rows), (block_count, MIXED_ROWS, rows)]
    scratch = [pltpu.VMEM((8, 2 * rows), jnp.float32), pltpu.SMEM((1,), jnp.int32)]
    if last:
        out_shape = jax.ShapeDtypeStruct((block_count * HEAD_SIZE + lse_rows(block_count), rows), jnp.bfloat16)
        scratch = [pltpu.VMEM(shape, jnp.float32) for shape in state] + scratch
        scratch = [pltpu.VMEM((-(-block_count // 8) * 8, rows), jnp.float32)] + scratch
    else:
        out_shape = tuple(jax.ShapeDtypeStruct(shape, jnp.float32) for shape in state)
    return pl.pallas_call(
        functools.partial(cross_kernel, key_count, len(images), offset, last, len(queries)),
        out_shape=out_shape,
        in_specs=[SMEM] + [VMEM] * (len(queries) + len(images) + len(before)),
        out_specs=VMEM if last else (VMEM,) * 2,
        scratch_shapes=scratch,
        compiler_params=pltpu.CompilerParams(vmem_limit_bytes=VMEM_LIMIT),
        cost_estimate=MUCH,
        name="cross_last" if last else "cross_first",
    )(table, *queries, *images, *before)


def lse_of(ref, block_count):
    tail = ref[block_count * HEAD_SIZE :, :].astype(jnp.float32)
    return tail[0:block_count] + tail[block_count : 2 * block_count] + tail[2 * block_count : 3 * block_count]


def lse_pieces(lse, block_count):
    first = lse.astype(jnp.bfloat16).astype(jnp.float32)
    second = (lse - first).astype(jnp.bfloat16).astype(jnp.float32)
    pieces = [first, second, lse - first - second]
    spare = lse_rows(block_count) - 3 * block_count
    if spare:
        pieces.append(jnp.zeros((spare, lse.shape[1]), jnp.float32))
    return jnp.concatenate(pieces, axis=0).astype(jnp.bfloat16)


def mixed_block(part_refs, weights, block):
    at = slice(block * HEAD_SIZE, (block + 1) * HEAD_SIZE)
    terms = [weight[block : block + 1, :] * ref[at, :].astype(jnp.float32) for ref, weight in zip(part_refs, weights)]
    return functools.reduce(jnp.add, terms)


def combine_kernel(held, last, *refs):
    if held:
        mixed_ref, lse_ref, part_ref, *out_refs = refs
        block_count = lse_ref.shape[0]
        lse = [lse_ref[...], lse_of(part_ref, block_count)]
    else:
        mixed_ref, part_ref, *out_refs = refs
        block_count = packed_blocks(part_ref.shape[0])
        lse = [lse_of(mixed_ref, block_count), lse_of(part_ref, block_count)]
    highest = functools.reduce(jnp.maximum, lse)
    weights = [jnp.exp2(one - highest) for one in lse]
    total = functools.reduce(jnp.add, weights)
    weights = [one / total for one in weights]
    for block in range(block_count):
        mixed = mixed_block((mixed_ref, part_ref), weights, block)
        if last:
            store_heads(out_refs[0], block, mixed)
        else:
            out_refs[0][block * HEAD_SIZE : (block + 1) * HEAD_SIZE, :] = mixed
    if not last:
        out_refs[1][...] = highest + jnp.log2(total)


def store_heads(out_ref, block, mixed):
    at = slice(block * MASK_BLOCK_TOKENS, (block + 1) * MASK_BLOCK_TOKENS)
    for head in range(out_ref.shape[1] // HEAD_SIZE):
        piece = mixed[:, head * MASK_BLOCK_TOKENS : (head + 1) * MASK_BLOCK_TOKENS]
        out_ref[at, head * HEAD_SIZE : (head + 1) * HEAD_SIZE] = piece.T.astype(jnp.bfloat16)


def combined(so_far, part, shape, last):
    tokens, columns = shape
    held = len(so_far) == 2
    block_count = tokens // MASK_BLOCK_TOKENS
    rows = columns // HEAD_SIZE * MASK_BLOCK_TOKENS
    if last:
        out_shape = jax.ShapeDtypeStruct(shape, jnp.bfloat16)
    else:
        out_shape = (
            jax.ShapeDtypeStruct((block_count * HEAD_SIZE, rows), jnp.float32),
            jax.ShapeDtypeStruct((block_count, rows), jnp.float32),
        )
    return pl.pallas_call(
        functools.partial(combine_kernel, held, last),
        out_shape=out_shape,
        in_specs=[VMEM] * (len(so_far) + 1),
        out_specs=VMEM if last else (VMEM,) * 2,
        compiler_params=pltpu.CompilerParams(vmem_limit_bytes=VMEM_LIMIT),
        cost_estimate=MUCH,
        name="combine_last" if last else "combine",
    )(*so_far, part)


def pair_queries(q_ref, first, blocks):
    return jnp.concatenate(
        [
            stacked_heads(q_ref[block * MASK_BLOCK_TOKENS : (block + 1) * MASK_BLOCK_TOKENS, :])
            for block in range(first, first + blocks)
        ],
        axis=0,
    )


def self_first_kernel(group, q_ref, text_ref, high_ref, mixed_ref, value_ref):
    tokens, columns = q_ref.shape
    rows = columns // HEAD_SIZE * MASK_BLOCK_TOKENS
    value_ref[...] = text_ref[:, HEAD_SIZE:].T
    for index in range(tokens // MASK_BLOCK_TOKENS // group):
        first = index * group
        start, stop = first * MASK_BLOCK_TOKENS, (first + group) * MASK_BLOCK_TOKENS
        scores = nt_dot(text_ref[0:stop, 0:HEAD_SIZE], pair_queries(q_ref, first, group))
        tail = scores[start:, :]
        key_id = lax.broadcasted_iota(jnp.int32, tail.shape, 0)
        column = lax.broadcasted_iota(jnp.int32, tail.shape, 1)
        query_id = column // rows * MASK_BLOCK_TOKENS + column % MASK_BLOCK_TOKENS
        tail = jnp.where(key_id <= query_id, tail, LOWEST)
        scores = jnp.concatenate([scores[:start, :], tail], axis=0) if start else tail
        high = jnp.full((1, group * rows), LOWEST, jnp.float32)
        mixed = jnp.zeros((MIXED_ROWS, group * rows), jnp.float32)
        high, mixed = fold(high, mixed, scores, value_ref[:, 0:stop], True)
        high_ref[index] = jnp.broadcast_to(high, high_ref.shape[1:])
        mixed_ref[index] = mixed


def self_last_kernel(group, pieces, position_ref, q_ref, high_ref, mixed_ref, *refs):
    texts = refs[:pieces]
    out_ref, value_ref, new_high_ref, new_mixed_ref = refs[pieces:]
    rows = q_ref.shape[1] // HEAD_SIZE * MASK_BLOCK_TOKENS
    new_high_ref[...] = high_ref[...]
    new_mixed_ref[...] = mixed_ref[...]
    for piece in range(pieces):

        @pl.when(position_ref[0] >= piece + 1)
        def _(piece=piece):
            value_ref[...] = texts[piece][:, HEAD_SIZE:].T
            for index in range(high_ref.shape[0]):
                scores = nt_dot(texts[piece][:, 0:HEAD_SIZE], pair_queries(q_ref, index * group, group))
                high, mixed = fold(new_high_ref[index, 0:1, :], new_mixed_ref[index], scores, value_ref[...], True)
                new_high_ref[index] = jnp.broadcast_to(high, high_ref.shape[1:])
                new_mixed_ref[index] = mixed

    for index in range(high_ref.shape[0]):
        total = new_mixed_ref[index, HEAD_SIZE : HEAD_SIZE + 1, :]
        mixed = new_mixed_ref[index, 0:HEAD_SIZE, :] / total
        for block in range(group):
            store_heads(out_ref, index * group + block, mixed[:, block * rows : (block + 1) * rows])


def self_first(queries, text):
    tokens, columns = queries.shape
    block_count = tokens // MASK_BLOCK_TOKENS
    group = 1 if block_count % 2 else 2
    width = group * columns // HEAD_SIZE * MASK_BLOCK_TOKENS
    return pl.pallas_call(
        functools.partial(self_first_kernel, group),
        out_shape=(
            jax.ShapeDtypeStruct((block_count // group, 8, width), jnp.float32),
            jax.ShapeDtypeStruct((block_count // group, MIXED_ROWS, width), jnp.float32),
        ),
        in_specs=[VMEM] * 2,
        out_specs=(VMEM,) * 2,
        scratch_shapes=[pltpu.VMEM((HEAD_SIZE, tokens), jnp.bfloat16)],
        compiler_params=pltpu.CompilerParams(vmem_limit_bytes=VMEM_LIMIT),
        cost_estimate=LITTLE,
        name="self_first",
    )(queries, text)


def self_last(position, queries, state, texts):
    tokens, columns = queries.shape
    group = tokens // MASK_BLOCK_TOKENS // state[0].shape[0]
    return pl.pallas_call(
        functools.partial(self_last_kernel, group, len(texts)),
        out_shape=jax.ShapeDtypeStruct((tokens, columns), jnp.bfloat16),
        in_specs=[SMEM] + [VMEM] * (3 + len(texts)),
        out_specs=VMEM,
        scratch_shapes=[pltpu.VMEM((HEAD_SIZE, tokens), jnp.bfloat16)]
        + [pltpu.VMEM(one.shape, jnp.float32) for one in state],
        compiler_params=pltpu.CompilerParams(vmem_limit_bytes=VMEM_LIMIT),
        cost_estimate=LITTLE,
        name="self_last",
    )(position, queries, *state, *texts)


def shifted(value, axis, steps):
    count = lax.axis_size(axis)
    return lax.ppermute(value, axis, [(source, (source + steps) % count) for source in range(count)])


def swapped(value, axis, bits):
    return lax.ppermute(value, axis, [(source, source ^ bits) for source in range(lax.axis_size(axis))])


def after(value, earlier):
    return lax.optimization_barrier((value, earlier))[0]


def per_device(
    self_queries, text_kv, cross_queries, image_kv, block_images, image_owner
):
    rows = self_queries.shape[0]
    key_count = image_kv.shape[2]
    cycle = lax.axis_size("blk")
    ring = lax.axis_size("enc")
    place = lax.axis_index("enc")
    inside = ((place > 0) & (place < ring - 1)).astype(jnp.int32)[None]
    position = lax.axis_index("blk").astype(jnp.int32)[None]

    raw = [image_kv]
    for _ in range(1, cycle):
        raw.append(shifted(raw[-1], "blk", 1))
    images = [prepare(image[0]) for image in raw]
    if ring == 4:
        queries = {step: [swapped(cross_queries, "enc", step)] for step in (2, 1)}
        middle = lax.ppermute(cross_queries, "enc", [(0, 0), (1, 2), (2, 1), (3, 3)])
        queries[3] = [middle, swapped(queries[2][0], "enc", 1)]
    else:
        queries = {step: [shifted(cross_queries, "enc", ring - step)] for step in range(1, ring)}
    queries[0] = [cross_queries]
    table = seen_table(position, inside, block_images, image_owner)

    latest = [None]

    def in_turn(arrays):
        return arrays if latest[0] is None else [after(one, latest[0]) for one in arrays]

    def begun(step):
        latest[0] = cross_part(table, in_turn(queries[step]), images[:1], key_count, 0, False)
        return latest[0]

    def finished(step, state=None):
        used = images if state is None else images[1:]
        before = () if state is None else state
        offset = 0 if state is None else 1
        latest[0] = cross_part(table, in_turn(queries[step]), used, key_count, offset, True, before)
        return latest[0]

    split = cycle > 1
    own = begun(0) if split else None
    steps = [2, 3, 1] if ring == 4 else list(range(1, ring))
    states = {step: begun(step) for step in steps[:1]} if split else {}
    received, texts = [], []
    for step in steps:
        part = finished(step, states.get(step))
        if not texts:
            texts.append(after(text_kv, part).reshape(rows, 2 * HEAD_SIZE))
            for _ in range(1, cycle):
                texts.append(shifted(texts[-1], "blk", 1))
        received.append(swapped(part, "enc", step) if ring == 4 else shifted(part, "enc", step))
    own_part = finished(0, own)
    self_state = latest[0] = self_first(in_turn([self_queries])[0], texts[0])
    self_out = latest[0] = self_last(position, in_turn([self_queries])[0], self_state, texts[1:])
    so_far = in_turn([own_part])
    for index, part in enumerate(received):
        so_far = combined(so_far, part, cross_queries.shape, index + 1 == len(received))
    return (self_out, so_far)


def solution(mesh):
    placed = (
        P("blk", ("tp", "enc")),
        P("blk", None, "tp"),
        P("blk", ("tp", "enc")),
        P("blk", None, "enc", "tp"),
        P("blk", None),
        P(),
    )
    return jax.shard_map(
        per_device,
        mesh=mesh,
        in_specs=placed,
        out_specs=(P("blk", ("tp", "enc")), P("blk", ("tp", "enc"))),
        check_vma=False,
    )
```

```python
import functools
import math

import jax
import jax.numpy as jnp
from jax import lax
from jax.experimental import pallas as pl
from jax.experimental.pallas import tpu as pltpu
from jax.sharding import PartitionSpec as P

HEAD_SIZE = 128
MASK_BLOCK_TOKENS = 128
LANES = 128
LOWEST = -1e30
MIXED_ROWS = HEAD_SIZE + 16
SHIFT_KEYS = 256
MOST_SUM = 2.0**100
LOG2_SCALE = math.log2(math.e) / math.sqrt(HEAD_SIZE)
VMEM_LIMIT = 48 * 1024 * 1024

LITTLE = pl.CostEstimate(flops=0, bytes_accessed=1024, transcendentals=0)
MUCH = pl.CostEstimate(flops=2_000_000_000, bytes_accessed=1024, transcendentals=0)

VMEM = pl.BlockSpec(memory_space=pltpu.VMEM)
SMEM = pl.BlockSpec(memory_space=pltpu.SMEM)


def padded(count):
    return -(-count // LANES) * LANES


def nt_dot(a, b):
    return lax.dot_general(a, b, (((1,), (1,)), ((), ())), preferred_element_type=jnp.float32)


def at_block(block, size=MASK_BLOCK_TOKENS):
    return pl.ds(pl.multiple_of(block * size, size), size)


def stacked_heads(rows):
    heads = rows.shape[1] // HEAD_SIZE
    return jnp.concatenate([rows[:, h * HEAD_SIZE : (h + 1) * HEAD_SIZE] for h in range(heads)], axis=0)


def with_ones(value_t):
    shape = (MIXED_ROWS - HEAD_SIZE, value_t.shape[1])
    ones = (lax.broadcasted_iota(jnp.int32, shape, 0) == 0).astype(jnp.bfloat16)
    return jnp.concatenate([value_t, ones], axis=0)


def fold(high, mixed, scores, value_t, exact):
    seen = scores if exact else scores[0 : min(SHIFT_KEYS, scores.shape[0]), :]
    new_high = jnp.maximum(high, jnp.max(seen, axis=0, keepdims=True))
    weights = jnp.exp2(scores * LOG2_SCALE - new_high * LOG2_SCALE).astype(jnp.bfloat16)
    fading = jnp.exp2((high - new_high) * LOG2_SCALE)
    mixed = mixed * fading + jnp.dot(with_ones(value_t), weights, preferred_element_type=jnp.float32)
    return new_high, mixed


def prepare_kernel(kv_ref, out_ref):
    count = kv_ref.shape[1]
    whole = count // LANES * LANES
    rest = count - whole
    out_ref[0, 0:whole, :] = kv_ref[0, 0:whole, :]
    for at in range(0, whole, LANES):
        out_ref[1, at : at + LANES, :] = kv_ref[1, at : at + LANES, :].T
    if rest:
        empty = jnp.zeros((LANES - rest, HEAD_SIZE), jnp.float32)
        tail_key = jnp.concatenate([kv_ref[0, whole:count, :].astype(jnp.float32), empty], axis=0)
        tail_value = jnp.concatenate([kv_ref[1, whole:count, :].astype(jnp.float32), empty], axis=0)
        out_ref[0, whole : whole + LANES, :] = tail_key.astype(jnp.bfloat16)
        out_ref[1, whole : whole + LANES, :] = tail_value.T.astype(jnp.bfloat16)


def prepare(kv):
    return pl.pallas_call(
        prepare_kernel,
        out_shape=jax.ShapeDtypeStruct((2, padded(kv.shape[1]), HEAD_SIZE), jnp.bfloat16),
        in_specs=[VMEM],
        out_specs=VMEM,
        compiler_params=pltpu.CompilerParams(vmem_limit_bytes=VMEM_LIMIT),
        cost_estimate=LITTLE,
        name="prepare",
    )(kv)


def lse_rows(block_count):
    return -(-3 * block_count // 16) * 16


def packed_blocks(rows):
    return next(count for count in range(1, rows) if count * HEAD_SIZE + lse_rows(count) == rows)


def table_kernel(position_ref, inside_ref, images_ref, owner_ref, out_ref, table_ref):
    slots, block_count = images_ref.shape
    for piece in range(slots):
        slot = lax.rem(position_ref[0] + (slots - piece), slots)
        base = piece * (block_count + 1)
        count = jnp.int32(0)
        for block in range(block_count):
            table_ref[base + 1 + block] = jnp.int32(0)
        for block in range(block_count):
            seen = lax.fori_loop(
                0,
                slots,
                lambda image, sum, block=block, slot=slot: sum
                + jnp.where(owner_ref[image] == slot, images_ref[image, block], 0),
                jnp.int32(0),
            )

            @pl.when(seen > 0)
            def _(base=base, block=block, count=count):
                table_ref[base + 1 + count] = jnp.int32(block)

            count = count + jnp.where(seen > 0, 1, 0)
        table_ref[base] = count
    lane = lax.broadcasted_iota(jnp.int32, out_ref.shape, 1)
    table = jnp.where(lane == out_ref.shape[1] - 1, inside_ref[0], 0)
    for index in range(table_ref.shape[0]):
        table = jnp.where(lane == index, table_ref[index], table)
    out_ref[...] = table


def seen_table(position, inside, block_images, image_owner):
    block_count, slots = block_images.shape
    size = slots * (block_count + 1)
    return pl.pallas_call(
        table_kernel,
        out_shape=jax.ShapeDtypeStruct((1, padded(size + 1)), jnp.int32),
        in_specs=[SMEM] * 4,
        out_specs=VMEM,
        scratch_shapes=[pltpu.SMEM((size,), jnp.int32)],
        compiler_params=pltpu.CompilerParams(vmem_limit_bytes=VMEM_LIMIT),
        name="seen_table",
    )(position, inside, block_images.T, image_owner)


def chunks_of(width):
    tiles = width // LANES
    cuts = sorted({tiles * index // 3 * LANES for index in range(3)} | {width})
    return list(zip(cuts, cuts[1:]))


def cross_kernel(key_count, pieces, offset, last, parts, table_ref, *refs):
    q_refs, images, refs = refs[:parts], refs[parts : parts + pieces], refs[parts + pieces :]
    if offset:
        before, refs = refs[:2], refs[2:]
    if last:
        out_ref, lse_ref, high_ref, mixed_ref, peak_ref, redo_ref = refs
    else:
        high_ref, mixed_ref, peak_ref, redo_ref = refs
    block_count = q_refs[0].shape[0] // MASK_BLOCK_TOKENS
    rows = q_refs[0].shape[1] // HEAD_SIZE * MASK_BLOCK_TOKENS
    peak_ref[...] = jnp.full_like(peak_ref, LOWEST)
    redo_ref[0] = jnp.int32(0)

    def fold_pair(blocks, image, exact, held):
        width = image.shape[1]
        queries = [q_refs[0][at_block(block), :] for block in blocks]
        if parts > 1:
            first = table_ref[0, table_ref.shape[1] - 1] > 0
            queries = [jnp.where(first, one, q_refs[1][at_block(block), :]) for one, block in zip(queries, blocks)]
        queries = jnp.concatenate([stacked_heads(one) for one in queries], axis=0)
        chunks = chunks_of(width)

        def scores_of(start, stop):
            scores = nt_dot(image[0, start:stop, :], queries)
            if stop > key_count:
                body = stop - start - LANES
                tail = scores[body:, :]
                key_id = start + body + lax.broadcasted_iota(jnp.int32, tail.shape, 0)
                tail = jnp.where(key_id < key_count, tail, LOWEST)
                scores = jnp.concatenate([scores[:body, :], tail], axis=0) if body else tail
            return scores

        @pl.when(exact)
        def _():
            tops = [jnp.max(scores_of(*chunk), axis=0, keepdims=True) for chunk in chunks]
            peak_ref[0:1, :] = functools.reduce(jnp.maximum, tops)

        if held is None:
            high = jnp.full((1, 2 * rows), LOWEST, jnp.float32)
            mixed = jnp.zeros((MIXED_ROWS, 2 * rows), jnp.float32)
        else:
            high = jnp.concatenate([held[0][block][0:1] for block in blocks], axis=1)
            mixed = jnp.concatenate([held[1][block] for block in blocks], axis=1)
        scores = scores_of(*chunks[0])
        seen = jnp.max(scores[0 : min(SHIFT_KEYS, scores.shape[0])], axis=0, keepdims=True)
        new_high = jnp.maximum(jnp.maximum(high, seen), peak_ref[0:1, :])
        shift = new_high * LOG2_SCALE
        mixed = mixed * jnp.exp2((high - new_high) * LOG2_SCALE)
        for index, (start, stop) in enumerate(chunks):
            following = scores_of(*chunks[index + 1]) if index + 1 < len(chunks) else None
            weights = jnp.exp2(scores * LOG2_SCALE - shift).astype(jnp.bfloat16)
            value_t = jnp.concatenate([image[1, c : c + LANES, :] for c in range(start, stop, LANES)], axis=1)
            mixed = mixed + jnp.dot(with_ones(value_t), weights, preferred_element_type=jnp.float32)
            scores = following
        for index, block in enumerate(blocks):
            own = slice(index * rows, (index + 1) * rows)
            high_ref[block] = jnp.broadcast_to(new_high[:, own], high_ref.shape[1:])
            mixed_ref[block] = mixed[:, own]

    def finish():
        for block in range(block_count):
            total = mixed_ref[block, HEAD_SIZE : HEAD_SIZE + 1, :]
            out_ref[block * HEAD_SIZE : (block + 1) * HEAD_SIZE, :] = (
                mixed_ref[block, 0:HEAD_SIZE, :] * (1.0 / total)
            ).astype(jnp.bfloat16)
            lse_ref[block : block + 1, :] = high_ref[block, 0:1, :] * LOG2_SCALE + jnp.log2(total)
        out_ref[block_count * HEAD_SIZE :, :] = lse_pieces(lse_ref[0:block_count, :], block_count)

    def attempt(trial, carry):
        @pl.when((trial == 0) | (redo_ref[0] > 0))
        def _():
            for piece in range(pieces):
                base = (offset + piece) * (block_count + 1)
                count = table_ref[0, base]
                if piece == 0:
                    held = before if offset else None
                    for block in range(block_count):
                        seen = functools.reduce(
                            jnp.logical_or,
                            [(count > index) & (table_ref[0, base + 1 + index] == block) for index in range(block_count)],
                        )

                        @pl.when(jnp.logical_not(seen))
                        def _(block=block):
                            if held is None:
                                high_ref[block] = jnp.full(high_ref.shape[1:], LOWEST, jnp.float32)
                                mixed_ref[block] = jnp.zeros(mixed_ref.shape[1:], jnp.float32)
                            else:
                                high_ref[block] = held[0][block]
                                mixed_ref[block] = held[1][block]

                else:
                    held = (high_ref, mixed_ref)

                def pair_step(pair, carry, piece=piece, base=base, count=count, held=held):
                    blocks = [table_ref[0, base + 1 + 2 * pair], table_ref[0, base + jnp.minimum(2 * pair + 2, count)]]
                    fold_pair(blocks, images[piece], trial > 0, held)
                    return carry

                lax.fori_loop(0, (count + 1) // 2, pair_step, 0)
            most = functools.reduce(
                jnp.maximum, [mixed_ref[block, HEAD_SIZE : HEAD_SIZE + 1, :] for block in range(block_count)]
            )
            if last:
                finish()
            redo_ref[0] = 1 - jnp.min((most <= MOST_SUM).astype(jnp.int32))

        return carry

    lax.fori_loop(0, 2, attempt, 0)


def cross_part(table, queries, images, key_count, offset, last, before=()):
    tokens, columns = queries[0].shape
    block_count = tokens // MASK_BLOCK_TOKENS
    rows = columns // HEAD_SIZE * MASK_BLOCK_TOKENS
    state = [(block_count, 8, rows), (block_count, MIXED_ROWS, rows)]
    scratch = [pltpu.VMEM((8, 2 * rows), jnp.float32), pltpu.SMEM((1,), jnp.int32)]
    if last:
        out_shape = jax.ShapeDtypeStruct((block_count * HEAD_SIZE + lse_rows(block_count), rows), jnp.bfloat16)
        scratch = [pltpu.VMEM(shape, jnp.float32) for shape in state] + scratch
        scratch = [pltpu.VMEM((-(-block_count // 8) * 8, rows), jnp.float32)] + scratch
    else:
        out_shape = tuple(jax.ShapeDtypeStruct(shape, jnp.float32) for shape in state)
    return pl.pallas_call(
        functools.partial(cross_kernel, key_count, len(images), offset, last, len(queries)),
        out_shape=out_shape,
        in_specs=[SMEM] + [VMEM] * (len(queries) + len(images) + len(before)),
        out_specs=VMEM if last else (VMEM,) * 2,
        scratch_shapes=scratch,
        compiler_params=pltpu.CompilerParams(vmem_limit_bytes=VMEM_LIMIT),
        cost_estimate=MUCH,
        name="cross_last" if last else "cross_first",
    )(table, *queries, *images, *before)


def lse_of(ref, block_count):
    tail = ref[block_count * HEAD_SIZE :, :].astype(jnp.float32)
    return tail[0:block_count] + tail[block_count : 2 * block_count] + tail[2 * block_count : 3 * block_count]


def lse_pieces(lse, block_count):
    first = lse.astype(jnp.bfloat16).astype(jnp.float32)
    second = (lse - first).astype(jnp.bfloat16).astype(jnp.float32)
    pieces = [first, second, lse - first - second]
    spare = lse_rows(block_count) - 3 * block_count
    if spare:
        pieces.append(jnp.zeros((spare, lse.shape[1]), jnp.float32))
    return jnp.concatenate(pieces, axis=0).astype(jnp.bfloat16)


def mixed_block(part_refs, weights, block):
    at = slice(block * HEAD_SIZE, (block + 1) * HEAD_SIZE)
    terms = [weight[block : block + 1, :] * ref[at, :].astype(jnp.float32) for ref, weight in zip(part_refs, weights)]
    return functools.reduce(jnp.add, terms)


def combine_kernel(held, last, *refs):
    if held:
        mixed_ref, lse_ref, part_ref, *out_refs = refs
        block_count = lse_ref.shape[0]
        lse = [lse_ref[...], lse_of(part_ref, block_count)]
    else:
        mixed_ref, part_ref, *out_refs = refs
        block_count = packed_blocks(part_ref.shape[0])
        lse = [lse_of(mixed_ref, block_count), lse_of(part_ref, block_count)]
    highest = functools.reduce(jnp.maximum, lse)
    weights = [jnp.exp2(one - highest) for one in lse]
    total = functools.reduce(jnp.add, weights)
    weights = [one / total for one in weights]
    for block in range(block_count):
        mixed = mixed_block((mixed_ref, part_ref), weights, block)
        if last:
            store_heads(out_refs[0], block, mixed)
        else:
            out_refs[0][block * HEAD_SIZE : (block + 1) * HEAD_SIZE, :] = mixed
    if not last:
        out_refs[1][...] = highest + jnp.log2(total)


def store_heads(out_ref, block, mixed):
    at = slice(block * MASK_BLOCK_TOKENS, (block + 1) * MASK_BLOCK_TOKENS)
    for head in range(out_ref.shape[1] // HEAD_SIZE):
        piece = mixed[:, head * MASK_BLOCK_TOKENS : (head + 1) * MASK_BLOCK_TOKENS]
        out_ref[at, head * HEAD_SIZE : (head + 1) * HEAD_SIZE] = piece.T.astype(jnp.bfloat16)


def combined(so_far, part, shape, last):
    tokens, columns = shape
    held = len(so_far) == 2
    block_count = tokens // MASK_BLOCK_TOKENS
    rows = columns // HEAD_SIZE * MASK_BLOCK_TOKENS
    if last:
        out_shape = jax.ShapeDtypeStruct(shape, jnp.bfloat16)
    else:
        out_shape = (
            jax.ShapeDtypeStruct((block_count * HEAD_SIZE, rows), jnp.float32),
            jax.ShapeDtypeStruct((block_count, rows), jnp.float32),
        )
    return pl.pallas_call(
        functools.partial(combine_kernel, held, last),
        out_shape=out_shape,
        in_specs=[VMEM] * (len(so_far) + 1),
        out_specs=VMEM if last else (VMEM,) * 2,
        compiler_params=pltpu.CompilerParams(vmem_limit_bytes=VMEM_LIMIT),
        cost_estimate=MUCH,
        name="combine_last" if last else "combine",
    )(*so_far, part)


def pair_queries(q_ref, first, blocks):
    return jnp.concatenate(
        [
            stacked_heads(q_ref[block * MASK_BLOCK_TOKENS : (block + 1) * MASK_BLOCK_TOKENS, :])
            for block in range(first, first + blocks)
        ],
        axis=0,
    )


def self_first_kernel(group, q_ref, text_ref, high_ref, mixed_ref, value_ref):
    tokens, columns = q_ref.shape
    rows = columns // HEAD_SIZE * MASK_BLOCK_TOKENS
    value_ref[...] = text_ref[:, HEAD_SIZE:].T
    for index in range(tokens // MASK_BLOCK_TOKENS // group):
        first = index * group
        start, stop = first * MASK_BLOCK_TOKENS, (first + group) * MASK_BLOCK_TOKENS
        scores = nt_dot(text_ref[0:stop, 0:HEAD_SIZE], pair_queries(q_ref, first, group))
        tail = scores[start:, :]
        key_id = lax.broadcasted_iota(jnp.int32, tail.shape, 0)
        column = lax.broadcasted_iota(jnp.int32, tail.shape, 1)
        query_id = column // rows * MASK_BLOCK_TOKENS + column % MASK_BLOCK_TOKENS
        tail = jnp.where(key_id <= query_id, tail, LOWEST)
        scores = jnp.concatenate([scores[:start, :], tail], axis=0) if start else tail
        high = jnp.full((1, group * rows), LOWEST, jnp.float32)
        mixed = jnp.zeros((MIXED_ROWS, group * rows), jnp.float32)
        high, mixed = fold(high, mixed, scores, value_ref[:, 0:stop], True)
        high_ref[index] = jnp.broadcast_to(high, high_ref.shape[1:])
        mixed_ref[index] = mixed


def self_last_kernel(group, pieces, position_ref, q_ref, high_ref, mixed_ref, *refs):
    texts = refs[:pieces]
    out_ref, value_ref, new_high_ref, new_mixed_ref = refs[pieces:]
    rows = q_ref.shape[1] // HEAD_SIZE * MASK_BLOCK_TOKENS
    new_high_ref[...] = high_ref[...]
    new_mixed_ref[...] = mixed_ref[...]
    for piece in range(pieces):

        @pl.when(position_ref[0] >= piece + 1)
        def _(piece=piece):
            value_ref[...] = texts[piece][:, HEAD_SIZE:].T
            for index in range(high_ref.shape[0]):
                scores = nt_dot(texts[piece][:, 0:HEAD_SIZE], pair_queries(q_ref, index * group, group))
                high, mixed = fold(new_high_ref[index, 0:1, :], new_mixed_ref[index], scores, value_ref[...], True)
                new_high_ref[index] = jnp.broadcast_to(high, high_ref.shape[1:])
                new_mixed_ref[index] = mixed

    for index in range(high_ref.shape[0]):
        total = new_mixed_ref[index, HEAD_SIZE : HEAD_SIZE + 1, :]
        mixed = new_mixed_ref[index, 0:HEAD_SIZE, :] / total
        for block in range(group):
            store_heads(out_ref, index * group + block, mixed[:, block * rows : (block + 1) * rows])


def self_first(queries, text):
    tokens, columns = queries.shape
    block_count = tokens // MASK_BLOCK_TOKENS
    group = 1 if block_count % 2 else 2
    width = group * columns // HEAD_SIZE * MASK_BLOCK_TOKENS
    return pl.pallas_call(
        functools.partial(self_first_kernel, group),
        out_shape=(
            jax.ShapeDtypeStruct((block_count // group, 8, width), jnp.float32),
            jax.ShapeDtypeStruct((block_count // group, MIXED_ROWS, width), jnp.float32),
        ),
        in_specs=[VMEM] * 2,
        out_specs=(VMEM,) * 2,
        scratch_shapes=[pltpu.VMEM((HEAD_SIZE, tokens), jnp.bfloat16)],
        compiler_params=pltpu.CompilerParams(vmem_limit_bytes=VMEM_LIMIT),
        cost_estimate=LITTLE,
        name="self_first",
    )(queries, text)


def self_last(position, queries, state, texts):
    tokens, columns = queries.shape
    group = tokens // MASK_BLOCK_TOKENS // state[0].shape[0]
    return pl.pallas_call(
        functools.partial(self_last_kernel, group, len(texts)),
        out_shape=jax.ShapeDtypeStruct((tokens, columns), jnp.bfloat16),
        in_specs=[SMEM] + [VMEM] * (3 + len(texts)),
        out_specs=VMEM,
        scratch_shapes=[pltpu.VMEM((HEAD_SIZE, tokens), jnp.bfloat16)]
        + [pltpu.VMEM(one.shape, jnp.float32) for one in state],
        compiler_params=pltpu.CompilerParams(vmem_limit_bytes=VMEM_LIMIT),
        cost_estimate=LITTLE,
        name="self_last",
    )(position, queries, *state, *texts)


def shifted(value, axis, steps):
    count = lax.axis_size(axis)
    return lax.ppermute(value, axis, [(source, (source + steps) % count) for source in range(count)])


def swapped(value, axis, bits):
    return lax.ppermute(value, axis, [(source, source ^ bits) for source in range(lax.axis_size(axis))])


def after(value, earlier):
    return lax.optimization_barrier((value, earlier))[0]


def per_device(
    self_queries, text_kv, cross_queries, image_kv, block_images, image_owner
):
    rows = self_queries.shape[0]
    key_count = image_kv.shape[2]
    cycle = lax.axis_size("blk")
    ring = lax.axis_size("enc")
    place = lax.axis_index("enc")
    inside = ((place > 0) & (place < ring - 1)).astype(jnp.int32)[None]
    position = lax.axis_index("blk").astype(jnp.int32)[None]

    raw = [image_kv]
    for _ in range(1, cycle):
        raw.append(shifted(raw[-1], "blk", 1))
    images = [prepare(image[0]) for image in raw]
    if ring == 4:
        queries = {step: [swapped(cross_queries, "enc", step)] for step in (2, 1)}
        middle = lax.ppermute(cross_queries, "enc", [(0, 0), (1, 2), (2, 1), (3, 3)])
        queries[3] = [middle, swapped(queries[2][0], "enc", 1)]
    else:
        queries = {step: [shifted(cross_queries, "enc", ring - step)] for step in range(1, ring)}
    queries[0] = [cross_queries]
    table = seen_table(position, inside, block_images, image_owner)

    latest = [None]

    def in_turn(arrays):
        return arrays if latest[0] is None else [after(one, latest[0]) for one in arrays]

    def begun(step):
        latest[0] = cross_part(table, in_turn(queries[step]), images[:1], key_count, 0, False)
        return latest[0]

    def finished(step, state=None):
        used = images if state is None else images[1:]
        before = () if state is None else state
        offset = 0 if state is None else 1
        latest[0] = cross_part(table, in_turn(queries[step]), used, key_count, offset, True, before)
        return latest[0]

    split = cycle > 1
    own = begun(0) if split else None
    steps = [2, 3, 1] if ring == 4 else list(range(1, ring))
    states = {step: begun(step) for step in steps[:1]} if split else {}
    received, texts = [], []
    for step in steps:
        part = finished(step, states.get(step))
        if not texts:
            texts.append(after(text_kv, part).reshape(rows, 2 * HEAD_SIZE))
            for _ in range(1, cycle):
                texts.append(shifted(texts[-1], "blk", 1))
        received.append(swapped(part, "enc", step) if ring == 4 else shifted(part, "enc", step))
    own_part = finished(0, own)
    self_state = latest[0] = self_first(in_turn([self_queries])[0], texts[0])
    self_out = latest[0] = self_last(position, in_turn([self_queries])[0], self_state, texts[1:])
    so_far = in_turn([own_part])
    for index, part in enumerate(received):
        so_far = combined(so_far, part, cross_queries.shape, index + 1 == len(received))
    return (self_out, so_far)


def solution(mesh):
    placed = (
        P("blk", ("tp", "enc")),
        P("blk", None, "tp"),
        P("blk", ("tp", "enc")),
        P("blk", None, "enc", "tp"),
        P("blk", None),
        P(),
    )
    return jax.shard_map(
        per_device,
        mesh=mesh,
        in_specs=placed,
        out_specs=(P("blk", ("tp", "enc")), P("blk", ("tp", "enc"))),
        check_vma=False,
    )
```
